32 devices in a mesh: gx: 4 (over z), gy: 8 (over y, x, core).
Axes of the slice: x: 2, y: 2, z: 4, core: 2. Of those that a mesh axis runs over, the one named last changes fastest.
Arguments:
- initial_state: float32 [2, 16, 48, 1024], P(None, 'gx', None, 'gy'), may hold values from -6 to 6
- eddy_diffusivity: float32 [16, 48, 1024], P('gx', None, 'gy'), may hold values from 0.02 to 0.12
- velocity: float32 [3, 16, 48, 1024], P(None, 'gx', None, 'gy'), may hold values from -0.08 to 0.08
- target: float32 [2, 16, 48, 1024], P(None, 'gx', None, 'gy'), may hold values from -6 to 6
- sensor_cell: int32 [2048], P(('gx', 'gy')), may hold values from 0 to 24575
- sensor_owner: int32 [2048, 1], P(('gx', 'gy')), may hold values from 0 to 31; in each aligned block of 64 rows (0 to 63, 64 to 127, ...) at most 4 rows name the same one
- observations: float32 [2048, 2, 4], P(('gx', 'gy')), may hold values from -6 to 6
- actuator_block: int32 [512], P(('gx', 'gy')), may hold values from 0 to 191
- actuator_owner: int32 [512, 1], P(('gx', 'gy')), may hold values from 0 to 7; in each aligned block of 16 rows (0 to 15, 16 to 31, ...) at most 4 rows name the same one
- controls: float32 [512, 2], P(('gx', 'gy')), may hold values from -6 to 6
- footprint: float32 [512, 128], P(('gx', 'gy')), may hold values from 0 to 1
Outputs:
- final_state: float32 [2, 16, 48, 1024], P(None, 'gx', None, 'gy')
- initial_sensitivity: float32 [2, 16, 48, 1024], P(None, 'gx', None, 'gy')
- actuator_gradient: float32 [512, 2], P(('gx', 'gy'))
The draws below stay inside these ranges and needn't reach their ends.
Inputs may be any that keep to these rules, and one draw needn't show every extreme that they name: `sensor_owner`: among the 64 rows of one device, no owner is named more than 4 times, a bound that some block reaches. `actuator_owner`: among the 16 rows of one device, no owner is named more than 4 times, a bound that some block reaches.
All inputs are finite; a program needn't handle non-finite values.
Results may differ from the reference program's by a relative error of at most 0.00002.
Values sent between devices are 32-bit elements; how exact they have to be, the bound alone decides.
No kernel may reach another device: no remote copies, remote signals or barrier semaphores. Data moves between devices by JAX's collectives and lax.ppermute only.
A program may use at most 128 MiB of HBM per device.

```python
import math
import jax
import jax.numpy as jnp
import numpy as np

CX = 4
CY = 128
NZ = 48
NSTEPS = 4
FX = 4
FZ = 8
FY = 4
CAPS = 4
CAPA = 4
FOOT = 128
NX = 16
NY = 1024
OWNERS = 32
SENS_DEV = 64
SENSORS = 2048
ACT_DEV = 16
ACTS = 512
CELLS_DEV = 24576
BLOCKS_DEV = 192
N_GY = 8


def set_ends(drawn, stream_key, least, largest):
    longest = drawn.shape.index(max(drawn.shape))
    spots = []
    for shift in (0, 1):
        where = [jax.random.randint(jax.random.fold_in(stream_key, axis), (), 0, length) for axis, length in enumerate(drawn.shape)]
        where[longest] = (where[longest] + shift) % drawn.shape[longest]
        spots.append(tuple(where))
    return drawn.at[spots[0]].set(least).at[spots[1]].set(largest)


def levels(stream_key, shape, shards, smallest, largest):
    def one(axis_at, blocks):
        heights = jax.random.uniform(jax.random.fold_in(jax.random.fold_in(stream_key, 6), axis_at), (blocks,), jnp.float32, smallest / len(shards), largest / len(shards))
        return jnp.repeat(jnp.exp(heights), shape[axis_at] // blocks).reshape((-1,) + (1,) * (len(shape) - axis_at - 1))

    factor_of = one(*shards[0])
    for cut in shards[1:]:
        factor_of = factor_of * one(*cut)
    return factor_of


def assign_block(key, own, number, rows, amount, top, limit, skew):
    order = jax.random.permutation(key, amount)
    packed, usual = portions_of(amount, rows * top, limit, skew, True), portions_of(amount, rows * top, limit, skew, False)
    places = jnp.arange(amount)

    def named(tallies, turn):
        used = int((tallies > 0).sum())
        fixed = max(1, used // 4)
        passed = fixed + (places - fixed + turn * (used - fixed)) % max(1, amount - fixed)
        return jnp.zeros((amount,), jnp.int32).at[order[jnp.where(places < fixed, places, passed)]].set(jnp.asarray(tallies, jnp.int32))

    tallies = jnp.where(number % 4 == 0, named(packed, number // 4), named(usual, number - number // 4 - 1))
    mixed = jax.random.permutation(jax.random.fold_in(own, 3), amount)
    source_of, sink = mixed[0:amount // 2 * 2:2], mixed[1:amount // 2 * 2:2]
    margin = jnp.minimum(tallies[source_of] - 1, limit - tallies[sink]) // 2
    margin = jnp.where((source_of == order[0]) | (sink == order[0]) | (tallies[sink] == 0), 0, jnp.maximum(margin, 0))
    passed = jax.random.randint(jax.random.fold_in(own, 4), (amount // 2,), 0, 1 << 20) % (margin + 1)
    tallies = tallies.at[source_of].add(-passed).at[sink].add(passed)
    items = jnp.searchsorted(jnp.cumsum(tallies), jnp.arange(rows * top), side="right").astype(jnp.int32)
    grid = items.reshape(top, rows).T
    grid = grid[jax.random.permutation(jax.random.fold_in(own, 1), rows)]
    turn = jax.random.randint(jax.random.fold_in(own, 2), (rows, 1), 0, top)
    return jnp.take_along_axis(grid, (jnp.arange(top)[None, :] + turn) % top, axis=1)


def portions_of(count, total, most, slope, full):
    weights = [(1 << 20) // math.isqrt(rank ** slope) + 1 for rank in range(1, count + 1)]
    largest = most if full else min(most, max(-(-total // count), total * weights[0] // sum(weights)))
    least = 1 if total - largest >= count - 1 else 0
    given, spare = [largest] + [least] * (count - 1), total - largest - least * (count - 1)
    while spare > 0:
        movable = [i for i in range(1, count) if given[i] < largest] or [i for i in range(1, count) if given[i] < most]
        mass, left = sum([weights[i] for i in movable]), spare
        for i in movable:
            extra = min(most - given[i], max(1, left * weights[i] // mass), spare)
            given[i] = given[i] + extra
            spare = spare - extra
    return np.array(given)


def bell_draw(rng, extent, deviation, reach, shards=(), kind=jnp.bfloat16):
    values = jax.random.normal(rng, extent, jnp.float32) * deviation
    if len(shards) > 0:
        values = levels(rng, extent, shards, -0.22, 0.18) * values
    return jnp.clip(values, min=-reach, max=reach).astype(kind)


def setup_inputs(seed: int = 0) -> dict:
    key_list = jax.random.split(jax.random.key(seed), 12)
    initial_state = bell_draw(key_list[0], (2, NX, NZ, NY), 1.0, 6.0, ((1, 4), (3, 8)), jnp.float32)
    eddy_diffusivity = jnp.clip(jnp.exp(math.log(0.12) - 1.7917595 * jax.random.uniform(key_list[1], (NX, NZ, NY), jnp.float32) ** levels(key_list[1], (NX, NZ, NY), ((0, 4), (2, 8)), -0.2, 0.2)), 0.02, 0.12)
    velocity = jnp.clip(jax.random.uniform(key_list[2], (3, NX, NZ, NY), jnp.float32, -0.08, 0.08) * levels(key_list[2], (3, NX, NZ, NY), ((1, 4), (3, 8)), -0.4, 0.0), -0.08, 0.08)
    target = bell_draw(key_list[3], (2, NX, NZ, NY), 1.0, 6.0, ((1, 4), (3, 8)), jnp.float32)
    sensor_cell = set_ends(jax.random.randint(key_list[4], (SENSORS,), 0, CELLS_DEV), jax.random.fold_in(key_list[4], 1), 0, CELLS_DEV - 1).astype(jnp.int32)
    sensor_owner_keys = jax.random.split(jax.random.fold_in(key_list[5], 1), SENSORS // SENS_DEV)
    sensor_owner_turns = jax.random.permutation(jax.random.fold_in(key_list[5], 3), SENSORS // SENS_DEV)
    sensor_owner = jax.vmap(lambda own, number: assign_block(jax.random.fold_in(key_list[5], 2), own, number, SENS_DEV, OWNERS, 1, CAPS, 2))(sensor_owner_keys, sensor_owner_turns).reshape((SENSORS, 1))
    observations = bell_draw(key_list[6], (SENSORS, 2, NSTEPS), 1.0, 6.0, ((0, 32),), jnp.float32)
    actuator_block = set_ends(jax.random.randint(key_list[7], (ACTS,), 0, BLOCKS_DEV), jax.random.fold_in(key_list[7], 1), 0, BLOCKS_DEV - 1).astype(jnp.int32)
    actuator_owner_keys = jax.random.split(jax.random.fold_in(key_list[8], 1), ACTS // ACT_DEV)
    actuator_owner_turns = jax.random.permutation(jax.random.fold_in(key_list[8], 3), ACTS // ACT_DEV)
    actuator_owner = jax.vmap(lambda own, number: assign_block(jax.random.fold_in(key_list[8], 2), own, number, ACT_DEV, N_GY, 1, CAPA, 2))(actuator_owner_keys, actuator_owner_turns).reshape((ACTS, 1))
    controls = bell_draw(key_list[9], (ACTS, 2), 1.0, 6.0, ((0, 32),), jnp.float32)
    footprint = jnp.clip(1.0 * jax.random.uniform(key_list[10], (ACTS, FOOT), jnp.float32) ** levels(key_list[10], (ACTS, FOOT), ((0, 32),), -0.2, 0.2), 0.0, 1.0)
    return {"initial_state": initial_state, "eddy_diffusivity": eddy_diffusivity, "velocity": velocity, "target": target, "sensor_cell": sensor_cell, "sensor_owner": sensor_owner, "observations": observations, "actuator_block": actuator_block, "actuator_owner": actuator_owner, "controls": controls, "footprint": footprint}


prandtl = 0.85


def species_scale():
    return jnp.array([1.0, 1.0 / prandtl], jnp.float32).reshape(2, 1, 1, 1)


def shift_z(values, upward):
    blank = jnp.zeros_like(values[..., :1, :])
    if upward:
        return jnp.concatenate([values[..., 1:, :], blank], axis=-2)
    return jnp.concatenate([blank, values[..., :-1, :]], axis=-2)


def neighbours(values):
    centre = values[..., 1:-1, :, 1:-1]
    return (centre, values[..., 2:, :, 1:-1], values[..., :-2, :, 1:-1],
            values[..., 1:-1, :, 2:], values[..., 1:-1, :, :-2],
            shift_z(centre, True), shift_z(centre, False))


def diffusion(beside_all, kappas):
    centre = beside_all[0]
    summed = jnp.zeros_like(centre)
    for side_id in range(1, 7):
        summed = summed + 0.5 * (kappas[0] + kappas[side_id]) * (beside_all[side_id] - centre)
    return summed * species_scale()


def forward_step(padded, coeffs):
    beside_all = neighbours(padded)
    kappas = neighbours(coeffs[0])
    vel_x = coeffs[1][1:-1, :, 1:-1]
    vel_y = coeffs[2][1:-1, :, 1:-1]
    vel_z = coeffs[3][1:-1, :, 1:-1]
    source = coeffs[4:6][:, 1:-1, :, 1:-1]
    advect = vel_x * (beside_all[1] - beside_all[2]) + vel_y * (beside_all[3] - beside_all[4]) + vel_z * (beside_all[5] - beside_all[6])
    return beside_all[0] + diffusion(beside_all, kappas) - 0.5 * advect + source


def adjoint_step(padded, coeffs):
    beside_all = neighbours(padded)
    kappas = neighbours(coeffs[0])
    carried = jnp.zeros_like(beside_all[0])
    for axis_id, pair_ids in enumerate(((1, 2), (3, 4), (5, 6))):
        shifted = neighbours(coeffs[1 + axis_id] * padded)
        carried = carried + shifted[pair_ids[0]] - shifted[pair_ids[1]]
    return beside_all[0] + diffusion(beside_all, kappas) + 0.5 * carried


def pad_grid(values):
    return jnp.pad(values, ((0, 0), (1, 1), (0, 0), (1, 1)))


def reference(initial_state, eddy_diffusivity, velocity, target, sensor_cell, sensor_owner, observations, actuator_block, actuator_owner, controls, footprint):
    cell_total = NX * NZ * NY
    record_id = jnp.arange(ACTS, dtype=jnp.int32)
    row_x = (record_id // ACT_DEV) // N_GY
    col_y = actuator_owner[:, 0]
    blocks_z = NZ // FZ
    blocks_y = CY // FY
    block_x = actuator_block // (blocks_z * blocks_y)
    block_z = (actuator_block // blocks_y) % blocks_z
    block_y = actuator_block % blocks_y
    foot_pos = jnp.arange(FOOT, dtype=jnp.int32)
    foot_x = foot_pos // (FZ * FY)
    foot_z = (foot_pos // FY) % FZ
    foot_y = foot_pos % FY
    cell_x = row_x[:, None] * CX + block_x[:, None] * FX + foot_x[None, :]
    cell_z = block_z[:, None] * FZ + foot_z[None, :]
    cell_y = col_y[:, None] * CY + block_y[:, None] * FY + foot_y[None, :]
    act_index = ((cell_x * NZ + cell_z) * NY + cell_y).astype(jnp.int32)
    strength = controls[:, :, None] * footprint[:, None, :]
    source = jnp.zeros((2, cell_total), jnp.float32).at[:, act_index.reshape(-1)].add(
        jnp.transpose(strength, (1, 0, 2)).reshape(2, -1)).reshape(2, NX, NZ, NY)

    owner_ids = sensor_owner[:, 0]
    local_x = sensor_cell // (NZ * CY)
    local_z = (sensor_cell // CY) % NZ
    local_y = sensor_cell % CY
    sensor_index = (((owner_ids // N_GY) * CX + local_x) * NZ + local_z) * NY + (owner_ids % N_GY) * CY + local_y
    sensor_index = sensor_index.astype(jnp.int32)

    coeffs = pad_grid(jnp.concatenate([eddy_diffusivity[None], velocity, source], axis=0))

    def inject(residual):
        return jnp.zeros((2, cell_total), jnp.float32).at[:, sensor_index].add(residual).reshape(2, NX, NZ, NY)

    current = initial_state
    misfits = []
    for step_id in range(NSTEPS):
        current = forward_step(pad_grid(current), coeffs)
        values = current.reshape(2, -1)[:, sensor_index]
        misfits.append(values - observations[:, :, step_id].T)

    adjoint = current - target + inject(misfits[NSTEPS - 1])
    summed = adjoint
    for step_id in range(NSTEPS - 1, 0, -1):
        adjoint = adjoint_step(pad_grid(adjoint), coeffs) + inject(misfits[step_id - 1])
        summed = summed + adjoint
    sensitivity = adjoint_step(pad_grid(adjoint), coeffs)

    flat_summed = summed.reshape(2, -1)
    picked = flat_summed[:, act_index]
    gradient = jnp.sum(picked * footprint[None, :, :], axis=2).T
    return current, sensitivity, gradient
```

```python
import functools

import jax
import jax.numpy as jnp
from jax import lax
from jax.experimental import pallas as pl
from jax.experimental.pallas import tpu as pltpu
from jax.sharding import PartitionSpec as P

FX = 4
FZ = 8
FY = 4
CAPS = 4
CAPA = 4
FOOT = 128
RIM = 8
LANES = 128
SLOT_ROWS = 16
OBS_AT = 0
CELL_AT = 8
CTRL_AT = 16
BLOCK_AT = 18
PRANDTL = 0.85
SCALES = (1.0, 1.0 / PRANDTL)
F32 = jnp.float32
BF16 = jnp.bfloat16
VMEM_BYTES = 48 * 1024 * 1024


def iota(shape, dim):
    return lax.broadcasted_iota(jnp.int32, shape, dim)


def pieces(values, count=3):
    out = []
    for _ in range(count):
        part = values.astype(BF16)
        out.append(part)
        values = values - part.astype(F32)
    return out


def dot(a, b, dims=((1,), (0,))):
    return lax.dot_general(a, b, (dims, ((), ())), preferred_element_type=F32)


def pick(choice, values, dims=((1,), (0,)), count=3):
    total = None
    for part in pieces(values, count):
        term = dot(choice, part, dims)
        total = term if total is None else total + term
    return total


def spread(choice, values, dims=((1,), (0,)), count=3):
    total = None
    for part in pieces(values, count):
        term = dot(part, choice, dims)
        total = term if total is None else total + term
    return total


def roll(values, amount, axis):
    size = values.shape[axis]
    amount = amount % size
    if amount == 0:
        return values
    return pltpu.roll(values, amount, axis)


def swaps(count):
    even = [(i, i ^ 1) for i in range(count) if (i ^ 1) < count]
    odd = [(i, i + 1 if i % 2 else i - 1) for i in range(1, count) if (i % 2 == 0) or i + 1 < count]
    return even, odd


def exchange(values, axis):
    even, odd = swaps(lax.axis_size(axis))
    return lax.ppermute(values, axis, even), lax.ppermute(values, axis, odd)


def low_high(even, odd, is_odd):
    return jnp.where(is_odd, even, odd), jnp.where(is_odd, odd, even)


def call(body, out_shape, scratch, *args):
    return pl.pallas_call(
        body,
        out_shape=out_shape,
        scratch_shapes=scratch,
        compiler_params=pltpu.CompilerParams(vmem_limit_bytes=VMEM_BYTES),
    )(*args)


def rank_row(owner_col, owner_row):
    rows = owner_col.shape[0]
    same = (owner_col == owner_row) & (iota((rows, rows), 0) < iota((rows, rows), 1))
    return jnp.sum(same.astype(F32), axis=0, keepdims=True).astype(jnp.int32)


def rank_col(owner_col, owner_row):
    rows = owner_col.shape[0]
    same = (owner_col == owner_row) & (iota((rows, rows), 1) < iota((rows, rows), 0))
    return jnp.sum(same.astype(F32), axis=1, keepdims=True).astype(jnp.int32)


def strips_body(n_fields, state, kappa, vel, target, out):
    lane = iota((state.shape[2], LANES), 1)
    planes = []
    for ref, count in ((state, 2), (kappa, None), (vel, 3), (target, 2)):
        for f in range(count or 1):
            for p in range(FX):
                planes.append(ref[p] if count is None else ref[f, p])
    for tile in range(n_fields // 2):
        packed = jnp.zeros(lane.shape, F32)
        for g in range(2 * FX):
            moved = roll(planes[tile * 2 * FX + g], RIM + 2 * RIM * g, 1)
            packed = jnp.where(lane // (2 * RIM) == g, moved, packed)
        out[tile] = packed


def records_body(
    n_gx, n_gy, cell, s_owner, s_owner_row, obs, block, a_owner, a_owner_row, ctrl, foot, out, s_meta, a_meta
):
    sens, acts = cell.shape[0], block.shape[0]
    owners = n_gx * n_gy
    s_meta[...] = jnp.zeros((sens, LANES), F32)
    s_meta[:, OBS_AT : OBS_AT + 8] = obs[...]
    s_meta[:, CELL_AT : CELL_AT + 1] = (cell[...] + 1).astype(F32)
    a_meta[...] = jnp.zeros((acts, LANES), F32)
    a_meta[:, CTRL_AT : CTRL_AT + 2] = ctrl[...]
    a_meta[:, BLOCK_AT : BLOCK_AT + 1] = (block[...] + 1).astype(F32)
    s_row, a_row = s_owner_row[...], a_owner_row[...]
    s_rank = rank_row(s_owner[...], s_row)
    a_rank = rank_row(a_owner[...], a_row)
    s_all, a_all, f_all = s_meta[...], a_meta[...], foot[...]
    sens_rows = jnp.zeros((owners, LANES), F32)
    act_rows = jnp.zeros((n_gy, LANES), F32)
    foot_rows = []
    for k in range(CAPS):
        choice = ((s_row == iota((owners, sens), 0)) & (s_rank == k)).astype(BF16)
        sens_rows = sens_rows + roll(pick(choice, s_all), 32 * k, 1)
        choice = ((a_row == iota((n_gy, acts), 0)) & (a_rank == k)).astype(BF16)
        act_rows = act_rows + roll(pick(choice, a_all), 32 * k, 1)
        foot_rows.append(pick(choice, f_all))
    gy_of = iota((n_gy, LANES), 0)
    meta = jnp.concatenate(
        [sens_rows[i * n_gy : (i + 1) * n_gy] + act_rows for i in range(n_gx)], axis=0
    )
    meta_gy = iota((owners, LANES), 0) % n_gy
    for t in range(3):
        def moved(values, at):
            if t == 0:
                return jnp.where(at == 0, 0.0, roll(values, 1, 0))
            if t == 2:
                return jnp.where(at == n_gy - 1, 0.0, roll(values, values.shape[0] - 1, 0))
            return values
        for k in range(CAPA):
            rows = moved(foot_rows[k], gy_of)
            for i in range(n_gx):
                out[i * n_gy : (i + 1) * n_gy, 4 * t + k, :] = rows
        out[:, 12 + t, :] = moved(meta, meta_gy)
    out[:, 15, :] = jnp.zeros((owners, LANES), F32)


def rim_body(even, odd, out):
    is_odd = lax.rem(lax.axis_index("gy"), 2) == 1
    for tile in range(out.shape[0]):
        left, right = low_high(even[tile], odd[tile], is_odd)
        lane = iota(left.shape, 1)
        out[tile] = jnp.where(lane % (2 * RIM) < RIM, roll(right, -RIM, 1), roll(left, RIM, 1))


def source_body(n_gx, n_gy, height, wide_y, got, source, own_foot, own_meta, table, stacked, placing):
    records = n_gy * SLOT_ROWS
    blocks_y = wide_y // FY
    row_id = lax.axis_index("gx")
    r_of, r_to = iota((records, records), 0), iota((records, records), 1)
    slot = r_of % SLOT_ROWS
    moves = [
        (
            (slot < 12) & (slot % 4 == k) & (r_to == r_of - slot + 12 + slot // 4)
        ).astype(BF16)
        for k in range(CAPA)
    ]
    q_of, l_of = iota((FOOT, FOOT), 0), iota((FOOT, FOOT), 1)
    unpack = (l_of == (q_of % 32) * FY + q_of // 32).astype(BF16)
    for q in range(3):
        row = row_id + (q - 1)
        inside = (row >= 0) & (row < n_gx)
        base = jnp.clip(row, 0, n_gx - 1) * n_gy
        records_in = got[pl.ds(base, n_gy)].reshape(records, LANES)
        meta = jnp.zeros((records, LANES), F32)
        for k in range(CAPA):
            meta = meta + pick(moves[k], roll(records_in, -32 * k, 1))
        meta = jnp.where(inside, meta, 0.0)
        meta_t = meta.T
        block_row = meta_t[BLOCK_AT : BLOCK_AT + 1, :].astype(jnp.int32) - 1
        bz_row = block_row // blocks_y
        foot_t = pick(unpack, records_in, ((1,), (1,)))
        block_col = meta[:, BLOCK_AT : BLOCK_AT + 1].astype(jnp.int32) - 1
        by = block_col % blocks_y
        side = (iota((records, 1), 0) % SLOT_ROWS) // 4
        usable = (block_col >= 0) & (
            (side == 1)
            | ((side == 0) & (by * FY >= wide_y - RIM))
            | ((side == 2) & (by * FY < RIM))
        )
        start = jnp.where(side == 1, by * FY, wide_y + by * FY)
        start = jnp.where(usable, start, -FY)
        for fy in range(FY):
            placing[fy * records : (fy + 1) * records, :] = (
                iota((records, 2 * wide_y), 1) == start + fy
            ).astype(BF16)
        for s in range(2):
            force = meta_t[CTRL_AT + s : CTRL_AT + s + 1, :]
            for fy in range(FY):
                for x in range(FX):
                    piece = foot_t[fy * 32 + x * FZ : fy * 32 + (x + 1) * FZ, :]
                    scaled = piece * force
                    for bz in range(height // FZ):
                        rows = slice(x * height + bz * FZ, x * height + (bz + 1) * FZ)
                        stacked[rows, fy * records : (fy + 1) * records] = jnp.where(
                            bz_row == bz, scaled, 0.0
                        )
                        if q == 1 and s == 0:
                            own_foot[fy, rows, :] = jnp.where(bz_row == bz, piece, 0.0)
            source[s, q] = spread(placing[...], stacked[...])
        if q == 1:
            own_meta[...] = jnp.where((side == 1) & (block_col >= 0), meta, 0.0)
    devices = got.shape[0]
    for n, t in enumerate((1, 0, 2)):
        rows = got[:, 12 + t, :]
        for k in range(CAPS):
            at = (n * CAPS + k) * devices
            table[at : at + devices, :] = roll(rows, -32 * k, 1)


def rim_tile(packed, group):
    lane = iota(packed.shape, 1)
    right = roll(packed, -2 * RIM * group, 1)
    left = roll(packed, LANES - 2 * RIM - 2 * RIM * group, 1)
    return jnp.where(lane < RIM, right, jnp.where(lane >= LANES - RIM, left, 0.0))


def extended(field, main, main_e, main_o, rim, rim_e, rim_o, is_odd, x):
    tile, group = field // 2, (field % 2) * FX + x % FX
    if x // FX == 1:
        centre, halo = main[field, x % FX], rim[tile]
    elif x // FX == 0:
        centre = jnp.where(is_odd, main_e[field, x], main_o[field, x])
        halo = jnp.where(is_odd, rim_e[tile], rim_o[tile])
    else:
        centre = jnp.where(is_odd, main_o[field, x - 2 * FX], main_e[field, x - 2 * FX])
        halo = jnp.where(is_odd, rim_o[tile], rim_e[tile])
    return centre, rim_tile(halo, group)


def build_coeffs(n_gx, n_gy, refs, half_k, half_u, coeffs):
    main, main_e, main_o, rim, rim_e, rim_o = refs
    row_id, col_id = lax.axis_index("gx"), lax.axis_index("gy")
    is_odd = lax.rem(row_id, 2) == 1
    wide = 3 * FX
    for x in range(wide):
        for field in range(2, 6):
            centre, halo = extended(field, *refs, is_odd, x)
            dest = half_k.at[x] if field == 2 else half_u.at[field - 3, x]
            dest[:, :LANES] = 0.5 * centre
            dest[:, LANES:] = 0.5 * halo
    height = half_k.shape[1]
    shape = (height, 2 * LANES)
    lane, z = iota(shape, 1), iota(shape, 0)

    def lane_in(at):
        return (
            (at < LANES)
            | ((at < LANES + RIM) & (col_id < n_gy - 1))
            | ((at >= 2 * LANES - RIM) & (col_id > 0))
        )

    here = lane_in(lane)
    ahead = here & lane_in((lane + 1) % (2 * LANES))
    behind = here & lane_in((lane + 2 * LANES - 1) % (2 * LANES))

    def plane_in(x):
        return (
            ((x >= FX) | (row_id > 0)) & ((x < 2 * FX) | (row_id < n_gx - 1))
        )

    def one(x, carry):
        k = half_k[x]
        before, after = half_k[jnp.maximum(x - 1, 0)], half_k[jnp.minimum(x + 1, wide - 1)]
        inside = plane_in(x)
        faces = (
            k + after,
            k + before,
            k + roll(k, -1, 1),
            k + roll(k, 1, 1),
            k + jnp.where(z == height - 1, 0.0, roll(k, -1, 0)),
            k + jnp.where(z == 0, 0.0, roll(k, 1, 0)),
        )
        masks = (
            here & inside & plane_in(x + 1),
            here & inside & plane_in(x - 1),
            ahead & inside,
            behind & inside,
            here & inside & (z < height - 1),
            here & inside & (z > 0),
        )
        total = (faces[0] + faces[1]) + (faces[2] + faces[3]) + (faces[4] + faces[5])
        for s in range(2):
            coeffs[s, 6, x] = 1.0 - SCALES[s] * total
            for side in range(6):
                drift = half_u[side // 2, x]
                value = SCALES[s] * faces[side]
                value = value - drift if side % 2 == 0 else value + drift
                coeffs[s, side, x] = jnp.where(masks[side], value, 0.0)
        return carry

    lax.fori_loop(0, wide, one, 0)


def cell_parts(table_col, own_count, wide_y):
    cell = table_col.astype(jnp.int32) - 1
    return cell // wide_y, cell % wide_y, cell >= 0


def forward_body(n_gx, n_gy, steps, main, main_e, main_o, rim, rim_e, rim_o, source, table, target, final, sent, half_k, half_u, coeffs, cur):
    refs = (main, main_e, main_o, rim, rim_e, rim_o)
    is_odd = lax.rem(lax.axis_index("gx"), 2) == 1
    height = half_k.shape[1]
    build_coeffs(n_gx, n_gy, refs, half_k, half_u, coeffs)
    wide = 3 * FX
    for x in range(wide):
        for s in range(2):
            centre, halo = extended(s, *refs, is_odd, x)
            cur[0, s, x, :, :LANES] = centre
            cur[0, s, x, :, LANES:] = halo
    slots = table.shape[0]
    own = slots // 3
    records = table[...]
    cell = records[:, CELL_AT : CELL_AT + 1].astype(jnp.int32) - 1
    spot = cell // LANES
    at_y = cell % LANES
    slot_id = iota((slots, 1), 0)
    live = (cell >= 0) & (
        (slot_id < own)
        | ((slot_id < 2 * own) & (at_y >= LANES - RIM))
        | ((slot_id >= 2 * own) & (at_y < RIM))
    )
    cells = FX * height
    rows_hot = ((iota((slots, cells), 1) == spot) & live).astype(BF16)
    lane_hot = (iota((slots, LANES), 1) == at_y) & live
    rows_hot_t = None
    lane = iota((slots, LANES), 1)
    residuals = jnp.where(lane == CELL_AT, jnp.where(live, records, 0.0), 0.0)
    for n in range(steps):
        now, later = n % 2, (n + 1) % 2

        def one(x, carry):
            for s in range(2):
                c = cur[now, s, x]
                value = coeffs[s, 6, x] * c + source[s, x]
                value = value + coeffs[s, 0, x] * cur[now, s, x + 1]
                value = value + coeffs[s, 1, x] * cur[now, s, x - 1]
                value = value + coeffs[s, 2, x] * roll(c, -1, 1)
                value = value + coeffs[s, 3, x] * roll(c, 1, 1)
                value = value + coeffs[s, 4, x] * roll(c, -1, 0)
                value = value + coeffs[s, 5, x] * roll(c, 1, 0)
                cur[later, s, x] = value
            return carry

        lax.fori_loop(n + 1, wide - n - 1, one, 0)
        for s in range(2):
            field = cur[later, s, FX : 2 * FX].reshape(cells, 2 * LANES)
            got = jnp.concatenate(
                [
                    pick(rows_hot[:own], field[:, :LANES]),
                    pick(rows_hot[own:], field[:, LANES:]),
                ],
                axis=0,
            )
            value = jnp.sum(jnp.where(lane_hot, got, 0.0), axis=1, keepdims=True)
            at = OBS_AT + s * steps + n
            value = jnp.where(live, value - records[:, at : at + 1], 0.0)
            residuals = jnp.where(lane == at, value, residuals)
    last = steps % 2
    spot_row = residuals.T[CELL_AT : CELL_AT + 1, :].astype(jnp.int32) - 1
    spot_row = jnp.where(spot_row >= 0, spot_row // LANES, -1)
    rows_hot_t = (iota((cells, slots), 0) == spot_row).astype(BF16)
    sent_rim = jnp.zeros((height, LANES), F32)
    rim_lane = iota((height, LANES), 1)
    for s in range(2):
        at = OBS_AT + s * steps + steps - 1
        value = jnp.where(lane_hot, residuals[:, at : at + 1], 0.0)
        put_main = pick(rows_hot_t[:, :own], value[:own])
        put_rim = pick(rows_hot_t[:, own:], value[own:])
        for p in range(FX):
            rows = slice(p * height, (p + 1) * height)
            got = cur[last, s, FX + p]
            final[s, p] = got[:, :LANES]
            sent[(s * FX + p) * height : (s * FX + p + 1) * height, :] = (
                got[:, :LANES] - target[s, p] + put_main[rows]
            )
            halo = got[:, LANES:] - rim_tile(rim[3], s * FX + p) + put_rim[rows]
            g = s * FX + p
            inner = rim_lane - 2 * RIM * g
            right = roll(halo, 2 * RIM * g, 1)
            left = roll(halo, 2 * RIM * g + 2 * RIM, 1)
            sent_rim = jnp.where((inner >= 0) & (inner < RIM), right, sent_rim)
            sent_rim = jnp.where((inner >= RIM) & (inner < 2 * RIM), left, sent_rim)
    base = 2 * FX * height
    sent[base : base + height, :] = sent_rim
    rows = slots // 8
    packed = jnp.zeros((rows, LANES), F32)
    pack_lane = iota((rows, LANES), 1)
    for b in range(8):
        packed = jnp.where(
            pack_lane // 16 == b, roll(residuals[b * rows : (b + 1) * rows], 16 * b, 1), packed
        )
    sent[base + height : base + height + rows, :] = packed


def adjoint_body(n_gx, n_gy, steps, main, main_e, main_o, rim, rim_e, rim_o, sent, sent_e, sent_o, own_foot, own_meta, first, gradient, half_k, half_u, coeffs, cur, puts, summed):
    refs = (main, main_e, main_o, rim, rim_e, rim_o)
    is_odd = lax.rem(lax.axis_index("gx"), 2) == 1
    height = half_k.shape[1]
    build_coeffs(n_gx, n_gy, refs, half_k, half_u, coeffs)
    wide = 3 * FX
    cells = FX * height
    base = 2 * FX * height
    rows = sent.shape[0] - base - height
    slots = rows * 8
    own = slots // 3
    for q in range(3):
        def take(lo, hi):
            if q == 1:
                return sent[lo:hi, :]
            if q == 0:
                return jnp.where(is_odd, sent_e[lo:hi, :], sent_o[lo:hi, :])
            return jnp.where(is_odd, sent_o[lo:hi, :], sent_e[lo:hi, :])
        packed_rim = take(base, base + height)
        for s in range(2):
            for p in range(FX):
                g = s * FX + p
                cur[0, s, q * FX + p, :, :LANES] = take(g * height, (g + 1) * height)
                cur[0, s, q * FX + p, :, LANES:] = rim_tile(packed_rim, g)
        packed = take(base + height, base + height + rows)
        records = jnp.concatenate([roll(packed, -16 * b, 1) for b in range(8)], axis=0)
        cell = records[:, CELL_AT : CELL_AT + 1].astype(jnp.int32) - 1
        live = cell >= 0
        lane_hot = (iota((slots, LANES), 1) == cell % LANES) & live
        cell_row = records.T[CELL_AT : CELL_AT + 1, :].astype(jnp.int32) - 1
        cell_row = jnp.where(cell_row >= 0, cell_row // LANES, -1)
        hot_t = (iota((cells, slots), 0) == cell_row).astype(BF16)
        for n in range(steps - 1):
            for s in range(2):
                at = OBS_AT + s * steps + n
                value = jnp.where(lane_hot, records[:, at : at + 1], 0.0)
                for side, part in enumerate((slice(0, own), slice(own, slots))):
                    put = pick(hot_t[:, part], value[part])
                    puts[n, s, q * FX : (q + 1) * FX, :, side * LANES : (side + 1) * LANES] = (
                        put.reshape(FX, height, LANES)
                    )
    for s in range(2):
        summed[s] = cur[0, s, FX : 2 * FX, :, :LANES]
    for turn in range(steps):
        now, later = turn % 2, (turn + 1) % 2
        n = steps - 2 - turn

        def one(x, carry):
            for s in range(2):
                w = cur[now, s, x]
                value = coeffs[s, 6, x] * w
                if n >= 0:
                    value = value + puts[n, s, x]
                value = value + coeffs[s, 1, x + 1] * cur[now, s, x + 1]
                value = value + coeffs[s, 0, x - 1] * cur[now, s, x - 1]
                value = value + roll(coeffs[s, 3, x] * w, -1, 1)
                value = value + roll(coeffs[s, 2, x] * w, 1, 1)
                value = value + roll(coeffs[s, 5, x] * w, -1, 0)
                value = value + roll(coeffs[s, 4, x] * w, 1, 0)
                cur[later, s, x] = value
            return carry

        lax.fori_loop(turn + 1, wide - turn - 1, one, 0)
        for s in range(2):
            if n >= 0:
                summed[s] = summed[s] + cur[later, s, FX : 2 * FX, :, :LANES]
            else:
                first[s] = cur[later, s, FX : 2 * FX, :, :LANES]
    records = own_meta.shape[0]
    block = own_meta[:, BLOCK_AT : BLOCK_AT + 1].astype(jnp.int32) - 1
    start = jnp.where(block >= 0, (block % (LANES // FY)) * FY, -FY)
    lane = iota((records, LANES), 1)
    out_row = iota((n_gy, records), 0)
    out_from = iota((n_gy, records), 1) // SLOT_ROWS
    for s in range(2):
        field = summed[s].reshape(cells, LANES)
        total = jnp.zeros((1, records), F32)
        for fy in range(FY):
            hot = (lane == start + fy).astype(BF16)
            seen = spread(hot, field, ((1,), (1,)))
            total = total + jnp.sum(seen * own_foot[fy], axis=0, keepdims=True)
        gradient[:, s, :] = jnp.where(out_row == out_from, total, 0.0)


def returned_body(got, owner, owner_row, out):
    acts = owner.shape[0]
    n_gy, _, records = got.shape
    rank = rank_col(owner[...], owner_row[...])
    choice = (owner[...] == iota((acts, n_gy), 1)).astype(BF16)
    at = lax.axis_index("gy") * SLOT_ROWS + CAPA + rank
    hot = iota((acts, records), 1) == at
    for s in range(2):
        rows = pick(choice, got[:, s, :])
        out[:, s : s + 1] = jnp.sum(jnp.where(hot, rows, 0.0), axis=1, keepdims=True)


def per_device(
    initial_state,
    eddy_diffusivity,
    velocity,
    target,
    sensor_cell,
    sensor_owner,
    observations,
    actuator_block,
    actuator_owner,
    controls,
    footprint,
):
    _, wide_x, height, wide_y = initial_state.shape
    steps = observations.shape[2]
    n_gx, n_gy = lax.axis_size("gx"), lax.axis_size("gy")
    devices = n_gx * n_gy
    sens, acts = sensor_cell.shape[0], actuator_block.shape[0]
    records = n_gy * SLOT_ROWS
    shape = jax.ShapeDtypeStruct
    vmem = pltpu.VMEM
    s_owner_row = sensor_owner.reshape(1, sens)
    a_owner_row = actuator_owner.reshape(1, acts)

    main = jnp.concatenate([initial_state, eddy_diffusivity[None], velocity], axis=0)
    outgoing = call(
        functools.partial(records_body, n_gx, n_gy),
        shape((devices, SLOT_ROWS, LANES), F32),
        [vmem((sens, LANES), F32), vmem((acts, LANES), F32)],
        sensor_cell.reshape(sens, 1),
        sensor_owner,
        s_owner_row,
        observations.reshape(sens, 2 * steps),
        actuator_block.reshape(acts, 1),
        actuator_owner,
        a_owner_row,
        controls,
        footprint,
    )
    strips = call(
        functools.partial(strips_body, 8),
        shape((4, height, LANES), F32),
        [],
        initial_state,
        eddy_diffusivity,
        velocity,
        target,
    )
    got = lax.all_to_all(outgoing, ("gx", "gy"), split_axis=0, concat_axis=0, tiled=True)
    main_e, main_o = exchange(main, "gx")
    strips_e, strips_o = exchange(strips, "gy")
    rim = call(rim_body, shape((4, height, LANES), F32), [], strips_e, strips_o)
    rim_e, rim_o = exchange(rim[:3], "gx")
    source, own_foot, own_meta, table = call(
        functools.partial(source_body, n_gx, n_gy, height, wide_y),
        (
            shape((2, 3, FX * height, 2 * LANES), F32),
            shape((FY, FX * height, records), F32),
            shape((records, LANES), F32),
            shape((3 * CAPS * devices, LANES), F32),
        ),
        [vmem((FX * height, FY * records), F32), vmem((FY * records, 2 * LANES), BF16)],
        got,
    )
    source = source.reshape(2, 3 * FX, height, 2 * LANES)
    slots = 3 * CAPS * devices
    sent_rows = 2 * FX * height + height + slots // 8
    fields = [
        vmem((3 * FX, height, 2 * LANES), F32),
        vmem((3, 3 * FX, height, 2 * LANES), F32),
        vmem((2, 7, 3 * FX, height, 2 * LANES), F32),
        vmem((2, 2, 3 * FX, height, 2 * LANES), F32),
    ]
    final, sent = call(
        functools.partial(forward_body, n_gx, n_gy, steps),
        (shape((2, FX, height, LANES), F32), shape((sent_rows, LANES), F32)),
        fields,
        main, main_e, main_o, rim, rim_e, rim_o, source, table, target,
    )
    sent_e, sent_o = exchange(sent, "gx")
    first, gradient = call(
        functools.partial(adjoint_body, n_gx, n_gy, steps),
        (shape((2, FX, height, LANES), F32), shape((n_gy, 2, records), F32)),
        fields
        + [
            vmem((steps - 1, 2, 3 * FX, height, 2 * LANES), F32),
            vmem((2, FX, height, LANES), F32),
        ],
        main, main_e, main_o, rim, rim_e, rim_o, sent, sent_e, sent_o, own_foot, own_meta,
    )
    back = lax.all_to_all(gradient, "gy", split_axis=0, concat_axis=0, tiled=True)
    returned = call(
        returned_body, shape((acts, 2), F32), [], back, actuator_owner, a_owner_row
    )
    return (final, first, returned)


def solution(mesh):
    in_specs = (
        P(None, "gx", None, "gy"),
        P("gx", None, "gy"),
        P(None, "gx", None, "gy"),
        P(None, "gx", None, "gy"),
        P(("gx", "gy")),
        P(("gx", "gy"), None),
        P(("gx", "gy"), None, None),
        P(("gx", "gy")),
        P(("gx", "gy"), None),
        P(("gx", "gy"), None),
        P(("gx", "gy"), None),
    )
    out_specs = (P(None, "gx", None, "gy"), P(None, "gx", None, "gy"), P(("gx", "gy"), None))
    return jax.shard_map(
        per_device, mesh=mesh, in_specs=in_specs, out_specs=out_specs, check_vma=False
    )
```

```python
import functools

import jax
import jax.numpy as jnp
from jax import lax
from jax.experimental import pallas as pl
from jax.experimental.pallas import tpu as pltpu
from jax.sharding import PartitionSpec as P

FX = 4
FZ = 8
FY = 4
CAPS = 4
CAPA = 4
FOOT = 128
RIM = 8
LANES = 128
SLOT_ROWS = 16
OBS_AT = 0
CELL_AT = 8
CTRL_AT = 16
BLOCK_AT = 18
PRANDTL = 0.85
SCALES = (1.0, 1.0 / PRANDTL)
F32 = jnp.float32
BF16 = jnp.bfloat16
COST = pl.CostEstimate(flops=0, transcendentals=0, bytes_accessed=60 * 1024 * 1024)
VMEM_BYTES = 20 * 1024 * 1024


def iota(shape, dim):
    return lax.broadcasted_iota(jnp.int32, shape, dim)


def pieces(values, count=3):
    out = []
    for _ in range(count):
        part = values.astype(BF16)
        out.append(part)
        values = values - part.astype(F32)
    return out


def dot(a, b, dims=((1,), (0,))):
    return lax.dot_general(a, b, (dims, ((), ())), preferred_element_type=F32)


def pick(choice, values, dims=((1,), (0,)), count=3):
    total = None
    for part in pieces(values, count):
        term = dot(choice, part, dims)
        total = term if total is None else total + term
    return total


def spread(choice, values, dims=((1,), (0,)), count=3):
    total = None
    for part in pieces(values, count):
        term = dot(part, choice, dims)
        total = term if total is None else total + term
    return total


def roll(values, amount, axis):
    size = values.shape[axis]
    amount = amount % size
    if amount == 0:
        return values
    return pltpu.roll(values, amount, axis)


def swaps(count):
    even = [(i, i ^ 1) for i in range(count) if (i ^ 1) < count]
    odd = [(i, i + 1 if i % 2 else i - 1) for i in range(1, count) if (i % 2 == 0) or i + 1 < count]
    return even, odd


def exchange(values, axis):
    even, odd = swaps(lax.axis_size(axis))
    return lax.ppermute(values, axis, even), lax.ppermute(values, axis, odd)


def low_high(even, odd, is_odd):
    return jnp.where(is_odd, even, odd), jnp.where(is_odd, odd, even)


def call(body, out_shape, scratch, *args, cost=None):
    return pl.pallas_call(
        body,
        cost_estimate=cost,
        out_shape=out_shape,
        scratch_shapes=scratch,
        compiler_params=pltpu.CompilerParams(vmem_limit_bytes=VMEM_BYTES),
    )(*args)


def slot_choices(owner_row, owners, count):
    records = owner_row.shape[1]
    named = owner_row == iota((owners, records), 0)
    earlier = (iota((records, records), 0) < iota((records, records), 1)).astype(BF16)
    rank = dot(named.astype(BF16), earlier)
    return [(named & (rank == k)).astype(BF16) for k in range(count)]


def records_out_body(n_gx, n_gy, cell, s_owner, obs, block, a_owner, ctrl, foot, out, s_meta, a_meta):
    owners = n_gx * n_gy
    steps = obs.shape[1]
    s_meta[...] = jnp.zeros(s_meta.shape, F32)
    for s in range(2):
        s_meta[OBS_AT + s * steps : OBS_AT + (s + 1) * steps, :] = obs[s]
    s_meta[CELL_AT : CELL_AT + 1, :] = (cell[...] + 1).astype(F32)
    a_meta[...] = jnp.zeros(a_meta.shape, F32)
    a_meta[CTRL_AT : CTRL_AT + 2, :] = ctrl[...]
    a_meta[BLOCK_AT : BLOCK_AT + 1, :] = (block[...] + 1).astype(F32)
    s_all, a_all, f_all = s_meta[...], a_meta[...], foot[...]
    s_choice = slot_choices(s_owner[...], owners, CAPS)
    a_choice = slot_choices(a_owner[...], n_gy, CAPA)
    sens_rows = jnp.zeros((owners, LANES), F32)
    act_rows = jnp.zeros((n_gy, LANES), F32)
    foot_rows = []
    for k in range(CAPS):
        sens_rows = sens_rows + roll(pick(s_choice[k], s_all, ((1,), (1,))), 32 * k, 1)
        act_rows = act_rows + roll(pick(a_choice[k], a_all, ((1,), (1,))), 32 * k, 1)
        foot_rows.append(pick(a_choice[k], f_all))
    gy_of = iota((n_gy, LANES), 0)
    meta = jnp.concatenate(
        [sens_rows[i * n_gy : (i + 1) * n_gy] + act_rows for i in range(n_gx)], axis=0
    )
    meta_gy = iota((owners, LANES), 0) % n_gy
    for t in range(3):
        def moved(values, at):
            if t == 0:
                return jnp.where(at == 0, 0.0, roll(values, 1, 0))
            if t == 2:
                return jnp.where(at == n_gy - 1, 0.0, roll(values, values.shape[0] - 1, 0))
            return values
        for k in range(CAPA):
            rows = moved(foot_rows[k], gy_of)
            for i in range(n_gx):
                out[i * n_gy : (i + 1) * n_gy, 4 * t + k, :] = rows
        out[:, 12 + t, :] = moved(meta, meta_gy)
    out[:, 15, :] = jnp.zeros((owners, LANES), F32)


def strips_body(state, kappa, vel, target, out):
    lane = iota((state.shape[2], LANES), 1)
    fields = [state.at[0], state.at[1], kappa, vel.at[0], vel.at[1], vel.at[2], target.at[0], target.at[1]]
    for tile in range(4):
        packed = jnp.zeros(lane.shape, F32)
        for g in range(2 * FX):
            plane = fields[2 * tile + g // FX][g % FX]
            packed = jnp.where(lane // (2 * RIM) == g, roll(plane, RIM + 2 * RIM * g, 1), packed)
        out[tile] = packed


def rim_body(even, odd, out):
    is_odd = lax.rem(lax.axis_index("gy"), 2) == 1
    for tile in range(out.shape[0]):
        left, right = low_high(even[tile], odd[tile], is_odd)
        lane = iota(left.shape, 1)
        out[tile] = jnp.where(lane % (2 * RIM) < RIM, roll(right, -RIM, 1), roll(left, RIM, 1))


def rim_tile(packed, group):
    lane = iota(packed.shape, 1)
    right = roll(packed, -2 * RIM * group, 1)
    left = roll(packed, LANES - 2 * RIM - 2 * RIM * group, 1)
    return jnp.where(lane < RIM, right, jnp.where(lane >= LANES - RIM, left, 0.0))


def extended(field, main, main_e, main_o, rim, rim_e, rim_o, is_odd, x):
    tile, group = field // 2, (field % 2) * FX + x % FX
    if x // FX == 1:
        centre, halo = main[field, x % FX], rim[tile]
    elif x // FX == 0:
        centre = jnp.where(is_odd, main_e[field, x], main_o[field, x])
        halo = jnp.where(is_odd, rim_e[tile], rim_o[tile])
    else:
        centre = jnp.where(is_odd, main_o[field, x - 2 * FX], main_e[field, x - 2 * FX])
        halo = jnp.where(is_odd, rim_o[tile], rim_e[tile])
    return centre, rim_tile(halo, group)


def records_in_body(
    n_gx, n_gy, height, wide_y, got, source, foot_hot, foot_own, spot_hot, lane_hot, readings, stacked, placing, table
):
    records = n_gy * SLOT_ROWS
    devices = n_gx * n_gy
    blocks_y = wide_y // FY
    row_id = lax.axis_index("gx")
    r_of, r_to = iota((records, records), 0), iota((records, records), 1)
    slot = r_of % SLOT_ROWS
    moves = [
        ((slot < 12) & (slot % 4 == k) & (r_to == r_of - slot + 12 + slot // 4)).astype(BF16)
        for k in range(CAPA)
    ]
    q_of, l_of = iota((FOOT, FOOT), 0), iota((FOOT, FOOT), 1)
    unpack = (l_of == (q_of % 32) * FY + q_of // 32).astype(BF16)
    side = (iota((records, 1), 0) % SLOT_ROWS) // 4
    wide_lane = iota((records, 2 * wide_y), 1)
    for q in range(3):
        row = row_id + (q - 1)
        inside = (row >= 0) & (row < n_gx)
        base = jnp.clip(row, 0, n_gx - 1) * n_gy
        records_in = got[pl.ds(base, n_gy)].reshape(records, LANES)
        meta = jnp.zeros((records, LANES), F32)
        for k in range(CAPA):
            meta = meta + pick(moves[k], roll(records_in, -32 * k, 1))
        meta = jnp.where(inside, meta, 0.0)
        meta_t = meta.T
        block_row = meta_t[BLOCK_AT : BLOCK_AT + 1, :].astype(jnp.int32) - 1
        bz_row = block_row // blocks_y
        foot_t = pick(unpack, records_in, ((1,), (1,)))
        block_col = meta[:, BLOCK_AT : BLOCK_AT + 1].astype(jnp.int32) - 1
        by = block_col % blocks_y
        usable = (block_col >= 0) & (
            (side == 1)
            | ((side == 0) & (by * FY >= wide_y - RIM))
            | ((side == 2) & (by * FY < RIM))
        )
        start = jnp.where(side == 1, by * FY, wide_y + by * FY)
        start = jnp.where(usable, start, -FY)
        for fy in range(FY):
            hot = (wide_lane == start + fy).astype(BF16)
            placing[fy * records : (fy + 1) * records, :] = hot
            if q == 1:
                own_start = jnp.where((side == 1) & usable, start, -FY)
                own = (iota((records, wide_y), 1) == own_start + fy).astype(BF16)
                foot_hot[fy * records : (fy + 1) * records, :] = own
        for s in range(2):
            force = meta_t[CTRL_AT + s : CTRL_AT + s + 1, :]
            for fy in range(FY):
                lanes = slice(fy * records, (fy + 1) * records)
                for x in range(FX):
                    piece = foot_t[fy * 32 + x * FZ : fy * 32 + (x + 1) * FZ, :]
                    scaled = piece * force
                    for bz in range(height // FZ):
                        rows = slice(x * height + bz * FZ, x * height + (bz + 1) * FZ)
                        stacked[rows, lanes] = jnp.where(bz_row == bz, scaled, 0.0)
                        if q == 1 and s == 0:
                            foot_own[rows, lanes] = jnp.where(bz_row == bz, piece, 0.0)
            source[s, q] = spread(placing[...], stacked[...], count=2)
    slots = 3 * CAPS * devices
    for n, t in enumerate((1, 0, 2)):
        rows = got[:, 12 + t, :]
        for k in range(CAPS):
            at = (n * CAPS + k) * devices
            table[at : at + devices, :] = roll(rows, -32 * k, 1)
    for part in range(slots // LANES):
        lanes = slice(part * LANES, (part + 1) * LANES)
        turned = table[lanes, :].T
        cell = turned[CELL_AT : CELL_AT + 1, :].astype(jnp.int32) - 1
        at_y = cell % LANES
        slot_id = iota((1, LANES), 1) + part * LANES
        live = (cell >= 0) & (
            (slot_id < slots // 3)
            | ((slot_id < slots // 3 * 2) & (at_y >= LANES - RIM))
            | ((slot_id >= slots // 3 * 2) & (at_y < RIM))
        )
        cell = jnp.where(live, cell, -1)
        readings[0:8, lanes] = turned[OBS_AT : OBS_AT + 8]
        readings[8:16, lanes] = jnp.broadcast_to((cell + 1).astype(F32), (8, LANES))
        spot, lane = hot_pair(cell, FX * height)
        spot_hot[:, lanes] = spot
        lane_hot[:, lanes] = lane


def hot_pair(cell, cells):
    spot = jnp.where(cell >= 0, cell // LANES, -1)
    at_y = jnp.where(cell >= 0, cell % LANES, -1)
    slots = cell.shape[1]
    return (
        (iota((cells, slots), 0) == spot).astype(BF16),
        (iota((LANES, slots), 0) == at_y).astype(BF16),
    )


def coeffs_body(main, main_e, main_o, rim, rim_e, rim_o, coeffs, start, half_k):
    refs = (main, main_e, main_o, rim, rim_e, rim_o)
    is_odd = lax.rem(lax.axis_index("gx"), 2) == 1
    wide = 3 * FX
    height = half_k.shape[1]
    shape = (height, 2 * LANES)
    z = iota(shape, 0)
    for x in range(wide):
        centre, halo = extended(2, *refs, is_odd, x)
        half_k[x, :, :LANES] = 0.5 * centre
        half_k[x, :, LANES:] = 0.5 * halo
        for s in range(2):
            centre, halo = extended(s, *refs, is_odd, x)
            start[s, x, :, :LANES] = centre
            start[s, x, :, LANES:] = halo
    for x in range(wide):
        k = half_k[x]
        faces = (
            k + half_k[min(x + 1, wide - 1)],
            k + half_k[max(x - 1, 0)],
            k + roll(k, -1, 1),
            k + roll(k, 1, 1),
            k + jnp.where(z == height - 1, 0.0, roll(k, -1, 0)),
            k + jnp.where(z == 0, 0.0, roll(k, 1, 0)),
        )
        total = (faces[0] + faces[1]) + (faces[2] + faces[3]) + (faces[4] + faces[5])
        drift = []
        for axis in range(3):
            centre, halo = extended(3 + axis, *refs, is_odd, x)
            drift.append(0.5 * jnp.concatenate([centre, halo], axis=1))
        for s in range(2):
            coeffs[s, 6, x] = 1.0 - SCALES[s] * total
            for face in range(6):
                value = faces[face] if s == 0 else SCALES[s] * faces[face]
                value = value - drift[face // 2] if face % 2 == 0 else value + drift[face // 2]
                if face == 4:
                    value = jnp.where(z == height - 1, 0.0, value)
                if face == 5:
                    value = jnp.where(z == 0, 0.0, value)
                coeffs[s, face, x] = value


def inside_rows(n_gx, n_gy):
    row_id, col_id = lax.axis_index("gx"), lax.axis_index("gy")
    lane = iota((1, 2 * LANES), 1)
    lanes_in = (
        (lane < LANES)
        | ((lane < LANES + RIM) & (col_id < n_gy - 1))
        | ((lane >= 2 * LANES - RIM) & (col_id > 0))
    ).astype(F32)
    low = jnp.where(row_id > 0, lanes_in, 0.0)
    high = jnp.where(row_id < n_gx - 1, lanes_in, 0.0)
    return lambda x: low if x < FX else (lanes_in if x < 2 * FX else high)


def forward_body(n_gx, n_gy, steps, coeffs, start, rim, source, spot_hot, lane_hot, readings, target, final, sent, residuals, cur):
    height = start.shape[2]
    wide = 3 * FX
    cells = FX * height
    slots = readings.shape[1]
    own = slots // 3
    inside = inside_rows(n_gx, n_gy)
    fields = [start, cur.at[0], cur.at[1], cur.at[0], cur.at[1]]
    residuals[...] = jnp.zeros(residuals.shape, F32)
    live = (readings[8:9, :] > 0.5).astype(F32)
    for n in range(steps):
        before, after = fields[n], fields[n + 1]
        for x in range(n + 1, wide - n - 1):
            row = inside(x)
            for s in range(2):
                c = before[s, x]
                value = coeffs[s, 6, x] * c + source[s, x]
                value = value + coeffs[s, 0, x] * before[s, x + 1]
                value = value + coeffs[s, 1, x] * before[s, x - 1]
                value = value + coeffs[s, 2, x] * roll(c, -1, 1)
                value = value + coeffs[s, 3, x] * roll(c, 1, 1)
                value = value + coeffs[s, 4, x] * roll(c, -1, 0)
                value = value + coeffs[s, 5, x] * roll(c, 1, 0)
                after[s, x] = value * row
        for s in range(2):
            field = after[s, FX : 2 * FX].reshape(cells, 2 * LANES)
            at = s * steps + n
            for half, lanes in enumerate((slice(0, own), slice(own, slots))):
                seen = spread(lane_hot[:, lanes], field[:, half * LANES : (half + 1) * LANES])
                seen = seen * spot_hot[:, lanes].astype(F32)
                value = jnp.sum(seen, axis=0, keepdims=True) - readings[at : at + 1, lanes]
                residuals[at : at + 1, lanes] = value * live[:, lanes]
    residuals[8:16, :] = readings[8:16, :]
    last = fields[steps]
    for s in range(2):
        at = s * steps + steps - 1
        put_main = inject(spot_hot[:, :own], lane_hot[:, :own], residuals[at : at + 1, :own])
        put_rim = inject(spot_hot[:, own:], lane_hot[:, own:], residuals[at : at + 1, own:])
        for p in range(FX):
            rows = slice(p * height, (p + 1) * height)
            got = last[s, FX + p]
            final[s, p] = got[:, :LANES]
            g = s * FX + p
            sent[g * height : (g + 1) * height, :] = got[:, :LANES] - target[s, p] + put_main[rows]
            halo = got[:, LANES:] - rim_tile(rim[3], g) + put_rim[rows]
            at_lane = iota((height, LANES), 1) - 2 * RIM * g
            right = roll(halo, 2 * RIM * g, 1)
            left = roll(halo, 2 * RIM * g + 2 * RIM, 1)
            packed = jnp.where((at_lane >= 0) & (at_lane < RIM), right, 0.0 if g == 0 else packed)
            packed = jnp.where((at_lane >= RIM) & (at_lane < 2 * RIM), left, packed)
    base = 2 * FX * height
    sent[base : base + height, :] = packed
    base = base + height
    for part in range(slots // LANES):
        lanes = slice(part * LANES, (part + 1) * LANES)
        rows = [residuals[s * steps + n : s * steps + n + 1, lanes] for s in range(2) for n in range(steps - 1)]
        for i, values in enumerate(rows + [residuals[8:9, lanes]] * (8 - len(rows))):
            sent[base + 8 * part + i : base + 8 * part + i + 1, :] = values


def inject(spot, lane, values):
    total = None
    for part in pieces(lane.astype(F32) * values, 2):
        term = dot(spot, part, ((1,), (1,)))
        total = term if total is None else total + term
    return total


def own_puts_body(steps, spot_hot, lane_hot, residuals, puts):
    slots = residuals.shape[1]
    own = slots // 3
    _, _, planes, height, _ = puts.shape
    for n in range(steps - 1):
        for s in range(2):
            at = s * steps + n
            for half, lanes in enumerate((slice(0, own), slice(own, slots))):
                put = inject(spot_hot[:, lanes], lane_hot[:, lanes], residuals[at : at + 1, lanes])
                puts[n, s, :, :, half * LANES : (half + 1) * LANES] = put.reshape(planes, height, LANES)


def adjoint_body(n_gx, n_gy, steps, coeffs, sent, sent_e, sent_o, own_puts, foot_hot, foot_own, gradient, second, cur, puts, summed):
    is_odd = lax.rem(lax.axis_index("gx"), 2) == 1
    height = coeffs.shape[3]
    wide = 3 * FX
    cells = FX * height
    base = 2 * FX * height
    table = base + height
    slots = (sent.shape[0] - table) // 8 * LANES
    own = slots // 3
    inside = inside_rows(n_gx, n_gy)
    for q in (1, 0, 2):
        def take(lo, hi):
            if q == 1:
                return sent[lo:hi, :]
            if q == 0:
                return jnp.where(is_odd, sent_e[lo:hi, :], sent_o[lo:hi, :])
            return jnp.where(is_odd, sent_o[lo:hi, :], sent_e[lo:hi, :])
        packed_rim = take(base, base + height)
        for s in range(2):
            for p in range(FX):
                g = s * FX + p
                cur[0, s, q * FX + p, :, :LANES] = take(g * height, (g + 1) * height)
                cur[0, s, q * FX + p, :, LANES:] = rim_tile(packed_rim, g)
        if q == 1:
            continue
        rows = jnp.concatenate(
            [take(table + 8 * i, table + 8 * i + 8) for i in range(slots // LANES)], axis=1
        )
        cell = rows[7:8, :].astype(jnp.int32) - 1
        spot, lane = hot_pair(cell, cells)
        for n in range(steps - 1):
            reach = (n + 1) * height
            part = slice(cells - reach, cells) if q == 0 else slice(0, reach)
            first = (FX - n - 1) if q == 0 else 2 * FX
            for s in range(2):
                at = s * (steps - 1) + n
                for half, lanes in enumerate((slice(0, own), slice(own, slots))):
                    put = inject(spot[part, lanes], lane[:, lanes], rows[at : at + 1, lanes])
                    puts[n, s, first : first + n + 1, :, half * LANES : (half + 1) * LANES] = (
                        put.reshape(n + 1, height, LANES)
                    )
    for s in range(2):
        summed[s * cells : (s + 1) * cells, :] = sent[s * cells : (s + 1) * cells, :]
    for turn in range(steps - 1):
        now, later = turn % 2, (turn + 1) % 2
        n = steps - 2 - turn
        for x in range(turn + 1, wide - turn - 1):
            for s in range(2):
                put = own_puts[n, s, x - FX] if FX <= x < 2 * FX else puts[n, s, x]
                value = adjoint_value(coeffs, cur.at[now], s, x, 0) + put
                value = value * inside(x)
                if turn == steps - 2:
                    second[s, x - steps + 1] = value
                else:
                    cur[later, s, x] = value
                if FX <= x < 2 * FX:
                    at = s * cells + (x - FX) * height
                    summed[at : at + height, :] = summed[at : at + height, :] + value[:, :LANES]
    seen = spread(foot_hot[...], summed[...], ((1,), (1,)), count=2)
    records = foot_own.shape[1] // FY
    out_row = iota((n_gy, records), 0)
    out_from = iota((n_gy, records), 1) // SLOT_ROWS
    for s in range(2):
        total = jnp.sum(seen[s * cells : (s + 1) * cells] * foot_own[...], axis=0, keepdims=True)
        row = total[:, :records]
        for fy in range(1, FY):
            row = row + total[:, fy * records : (fy + 1) * records]
        gradient[:, s, :] = jnp.where(out_row == out_from, row, 0.0)


def adjoint_value(coeffs, field, s, x, shift):
    w = field[s, x - shift]
    value = coeffs[s, 6, x] * w
    value = value + coeffs[s, 1, x + 1] * field[s, x + 1 - shift]
    value = value + coeffs[s, 0, x - 1] * field[s, x - 1 - shift]
    value = value + roll(coeffs[s, 3, x] * w, -1, 1)
    value = value + roll(coeffs[s, 2, x] * w, 1, 1)
    value = value + roll(coeffs[s, 5, x] * w, -1, 0)
    return value + roll(coeffs[s, 4, x] * w, 1, 0)


def last_body(steps, coeffs, second, first):
    for x in range(FX, 2 * FX):
        for s in range(2):
            first[s, x - FX] = adjoint_value(coeffs, second, s, x, steps - 1)[:, :LANES]


def returned_body(got, owner, out):
    n_gy, _, records = got.shape
    base = lax.axis_index("gy") * SLOT_ROWS + CAPA
    choice = slot_choices(owner[...], n_gy, CAPA)
    lane = iota((n_gy, records), 1)
    for s in range(2):
        rows = got[:, s, :]
        total = jnp.zeros(choice[0].shape, F32)
        for k in range(CAPA):
            column = jnp.sum(jnp.where(lane == base + k, rows, 0.0), axis=1, keepdims=True)
            total = total + choice[k].astype(F32) * column
        out[s : s + 1, :] = jnp.sum(total, axis=0, keepdims=True)


def per_device(
    initial_state,
    eddy_diffusivity,
    velocity,
    target,
    sensor_cell,
    sensor_owner,
    observations,
    actuator_block,
    actuator_owner,
    controls,
    footprint,
):
    _, wide_x, height, wide_y = initial_state.shape
    steps = observations.shape[2]
    n_gx, n_gy = lax.axis_size("gx"), lax.axis_size("gy")
    devices = n_gx * n_gy
    sens, acts = sensor_cell.shape[0], actuator_block.shape[0]
    records = n_gy * SLOT_ROWS
    slots = 3 * CAPS * devices
    cells = FX * height
    wide = 3 * FX
    shape = jax.ShapeDtypeStruct
    vmem = pltpu.VMEM
    a_owner_row = actuator_owner.reshape(1, acts)
    main = jnp.concatenate([initial_state, eddy_diffusivity[None], velocity], axis=0)
    outgoing = call(
        functools.partial(records_out_body, n_gx, n_gy),
        shape((devices, SLOT_ROWS, LANES), F32),
        [vmem((LANES, sens), F32), vmem((LANES, acts), F32)],
        sensor_cell.reshape(1, sens),
        sensor_owner.reshape(1, sens),
        observations.transpose(1, 2, 0),
        actuator_block.reshape(1, acts),
        a_owner_row,
        controls.T,
        footprint,
    )
    strips = call(
        strips_body,
        shape((4, height, LANES), F32),
        [],
        initial_state,
        eddy_diffusivity,
        velocity,
        target,
    )
    got = lax.all_to_all(outgoing, ("gx", "gy"), split_axis=0, concat_axis=0, tiled=True)
    main_e, main_o = exchange(main, "gx")
    strips_e, strips_o = exchange(strips, "gy")
    rim = call(rim_body, shape((4, height, LANES), F32), [], strips_e, strips_o)
    rim_e, rim_o = exchange(rim[:3], "gx")
    coeffs, start = call(
        coeffs_body,
        (
            shape((2, 7, wide, height, 2 * LANES), F32),
            shape((2, wide, height, 2 * LANES), F32),
        ),
        [vmem((wide, height, 2 * LANES), F32)],
        main, main_e, main_o, rim, rim_e, rim_o,
    )
    source, foot_hot, foot_own, spot_hot, lane_hot, readings = call(
        functools.partial(records_in_body, n_gx, n_gy, height, wide_y),
        (
            shape((2, 3, cells, 2 * LANES), F32),
            shape((FY * records, LANES), BF16),
            shape((cells, FY * records), F32),
            shape((cells, slots), BF16),
            shape((LANES, slots), BF16),
            shape((16, slots), F32),
        ),
        [
            vmem((cells, FY * records), F32),
            vmem((FY * records, 2 * LANES), BF16),
            vmem((slots, LANES), F32),
        ],
        got,
        cost=COST,
    )
    source = source.reshape(2, wide, height, 2 * LANES)
    sent_rows = 2 * cells + height + slots // LANES * 8
    final, sent, residuals = call(
        functools.partial(forward_body, n_gx, n_gy, steps),
        (
            shape((2, FX, height, LANES), F32),
            shape((sent_rows, LANES), F32),
            shape((16, slots), F32),
        ),
        [vmem((2, 2, wide, height, 2 * LANES), F32)],
        coeffs, start, rim, source, spot_hot, lane_hot, readings, target,
    )
    sent_e, sent_o = exchange(sent, "gx")
    own_puts = call(
        functools.partial(own_puts_body, steps),
        shape((steps - 1, 2, FX, height, 2 * LANES), F32),
        [],
        spot_hot, lane_hot, residuals,
    )
    gradient, second = call(
        functools.partial(adjoint_body, n_gx, n_gy, steps),
        (
            shape((n_gy, 2, records), F32),
            shape((2, wide - 2 * steps + 2, height, 2 * LANES), F32),
        ),
        [
            vmem((2, 2, wide, height, 2 * LANES), F32),
            vmem((steps - 1, 2, wide, height, 2 * LANES), F32),
            vmem((2 * cells, LANES), F32),
        ],
        coeffs, sent, sent_e, sent_o, own_puts, foot_hot, foot_own,
    )
    back = lax.all_to_all(gradient, "gy", split_axis=0, concat_axis=0, tiled=True)
    first = call(
        functools.partial(last_body, steps),
        shape((2, FX, height, LANES), F32),
        [],
        coeffs, second,
    )
    returned = call(returned_body, shape((2, acts), F32), [], back, a_owner_row)
    return (final, first, returned.T)


def solution(mesh):
    in_specs = (
        P(None, "gx", None, "gy"),
        P("gx", None, "gy"),
        P(None, "gx", None, "gy"),
        P(None, "gx", None, "gy"),
        P(("gx", "gy")),
        P(("gx", "gy"), None),
        P(("gx", "gy"), None, None),
        P(("gx", "gy")),
        P(("gx", "gy"), None),
        P(("gx", "gy"), None),
        P(("gx", "gy"), None),
    )
    out_specs = (P(None, "gx", None, "gy"), P(None, "gx", None, "gy"), P(("gx", "gy"), None))
    return jax.shard_map(
        per_device, mesh=mesh, in_specs=in_specs, out_specs=out_specs, check_vma=False
    )
```

```python
import functools

import jax
import jax.numpy as jnp
from jax import lax
from jax.experimental import pallas as pl
from jax.experimental.pallas import tpu as pltpu
from jax.sharding import PartitionSpec as P

FX = 4
FZ = 8
FY = 4
CAPS = 4
CAPA = 4
FOOT = 128
RIM = 8
LANES = 128
SLOT_ROWS = 16
OBS_AT = 0
CELL_AT = 8
PITCH = 10
CTRL_AT = 16
BLOCK_AT = 18
PRANDTL = 0.85
SCALES = (1.0, 1.0 / PRANDTL)
F32 = jnp.float32
BF16 = jnp.bfloat16
VMEM_BYTES = 20 * 1024 * 1024


def iota(shape, dim):
    return lax.broadcasted_iota(jnp.int32, shape, dim)


def pieces(values, count=3):
    out = []
    for _ in range(count):
        part = values.astype(BF16)
        out.append(part)
        values = values - part.astype(F32)
    return out


def dot(a, b, dims=((1,), (0,))):
    return lax.dot_general(a, b, (dims, ((), ())), preferred_element_type=F32)


def pick(choice, values, dims=((1,), (0,)), count=3):
    total = None
    for part in pieces(values, count):
        term = dot(choice, part, dims)
        total = term if total is None else total + term
    return total


def spread(choice, values, dims=((1,), (0,)), count=3):
    total = None
    for part in pieces(values, count):
        term = dot(part, choice, dims)
        total = term if total is None else total + term
    return total


def roll(values, amount, axis):
    size = values.shape[axis]
    amount = amount % size
    if amount == 0:
        return values
    return pltpu.roll(values, amount, axis)


def swaps(count):
    even = [(i, i ^ 1) for i in range(count) if (i ^ 1) < count]
    odd = [(i, i + 1 if i % 2 else i - 1) for i in range(1, count) if (i % 2 == 0) or i + 1 < count]
    return even, odd


def exchange(values, axis):
    even, odd = swaps(lax.axis_size(axis))
    return lax.ppermute(values, axis, even), lax.ppermute(values, axis, odd)


def low_high(even, odd, is_odd):
    return jnp.where(is_odd, even, odd), jnp.where(is_odd, odd, even)


def call(body, out_shape, scratch, *args, us=0.2):
    return pl.pallas_call(
        body,
        cost_estimate=pl.CostEstimate(
            flops=0, transcendentals=0, bytes_accessed=int(us * 3.6e6)
        ),
        out_shape=out_shape,
        scratch_shapes=scratch,
        compiler_params=pltpu.CompilerParams(vmem_limit_bytes=VMEM_BYTES),
    )(*args)


def slot_choices(owner_row, owners, count):
    records = owner_row.shape[1]
    named = owner_row == iota((owners, records), 0)
    earlier = (iota((records, records), 0) < iota((records, records), 1)).astype(BF16)
    rank = dot(named.astype(BF16), earlier)
    return [(named & (rank == k)).astype(BF16) for k in range(count)]


class row_slots:
    def __init__(self, ref, base, rows):
        self.ref, self.base, self.rows = ref, base, rows
        self.shape = ((ref.shape[0] - base) // rows, rows, ref.shape[1])

    def __getitem__(self, at):
        return self.ref[self.base + at * self.rows : self.base + (at + 1) * self.rows, :]

    def __setitem__(self, at, value):
        self.ref[self.base + at * self.rows : self.base + (at + 1) * self.rows, :] = value


class split_planes:
    def __init__(self, inner, outer):
        self.inner, self.outer = inner, outer

    def place(self, x):
        if FX - 1 <= x <= 2 * FX:
            return self.inner, x - FX + 1
        return self.outer, x if x < FX else x - FX - 2

    def __getitem__(self, at):
        ref, x = self.place(at[2])
        return ref[at[0], at[1], x]

    def __setitem__(self, at, value):
        ref, x = self.place(at[2])
        ref[at[0], at[1], x] = value


def without_bit(slot, bit):
    return (slot >> (bit + 1) << bit) | (slot & ((1 << bit) - 1))


def bit_of(axis, bit):
    return lax.rem(lax.axis_index(axis) >> bit, 2)


def split_slots(slots, axis, bit, send, keep):
    mine = bit_of(axis, bit) == 1
    for d, low in enumerate(slots):
        if d >> bit & 1:
            continue
        high = slots[d | 1 << bit]
        at = without_bit(d, bit)
        send[at] = jnp.where(mine, low, high)
        keep[at] = jnp.where(mine, high, low)


def join_slots(keep, got, axis, bit):
    mine = bit_of(axis, bit)
    return [
        jnp.where(mine == (d >> bit & 1), keep[without_bit(d, bit)], got[without_bit(d, bit)])
        for d in range(2 * keep.shape[0])
    ]


def route_body(axis, bit, keep, got, next_send, next_keep):
    got = row_slots(got, got.shape[0] - keep.shape[0] * keep.shape[1], keep.shape[1])
    next_send = row_slots(next_send, 0, keep.shape[1])
    split_slots(join_slots(keep, got, axis, bit), axis, bit + 1, next_send, next_keep)


def swap(values, axis, bit):
    count = lax.axis_size(axis)
    return lax.ppermute(values, axis, [(i, i ^ 1 << bit) for i in range(count)])


def route(keep, got, axis, after=None):
    bits = lax.axis_size(axis).bit_length() - 1
    for bit in range(bits - 1):
        send = jax.ShapeDtypeStruct((keep.shape[0] * keep.shape[1], LANES), F32)
        half = jax.ShapeDtypeStruct(keep.shape, F32)
        send, keep = call(functools.partial(route_body, axis, bit), (send, half), [], keep, got)
        if after is not None:
            send, after = lax.optimization_barrier((send, after))
        got = swap(send, axis, bit + 1)
    return keep, got


def records_out_body(n_gx, n_gy, cell, s_owner, obs, block, a_owner, ctrl, foot, send, keep, s_meta, a_meta, out):
    owners = n_gx * n_gy
    steps = obs.shape[1]
    s_meta[...] = jnp.zeros(s_meta.shape, F32)
    for s in range(2):
        s_meta[OBS_AT + s * steps : OBS_AT + (s + 1) * steps, :] = obs[s]
    s_meta[CELL_AT : CELL_AT + 1, :] = (cell[...] + 1).astype(F32)
    a_meta[...] = jnp.zeros(a_meta.shape, F32)
    a_meta[CTRL_AT : CTRL_AT + 2, :] = ctrl[...]
    a_meta[BLOCK_AT : BLOCK_AT + 1, :] = (block[...] + 1).astype(F32)
    s_all, a_all, f_all = s_meta[...], a_meta[...], foot[...]
    s_choice = slot_choices(s_owner[...], owners, CAPS)
    a_choice = slot_choices(a_owner[...], n_gy, CAPA)
    act_rows = jnp.zeros((n_gy, LANES), F32)
    sens_rows, foot_rows = [], []
    for k in range(CAPS):
        sens_rows.append(pick(s_choice[k], s_all, ((1,), (1,))))
        act_rows = act_rows + roll(pick(a_choice[k], a_all, ((1,), (1,))), 32 * k, 1)
        foot_rows.append(pick(a_choice[k], f_all))

    def moved(values, t):
        at = iota(values.shape, 0) % n_gy
        if t == 0:
            return jnp.where(at == 0, 0.0, roll(values, 1, 0))
        if t == 2:
            return jnp.where(at == n_gy - 1, 0.0, roll(values, values.shape[0] - 1, 0))
        return values

    packed = jnp.zeros((owners, LANES), F32)
    for t in range(3):
        for k in range(CAPS):
            out[:, 4 * t + k, :] = moved(foot_rows[k], t)
            packed = packed + roll(moved(sens_rows[k], t), PITCH * (CAPS * t + k), 1)
        out[:, 12 + t, :] = moved(act_rows, t)
    out[:, 15:, :] = jnp.zeros((n_gy, out.shape[1] - 15, LANES), F32)
    for d in range(n_gy):
        for i in range(n_gx):
            out[d, SLOT_ROWS + i : SLOT_ROWS + i + 1, :] = packed[i * n_gy + d : i * n_gy + d + 1]
    split_slots([out[d] for d in range(n_gy)], "gy", 0, row_slots(send, 0, out.shape[1]), keep)


def strips_body(state, kappa, vel, target, out):
    lane = iota((state.shape[2], LANES), 1)
    fields = [state.at[0], state.at[1], kappa, vel.at[0], vel.at[1], vel.at[2], target.at[0], target.at[1]]
    for tile in range(4):
        packed = jnp.zeros(lane.shape, F32)
        for g in range(2 * FX):
            plane = fields[2 * tile + g // FX][g % FX]
            packed = jnp.where(lane // (2 * RIM) == g, roll(plane, RIM + 2 * RIM * g, 1), packed)
        out[tile * lane.shape[0] : (tile + 1) * lane.shape[0], :] = packed


def rim_body(n_gx, even, odd, keep, got, sent, rim_target, sens_keep):
    is_odd = lax.rem(lax.axis_index("gy"), 2) == 1
    height = rim_target.shape[0]
    tiles = odd.shape[0] // height
    for tile in range(tiles):
        rows = slice(tile * height, (tile + 1) * height)
        left, right = low_high(even[rows, :], odd[rows, :], is_odd)
        lane = iota(left.shape, 1)
        value = jnp.where(lane % (2 * RIM) < RIM, roll(right, -RIM, 1), roll(left, RIM, 1))
        if tile == tiles - 1:
            rim_target[...] = value
        else:
            sent[rows, :] = value
    base = (tiles - 1) * height
    n_gy = 2 * keep.shape[0]
    rows = keep.shape[1]
    got = row_slots(got, got.shape[0] - keep.shape[0] * rows, rows)
    slots = join_slots(keep, got, "gy", n_gy.bit_length() - 2)
    for d in range(n_gy):
        sent[base + d * SLOT_ROWS : base + (d + 1) * SLOT_ROWS, :] = slots[d][:SLOT_ROWS]
    base = base + n_gy * SLOT_ROWS
    rows = [
        jnp.concatenate([slots[d][SLOT_ROWS + i : SLOT_ROWS + i + 1] for d in range(n_gy)], axis=0)
        for i in range(n_gx)
    ]
    split_slots(rows, "gx", 0, row_slots(sent, base, n_gy), sens_keep)


def rim_tile(packed, group):
    lane = iota(packed.shape, 1)
    right = roll(packed, -2 * RIM * group, 1)
    left = roll(packed, LANES - 2 * RIM - 2 * RIM * group, 1)
    return jnp.where(lane < RIM, right, jnp.where(lane >= LANES - RIM, left, 0.0))


def extended(field, main, main_e, main_o, rim, rim_e, rim_o, is_odd, x):
    height = main.shape[2]
    at, group = pl.ds(field // 2 * height, height), (field % 2) * FX + x % FX
    if x // FX == 1:
        centre, halo = main[field, x % FX], rim[at]
    elif x // FX == 0:
        centre = jnp.where(is_odd, main_e[field, x], main_o[field, x])
        halo = jnp.where(is_odd, rim_e[at], rim_o[at])
    else:
        centre = jnp.where(is_odd, main_o[field, x - 2 * FX], main_e[field, x - 2 * FX])
        halo = jnp.where(is_odd, rim_o[at], rim_e[at])
    return centre, rim_tile(halo, group)


def source_tile(n_gy, height, wide_y, records_in, planes, out, stacked, placing):
    records = n_gy * SLOT_ROWS
    blocks_y = wide_y // FY
    r_of, r_to = iota((records, records), 0), iota((records, records), 1)
    slot = r_of % SLOT_ROWS
    meta = jnp.zeros((records, LANES), F32)
    for k in range(CAPA):
        move = (slot < 12) & (slot % 4 == k) & (r_to == r_of - slot + 12 + slot // 4)
        meta = meta + pick(move.astype(BF16), roll(records_in, -32 * k, 1))
    q_of, l_of = iota((FOOT, FOOT), 0), iota((FOOT, FOOT), 1)
    unpack = (l_of == (q_of % 32) * FY + q_of // 32).astype(BF16)
    side = (iota((records, 1), 0) % SLOT_ROWS) // 4
    meta_t = meta.T
    block_row = meta_t[BLOCK_AT : BLOCK_AT + 1, :].astype(jnp.int32) - 1
    bz_row = block_row // blocks_y
    foot_t = pick(unpack, records_in, ((1,), (1,)), 2)
    block_col = meta[:, BLOCK_AT : BLOCK_AT + 1].astype(jnp.int32) - 1
    by = block_col % blocks_y
    usable = (block_col >= 0) & (
        (side == 1)
        | ((side == 0) & (by * FY >= wide_y - RIM))
        | ((side == 2) & (by * FY < RIM))
    )
    start = jnp.where(side == 1, by * FY, wide_y + by * FY)
    start = jnp.where(usable, start, -FY)
    wide_lane = iota((records, 2 * wide_y), 1)
    for fy in range(FY):
        placing[fy * records : (fy + 1) * records, :] = (wide_lane == start + fy).astype(BF16)
    rows_out = len(planes) * height
    for s in range(2):
        force = meta_t[CTRL_AT + s : CTRL_AT + s + 1, :]
        for fy in range(FY):
            lanes = slice(fy * records, (fy + 1) * records)
            for i, x in enumerate(planes):
                scaled = foot_t[fy * 32 + x * FZ : fy * 32 + (x + 1) * FZ, :] * force
                for bz in range(height // FZ):
                    at = i * height + bz * FZ
                    stacked[at : at + FZ, lanes] = jnp.where(bz_row == bz, scaled, 0.0)
        value = spread(placing[...], stacked[:rows_out, :], count=2)
        for i in range(len(planes)):
            out[s, i] = value[i * height : (i + 1) * height]
    return meta, meta_t


def own_source_body(n_gy, height, wide_y, got, source, foot_hot, foot_own, stacked, placing):
    records = n_gy * SLOT_ROWS
    blocks_y = wide_y // FY
    base = 3 * height
    records_in = got[base : base + records, :]
    meta, meta_t = source_tile(
        n_gy, height, wide_y, records_in, range(FX), source, stacked, placing
    )
    held = n_gy * CAPA
    r_of, r_to = iota((held, records), 0), iota((held, records), 1)
    own = (r_to == r_of // CAPA * SLOT_ROWS + CAPA + r_of % CAPA).astype(BF16)
    block_row = spread(own, meta_t[CTRL_AT : CTRL_AT + 8], ((1,), (1,)))[BLOCK_AT - CTRL_AT :]
    bz_row = (block_row[:1].astype(jnp.int32) - 1) // blocks_y
    block_col = pick(own, meta)[:, BLOCK_AT : BLOCK_AT + 1].astype(jnp.int32) - 1
    start = jnp.where(block_col >= 0, block_col % blocks_y * FY, -FY)
    q_of, l_of = iota((FOOT, FOOT), 0), iota((FOOT, FOOT), 1)
    unpack = (l_of == (q_of % 32) * FY + q_of // 32).astype(BF16)
    foot_t = pick(unpack, pick(own, records_in), ((1,), (1,)))
    lane = iota((held, wide_y), 1)
    for fy in range(FY):
        lanes = slice(fy * held, (fy + 1) * held)
        foot_hot[lanes, :] = (lane == start + fy).astype(BF16)
        for x in range(FX):
            piece = foot_t[fy * 32 + x * FZ : fy * 32 + (x + 1) * FZ, :]
            for bz in range(height // FZ):
                at = x * height + bz * FZ
                foot_own[at : at + FZ, lanes] = jnp.where(bz_row == bz, piece, 0.0)


def side_source_body(n_gy, height, wide_y, got_e, got_o, source, stacked, placing):
    is_odd = lax.rem(lax.axis_index("gx"), 2) == 1
    rows = slice(3 * height, 3 * height + n_gy * SLOT_ROWS)
    low, high = low_high(got_e[rows, :], got_o[rows, :], is_odd)
    for q, (records_in, planes) in enumerate(((low, range(1, FX)), (high, range(FX - 1)))):
        source_tile(n_gy, height, wide_y, records_in, planes, source.at[q], stacked, placing)


def sensors_body(height, keep, got, spot_hot, lane_hot, z_hot, rim_hot, readings, table):
    n_gx = 2 * keep.shape[0]
    got = row_slots(got, got.shape[0] - keep.shape[0] * keep.shape[1], keep.shape[1])
    rows = jnp.concatenate(join_slots(keep, got, "gx", n_gx.bit_length() - 2), axis=0)
    devices = rows.shape[0]
    slots = 3 * CAPS * devices
    own = slots // 3
    for n, t in enumerate((1, 0, 2)):
        for k in range(CAPS):
            at = (n * CAPS + k) * devices
            table[at : at + devices, :] = roll(rows, -PITCH * (CAPS * t + k), 1)
    cells = []
    for part in range(slots // LANES):
        lanes = slice(part * LANES, (part + 1) * LANES)
        turned = table[lanes, :].T
        cell = turned[CELL_AT : CELL_AT + 1, :].astype(jnp.int32) - 1
        at_y = cell % LANES
        slot_id = iota((1, LANES), 1) + part * LANES
        live = (cell >= 0) & (
            (slot_id < own)
            | ((slot_id < 2 * own) & (at_y >= LANES - RIM))
            | ((slot_id >= 2 * own) & (at_y < RIM))
        )
        cell = jnp.where(live, cell, -1)
        readings[0:8, lanes] = turned[OBS_AT : OBS_AT + 8]
        readings[8:16, lanes] = jnp.broadcast_to((cell + 1).astype(F32), (8, LANES))
        cells.append(cell)
    cell = jnp.concatenate(cells, axis=1)
    spot, lane = own_hot(cell[:, :own], height)
    spot_hot[...] = spot
    lane_hot[...] = lane
    z, rim = rim_hot_pair(cell[:, own:], height)
    z_hot[...] = z
    rim_hot[...] = rim


def own_hot(cell, height):
    spot = jnp.where(cell >= 0, cell // LANES, -1)
    at_y = jnp.where(cell >= 0, cell % LANES, -1)
    slots = cell.shape[1]
    return (
        (iota((FX * height, slots), 0) == spot).astype(BF16),
        (iota((LANES, slots), 0) == at_y).astype(BF16),
    )


def rim_hot_pair(cell, height):
    spot, at_y = cell // LANES, cell % LANES
    z = jnp.where(cell >= 0, spot % height, -1)
    lane = jnp.where(at_y < RIM, at_y, at_y - LANES + 2 * RIM)
    lane = jnp.where(cell >= 0, spot // height * 2 * RIM + lane, -1)
    slots = cell.shape[1]
    return (
        (iota((height, slots), 0) == z).astype(BF16),
        (iota((2 * RIM * FX, slots), 0) == lane).astype(BF16),
    )


def paired(hot):
    blank = jnp.zeros_like(hot)
    return jnp.concatenate(
        [jnp.concatenate([hot, blank], axis=1), jnp.concatenate([blank, hot], axis=1)], axis=0
    )


def inject(row_hot, lane_hot, values):
    placed = jnp.concatenate([lane_hot.astype(F32) * value for value in values], axis=0)
    total = None
    for part in pieces(placed, 2):
        term = dot(row_hot, part, ((1,), (1,)))
        total = term if total is None else total + term
    return total


def pack_rims(halos):
    packed = jnp.zeros(halos[0].shape, F32)
    lane = iota(packed.shape, 1)
    for g, halo in enumerate(halos):
        at = lane - 2 * RIM * g
        packed = jnp.where((at >= 0) & (at < RIM), roll(halo, 2 * RIM * g, 1), packed)
        packed = jnp.where(
            (at >= RIM) & (at < 2 * RIM), roll(halo, 2 * RIM * g + 2 * RIM, 1), packed
        )
    return packed


def coeffs_body(main, main_e, main_o, rim, rim_e, rim_o, coeffs, start, half_k):
    refs = (main, main_e, main_o, rim, rim_e, rim_o)
    is_odd = lax.rem(lax.axis_index("gx"), 2) == 1
    wide = 3 * FX
    height = half_k.shape[1]
    shape = (height, 2 * LANES)
    z = iota(shape, 0)
    for x in range(wide):
        centre, halo = extended(2, *refs, is_odd, x)
        half_k[x, :, :LANES] = 0.5 * centre
        half_k[x, :, LANES:] = 0.5 * halo
        for s in range(2):
            centre, halo = extended(s, *refs, is_odd, x)
            start[s, x, :, :LANES] = centre
            start[s, x, :, LANES:] = halo
    for x in range(wide):
        k = half_k[x]
        faces = (
            k + half_k[min(x + 1, wide - 1)],
            k + half_k[max(x - 1, 0)],
            k + roll(k, -1, 1),
            k + roll(k, 1, 1),
            k + jnp.where(z == height - 1, 0.0, roll(k, -1, 0)),
            k + jnp.where(z == 0, 0.0, roll(k, 1, 0)),
        )
        total = (faces[0] + faces[1]) + (faces[2] + faces[3]) + (faces[4] + faces[5])
        drift = []
        for axis in range(3):
            centre, halo = extended(3 + axis, *refs, is_odd, x)
            drift.append(0.5 * jnp.concatenate([centre, halo], axis=1))
        for s in range(2):
            coeffs[s, 6, x] = 1.0 - SCALES[s] * total
            for face in range(6):
                value = faces[face] if s == 0 else SCALES[s] * faces[face]
                value = value - drift[face // 2] if face % 2 == 0 else value + drift[face // 2]
                if face == 4:
                    value = jnp.where(z == height - 1, 0.0, value)
                if face == 5:
                    value = jnp.where(z == 0, 0.0, value)
                coeffs[s, face, x] = value


def inside_rows(n_gx, n_gy):
    row_id, col_id = lax.axis_index("gx"), lax.axis_index("gy")
    lane = iota((1, 2 * LANES), 1)
    lanes_in = (
        (lane < LANES)
        | ((lane < LANES + RIM) & (col_id < n_gy - 1))
        | ((lane >= 2 * LANES - RIM) & (col_id > 0))
    ).astype(F32)
    low = jnp.where(row_id > 0, lanes_in, 0.0)
    high = jnp.where(row_id < n_gx - 1, lanes_in, 0.0)
    return lambda x: low if x < FX else (lanes_in if x < 2 * FX else high)


def forward_body(n_gx, n_gy, steps, coeffs, start, rim_target, own_source, side_source, spot_hot, lane_hot, z_hot, rim_hot, readings, target, final, sent, residuals, cur):
    height = start.shape[2]
    wide = 3 * FX
    cells = FX * height
    slots = readings.shape[1]
    own = slots // 3
    rest = slots - own
    inside = inside_rows(n_gx, n_gy)
    fields = [start, cur.at[0], cur.at[1], cur.at[0], cur.at[1]]
    residuals[...] = jnp.zeros(residuals.shape, F32)
    live = (readings[8:9, :] > 0.5).astype(F32)
    lane_pair, rim_pair = paired(lane_hot[...]), paired(rim_hot[...])
    spots = spot_hot[...].astype(F32)
    heights = z_hot[...].astype(F32)

    def source(s, x):
        if x < FX:
            return side_source[0, s, x - 1]
        return own_source[s, x - FX] if x < 2 * FX else side_source[1, s, x - 2 * FX]

    for n in range(steps):
        before, after = fields[n], fields[n + 1]
        for x in range(n + 1, wide - n - 1):
            row = inside(x)
            for s in range(2):
                c = before[s, x]
                value = coeffs[s, 6, x] * c + source(s, x)
                value = value + coeffs[s, 0, x] * before[s, x + 1]
                value = value + coeffs[s, 1, x] * before[s, x - 1]
                value = value + coeffs[s, 2, x] * roll(c, -1, 1)
                value = value + coeffs[s, 3, x] * roll(c, 1, 1)
                value = value + coeffs[s, 4, x] * roll(c, -1, 0)
                value = value + coeffs[s, 5, x] * roll(c, 1, 0)
                after[s, x] = value * row
        both = jnp.concatenate(
            [after[s, FX : 2 * FX, :, :LANES].reshape(cells, LANES) for s in range(2)], axis=1
        )
        seen = spread(lane_pair, both)
        packed = pack_rims([after[s, FX + p, :, LANES:] for s in range(2) for p in range(FX)])
        seen_rim = spread(rim_pair, packed)
        for s in range(2):
            at = s * steps + n
            value = jnp.sum(seen[:, s * own : (s + 1) * own] * spots, axis=0, keepdims=True)
            value = (value - readings[at : at + 1, :own]) * live[:, :own]
            residuals[at : at + 1, :own] = value
            value = jnp.sum(seen_rim[:, s * rest : (s + 1) * rest] * heights, axis=0, keepdims=True)
            value = (value - readings[at : at + 1, own:]) * live[:, own:]
            residuals[at : at + 1, own:] = value
    residuals[8:16, :] = readings[8:16, :]
    last = fields[steps]
    ends = [residuals[s * steps + steps - 1 : (s + 1) * steps, :] for s in range(2)]
    put = inject(spot_hot[...], lane_hot[...], [end[:, :own] for end in ends])
    put_rim = inject(z_hot[...], rim_hot[...], [end[:, own:] for end in ends])
    for s in range(2):
        for p in range(FX):
            rows = slice(p * height, (p + 1) * height)
            got = last[s, FX + p, :, :LANES]
            final[s, p] = got
            g = s * FX + p
            sent[g * height : (g + 1) * height, :] = (
                got - target[s, p] + put[rows, s * LANES : (s + 1) * LANES]
            )
    base = 2 * FX * height
    sent[base : base + height, :] = packed - rim_target[...] + put_rim
    base = base + height
    for part in range(slots // LANES):
        lanes = slice(part * LANES, (part + 1) * LANES)
        rows = [residuals[s * steps + n : s * steps + n + 1, lanes] for s in range(2) for n in range(steps - 1)]
        for i, values in enumerate(rows + [residuals[8:9, lanes]] * (8 - len(rows))):
            sent[base + 8 * part + i : base + 8 * part + i + 1, :] = values


def own_puts_body(steps, spot_hot, lane_hot, z_hot, rim_hot, residuals, puts):
    slots = residuals.shape[1]
    own = slots // 3
    _, _, planes, height, _ = puts.shape
    for n in range(steps - 1):
        values = [residuals[s * steps + n : s * steps + n + 1, :] for s in range(2)]
        put = inject(spot_hot[...], lane_hot[...], [value[:, :own] for value in values])
        put_rim = inject(z_hot[...], rim_hot[...], [value[:, own:] for value in values])
        for s in range(2):
            for p in range(planes):
                rows = slice(p * height, (p + 1) * height)
                puts[n, s, p, :, :LANES] = put[rows, s * LANES : (s + 1) * LANES]
                puts[n, s, p, :, LANES:] = rim_tile(put_rim, s * FX + p)


def adjoint_body(n_gx, n_gy, steps, coeffs, sent, sent_e, sent_o, own_puts, foot_hot, foot_own, gradient, second, cur, puts, summed):
    is_odd = lax.rem(lax.axis_index("gx"), 2) == 1
    height = coeffs.shape[3]
    wide = 3 * FX
    cells = FX * height
    base = 2 * FX * height
    table = base + height
    slots = (sent.shape[0] - table) // 8 * LANES
    own = slots // 3
    inside = inside_rows(n_gx, n_gy)
    for q in (1, 0, 2):
        def take(lo, hi):
            if q == 1:
                return sent[lo:hi, :]
            if q == 0:
                return jnp.where(is_odd, sent_e[lo:hi, :], sent_o[lo:hi, :])
            return jnp.where(is_odd, sent_o[lo:hi, :], sent_e[lo:hi, :])
        packed_rim = take(base, base + height)
        for s in range(2):
            for p in range(FX):
                g = s * FX + p
                cur[0, s, q * FX + p, :, :LANES] = take(g * height, (g + 1) * height)
                cur[0, s, q * FX + p, :, LANES:] = rim_tile(packed_rim, g)
        if q == 1:
            continue
        rows = jnp.concatenate(
            [take(table + 8 * i, table + 8 * i + 8) for i in range(slots // LANES)], axis=1
        )
        cell = rows[7:8, :].astype(jnp.int32) - 1
        spot, lane = own_hot(cell[:, :own], height)
        z, rim = rim_hot_pair(cell[:, own:], height)
        for n in range(steps - 1):
            reach = (n + 1) * height
            part = slice(cells - reach, cells) if q == 0 else slice(0, reach)
            first = FX - n - 1 if q == 0 else 0
            values = [rows[s * (steps - 1) + n : s * (steps - 1) + n + 1, :] for s in range(2)]
            put = inject(spot[part], lane, [value[:, :own] for value in values])
            put_rim = inject(z, rim, [value[:, own:] for value in values])
            for s in range(2):
                for i in range(n + 1):
                    x = q * FX + first + i
                    puts[n, s, x, :, :LANES] = put[
                        i * height : (i + 1) * height, s * LANES : (s + 1) * LANES
                    ]
                    puts[n, s, x, :, LANES:] = rim_tile(put_rim, s * FX + first + i)
    for s in range(2):
        summed[s * cells : (s + 1) * cells, :] = sent[s * cells : (s + 1) * cells, :]
    for turn in range(steps - 1):
        now, later = turn % 2, (turn + 1) % 2
        n = steps - 2 - turn
        for x in range(turn + 1, wide - turn - 1):
            for s in range(2):
                put = own_puts[n, s, x - FX] if FX <= x < 2 * FX else puts[n, s, x]
                value = adjoint_value(coeffs, cur.at[now], s, x, 0) + put
                value = value * inside(x)
                if turn == steps - 2:
                    second[s, x - steps + 1] = value
                else:
                    cur[later, s, x] = value
                if FX <= x < 2 * FX:
                    at = s * cells + (x - FX) * height
                    summed[at : at + height, :] = summed[at : at + height, :] + value[:, :LANES]
    seen = spread(foot_hot[...], summed[...], ((1,), (1,)), count=2)
    width = foot_own.shape[1]
    held = width // FY
    out_row = iota((n_gy, width), 0)
    out_from = iota((n_gy, width), 1) // CAPA
    for s in range(2):
        row = jnp.sum(seen[s * cells : (s + 1) * cells] * foot_own[...], axis=0, keepdims=True)
        total = row
        for fy in range(1, FY):
            total = total + roll(row, -fy * held, 1)
        gradient[:, s, :] = jnp.where(out_row == out_from, total, 0.0)


def adjoint_value(coeffs, field, s, x, shift):
    w = field[s, x - shift]
    value = coeffs[s, 6, x] * w
    value = value + coeffs[s, 1, x + 1] * field[s, x + 1 - shift]
    value = value + coeffs[s, 0, x - 1] * field[s, x - 1 - shift]
    value = value + roll(coeffs[s, 3, x] * w, -1, 1)
    value = value + roll(coeffs[s, 2, x] * w, 1, 1)
    value = value + roll(coeffs[s, 5, x] * w, -1, 0)
    return value + roll(coeffs[s, 4, x] * w, 1, 0)


def last_body(steps, coeffs, second, first):
    for x in range(FX, 2 * FX):
        for s in range(2):
            first[s, x - FX] = adjoint_value(coeffs, second, s, x, steps - 1)[:, :LANES]


def returned_body(got, owner, out):
    n_gy, _, records = got.shape
    base = lax.axis_index("gy") * CAPA
    choice = slot_choices(owner[...], n_gy, CAPA)
    lane = iota((n_gy, records), 1)
    for s in range(2):
        rows = got[:, s, :]
        total = jnp.zeros(choice[0].shape, F32)
        for k in range(CAPA):
            column = jnp.sum(jnp.where(lane == base + k, rows, 0.0), axis=1, keepdims=True)
            total = total + choice[k].astype(F32) * column
        out[s : s + 1, :] = jnp.sum(total, axis=0, keepdims=True)


def per_device(
    initial_state,
    eddy_diffusivity,
    velocity,
    target,
    sensor_cell,
    sensor_owner,
    observations,
    actuator_block,
    actuator_owner,
    controls,
    footprint,
):
    _, wide_x, height, wide_y = initial_state.shape
    steps = observations.shape[2]
    n_gx, n_gy = lax.axis_size("gx"), lax.axis_size("gy")
    devices = n_gx * n_gy
    sens, acts = sensor_cell.shape[0], actuator_block.shape[0]
    records = n_gy * SLOT_ROWS
    slots = 3 * CAPS * devices
    cells = FX * height
    wide = 3 * FX
    shape = jax.ShapeDtypeStruct
    vmem = pltpu.VMEM
    a_owner_row = actuator_owner.reshape(1, acts)
    main = jnp.concatenate([initial_state, eddy_diffusivity[None], velocity], axis=0)
    slot_rows = SLOT_ROWS + -(-n_gx // 8) * 8
    half = shape((n_gy // 2, slot_rows, LANES), F32)
    sens_half = shape((n_gx // 2, n_gy, LANES), F32)
    strip_rows = 4 * height
    acts_send, acts_keep = call(
        functools.partial(records_out_body, n_gx, n_gy),
        (
            shape((n_gy // 2 * slot_rows, LANES), F32),
            half,
        ),
        [
            vmem((LANES, sens), F32),
            vmem((LANES, acts), F32),
            vmem((n_gy, slot_rows, LANES), F32),
        ],
        sensor_cell.reshape(1, sens),
        sensor_owner.reshape(1, sens),
        observations.transpose(1, 2, 0),
        actuator_block.reshape(1, acts),
        a_owner_row,
        controls.T,
        footprint,
    )
    strips = call(
        strips_body,
        shape((strip_rows, LANES), F32),
        [],
        initial_state,
        eddy_diffusivity,
        velocity,
        target,
    )
    main_e, main_o = exchange(main, "gx")
    strips_e, strips_o = exchange(strips, "gy")
    acts_keep, acts_got = route(acts_keep, swap(acts_send, "gy", 0), "gy")
    rim, rim_target, sens_keep = call(
        functools.partial(rim_body, n_gx),
        (
            shape((3 * height + records + n_gx // 2 * n_gy, LANES), F32),
            shape((height, LANES), F32),
            sens_half,
        ),
        [],
        strips_e, strips_o, acts_keep, acts_got,
    )
    rim_e, rim_o = exchange(rim, "gx")
    held = n_gy * CAPA
    scratch = [vmem((cells, FY * records), F32), vmem((FY * records, 2 * LANES), BF16)]
    own_source, foot_hot, foot_own = call(
        functools.partial(own_source_body, n_gy, height, wide_y),
        (
            shape((2, FX, height, 2 * LANES), F32),
            shape((FY * held, LANES), BF16),
            shape((cells, FY * held), F32),
        ),
        scratch,
        rim,
        us=1.5,
    )
    side_source = call(
        functools.partial(side_source_body, n_gy, height, wide_y),
        shape((2, 2, FX - 1, height, 2 * LANES), F32),
        scratch,
        rim_e, rim_o,
        us=1.5,
    )
    sens_keep, sens_got = route(sens_keep, rim_e, "gx", after=foot_hot)
    coeffs, start = call(
        coeffs_body,
        (
            shape((2, 7, wide, height, 2 * LANES), F32),
            shape((2, wide, height, 2 * LANES), F32),
        ),
        [vmem((wide, height, 2 * LANES), F32)],
        main, main_e, main_o, rim, rim_e, rim_o,
        us=1.6,
    )
    sens_keep, start = lax.optimization_barrier((sens_keep, start))
    own_slots = slots // 3
    rest = slots - own_slots
    *hots, readings = call(
        functools.partial(sensors_body, height),
        (
            shape((cells, own_slots), BF16),
            shape((LANES, own_slots), BF16),
            shape((height, rest), BF16),
            shape((2 * RIM * FX, rest), BF16),
            shape((16, slots), F32),
        ),
        [vmem((slots, LANES), F32)],
        sens_keep, sens_got,
    )
    sent_rows = 2 * cells + height + slots // LANES * 8
    final, sent, residuals = call(
        functools.partial(forward_body, n_gx, n_gy, steps),
        (
            shape((2, FX, height, LANES), F32),
            shape((sent_rows, LANES), F32),
            shape((16, slots), F32),
        ),
        [vmem((2, 2, wide, height, 2 * LANES), F32)],
        coeffs, start, rim_target, own_source, side_source, *hots, readings, target,
        us=5.0,
    )
    sent_e, sent_o = exchange(sent, "gx")
    own_puts = call(
        functools.partial(own_puts_body, steps),
        shape((steps - 1, 2, FX, height, 2 * LANES), F32),
        [],
        *hots, residuals,
        us=0.7,
    )
    gradient, second = call(
        functools.partial(adjoint_body, n_gx, n_gy, steps),
        (
            shape((n_gy, 2, FY * held), F32),
            shape((2, wide - 2 * steps + 2, height, 2 * LANES), F32),
        ),
        [
            vmem((2, 2, wide, height, 2 * LANES), F32),
            vmem((steps - 1, 2, wide, height, 2 * LANES), F32),
            vmem((2 * cells, LANES), F32),
        ],
        coeffs, sent, sent_e, sent_o, own_puts, foot_hot, foot_own,
        us=4.0,
    )
    back = lax.all_to_all(gradient, "gy", split_axis=0, concat_axis=0, tiled=True)
    first = call(
        functools.partial(last_body, steps),
        shape((2, FX, height, LANES), F32),
        [],
        coeffs, second,
        us=1.0,
    )
    returned = call(returned_body, shape((2, acts), F32), [], back, a_owner_row)
    return (final, first, returned.T)


def solution(mesh):
    in_specs = (
        P(None, "gx", None, "gy"),
        P("gx", None, "gy"),
        P(None, "gx", None, "gy"),
        P(None, "gx", None, "gy"),
        P(("gx", "gy")),
        P(("gx", "gy"), None),
        P(("gx", "gy"), None, None),
        P(("gx", "gy")),
        P(("gx", "gy"), None),
        P(("gx", "gy"), None),
        P(("gx", "gy"), None),
    )
    out_specs = (P(None, "gx", None, "gy"), P(None, "gx", None, "gy"), P(("gx", "gy"), None))
    return jax.shard_map(
        per_device, mesh=mesh, in_specs=in_specs, out_specs=out_specs, check_vma=False
    )
```

```python
import functools

import jax
import jax.numpy as jnp
from jax import lax
from jax.experimental import pallas as pl
from jax.experimental.pallas import tpu as pltpu
from jax.sharding import PartitionSpec as P

FX = 4
FZ = 8
FY = 4
CAPS = 4
CAPA = 4
FOOT = 128
RIM = 8
LANES = 128
SLOT_ROWS = 16
OBS_AT = 0
CELL_AT = 8
PITCH = 10
CTRL_AT = 16
BLOCK_AT = 18
PRANDTL = 0.85
SCALES = (1.0, 1.0 / PRANDTL)
F32 = jnp.float32
BF16 = jnp.bfloat16
VMEM_BYTES = 20 * 1024 * 1024


def iota(shape, dim):
    return lax.broadcasted_iota(jnp.int32, shape, dim)


def pieces(values, count=3):
    out = []
    for _ in range(count):
        part = values.astype(BF16)
        out.append(part)
        values = values - part.astype(F32)
    return out


def dot(a, b, dims=((1,), (0,))):
    return lax.dot_general(a, b, (dims, ((), ())), preferred_element_type=F32)


def pick(choice, values, dims=((1,), (0,)), count=3):
    total = None
    for part in pieces(values, count):
        term = dot(choice, part, dims)
        total = term if total is None else total + term
    return total


def spread(choice, values, dims=((1,), (0,)), count=3):
    total = None
    for part in pieces(values, count):
        term = dot(part, choice, dims)
        total = term if total is None else total + term
    return total


def roll(values, amount, axis):
    size = values.shape[axis]
    amount = amount % size
    if amount == 0:
        return values
    return pltpu.roll(values, amount, axis)


def swaps(count):
    even = [(i, i ^ 1) for i in range(count) if (i ^ 1) < count]
    odd = [(i, i + 1 if i % 2 else i - 1) for i in range(1, count) if (i % 2 == 0) or i + 1 < count]
    return even, odd


def exchange(values, axis):
    even, odd = swaps(lax.axis_size(axis))
    return lax.ppermute(values, axis, even), lax.ppermute(values, axis, odd)


def low_high(even, odd, is_odd):
    return jnp.where(is_odd, even, odd), jnp.where(is_odd, odd, even)


def call(body, out_shape, scratch, *args, us=0.2):
    return pl.pallas_call(
        body,
        cost_estimate=pl.CostEstimate(
            flops=0, transcendentals=0, bytes_accessed=int(us * 3.6e6)
        ),
        out_shape=out_shape,
        scratch_shapes=scratch,
        compiler_params=pltpu.CompilerParams(vmem_limit_bytes=VMEM_BYTES),
    )(*args)


def slot_choices(owner_row, owners, count):
    records = owner_row.shape[1]
    named = owner_row == iota((owners, records), 0)
    earlier = (iota((records, records), 0) < iota((records, records), 1)).astype(BF16)
    rank = dot(named.astype(BF16), earlier)
    return [(named & (rank == k)).astype(BF16) for k in range(count)]


class row_slots:
    def __init__(self, ref, base, rows):
        self.ref, self.base, self.rows = ref, base, rows
        self.shape = ((ref.shape[0] - base) // rows, rows, ref.shape[1])

    def __getitem__(self, at):
        return self.ref[self.base + at * self.rows : self.base + (at + 1) * self.rows, :]

    def __setitem__(self, at, value):
        self.ref[self.base + at * self.rows : self.base + (at + 1) * self.rows, :] = value


def without_bit(slot, bit):
    return (slot >> (bit + 1) << bit) | (slot & ((1 << bit) - 1))


def bit_of(axis, bit):
    return lax.rem(lax.axis_index(axis) >> bit, 2)


def split_slots(slots, axis, bit, send, keep):
    mine = bit_of(axis, bit) == 1
    for d, low in enumerate(slots):
        if d >> bit & 1:
            continue
        high = slots[d | 1 << bit]
        at = without_bit(d, bit)
        send[at] = jnp.where(mine, low, high)
        keep[at] = jnp.where(mine, high, low)


def join_slots(keep, got, axis, bit):
    mine = bit_of(axis, bit)
    return [
        jnp.where(mine == (d >> bit & 1), keep[without_bit(d, bit)], got[without_bit(d, bit)])
        for d in range(2 * keep.shape[0])
    ]


def route_body(axis, bit, keep, got, next_send, next_keep):
    got = row_slots(got, got.shape[0] - keep.shape[0] * keep.shape[1], keep.shape[1])
    next_send = row_slots(next_send, 0, keep.shape[1])
    split_slots(join_slots(keep, got, axis, bit), axis, bit + 1, next_send, next_keep)


def swap(values, axis, pattern, low):
    count = lax.axis_size(axis)
    return lax.ppermute(values, axis, [(i, i ^ pattern << low) for i in range(count)])


def route(keep, got, axis, after=None):
    bits = lax.axis_size(axis).bit_length() - 1
    for bit in range(bits - 1):
        send = jax.ShapeDtypeStruct((keep.shape[0] * keep.shape[1], LANES), F32)
        half = jax.ShapeDtypeStruct(keep.shape, F32)
        send, keep = call(functools.partial(route_body, axis, bit), (send, half), [], keep, got)
        if after is not None:
            send, after = lax.optimization_barrier((send, after))
        got = swap(send, axis, 1, bit + 1)
    return keep, got


def choose(mine, values):
    out = values[0]
    for m in range(1, len(values)):
        out = jnp.where(mine == m, values[m], out)
    return out


def group_slots(count, low, width):
    span = 1 << width
    rests = [d for d in range(count) if (d >> low) % span == 0]
    return [[rest | p << low for p in range(span)] for rest in rests]


def my_bits(axis, low, width):
    return lax.rem(lax.axis_index(axis) >> low, 1 << width)


def part_slots(slots, axis, low, width, outs):
    mine = my_bits(axis, low, width)
    span = 1 << width
    for at, group in enumerate(group_slots(len(slots), low, width)):
        for v in range(span):
            outs[v][at] = choose(mine, [slots[group[m ^ v]] for m in range(span)])


def merge_slots(parts, count, axis, low, width):
    mine = my_bits(axis, low, width)
    span = 1 << width
    slots = [None] * count
    for at, group in enumerate(group_slots(count, low, width)):
        for p in range(span):
            slots[group[p]] = choose(mine, [parts[m ^ p][at] for m in range(span)])
    return slots


def stages(count):
    bits = count.bit_length() - 1
    return [(0, 1)] + [(low, min(2, bits - low)) for low in range(1, bits, 2)]


def return_body(count, before, after, *refs):
    parts, outs = refs[: 1 << before[1]], refs[1 << before[1] :]
    part_slots(merge_slots(parts, count, "gy", *before), "gy", *after, outs)


def send_back(parts, count):
    plan = stages(count)
    for i, stage in enumerate(plan):
        parts = [parts[0]] + [swap(p, "gy", v, stage[0]) for v, p in enumerate(parts) if v]
        if i + 1 < len(plan):
            after = plan[i + 1]
            piece = jax.ShapeDtypeStruct((count >> after[1],) + parts[0].shape[1:], F32)
            parts = call(
                functools.partial(return_body, count, stage, after),
                (piece,) * (1 << after[1]),
                [],
                *parts,
            )
    return parts


def records_out_body(n_gx, n_gy, cell, s_owner, obs, block, a_owner, ctrl, foot, send, keep, s_meta, a_meta, out):
    owners = n_gx * n_gy
    steps = obs.shape[1]
    s_meta[...] = jnp.zeros(s_meta.shape, F32)
    for s in range(2):
        s_meta[OBS_AT + s * steps : OBS_AT + (s + 1) * steps, :] = obs[s]
    s_meta[CELL_AT : CELL_AT + 1, :] = (cell[...] + 1).astype(F32)
    a_meta[...] = jnp.zeros(a_meta.shape, F32)
    a_meta[CTRL_AT : CTRL_AT + 2, :] = ctrl[...]
    a_meta[BLOCK_AT : BLOCK_AT + 1, :] = (block[...] + 1).astype(F32)
    s_all, a_all, f_all = s_meta[...], a_meta[...], foot[...]
    s_choice = slot_choices(s_owner[...], owners, CAPS)
    a_choice = slot_choices(a_owner[...], n_gy, CAPA)
    act_rows = jnp.zeros((n_gy, LANES), F32)
    sens_rows, foot_rows = [], []
    for k in range(CAPS):
        sens_rows.append(pick(s_choice[k], s_all, ((1,), (1,))))
        act_rows = act_rows + roll(pick(a_choice[k], a_all, ((1,), (1,))), 32 * k, 1)
        foot_rows.append(pick(a_choice[k], f_all))

    def moved(values, t):
        at = iota(values.shape, 0) % n_gy
        if t == 0:
            return jnp.where(at == 0, 0.0, roll(values, 1, 0))
        if t == 2:
            return jnp.where(at == n_gy - 1, 0.0, roll(values, values.shape[0] - 1, 0))
        return values

    packed = jnp.zeros((owners, LANES), F32)
    for t in range(3):
        for k in range(CAPS):
            out[:, 4 * t + k, :] = moved(foot_rows[k], t)
            packed = packed + roll(moved(sens_rows[k], t), PITCH * (CAPS * t + k), 1)
        out[:, 12 + t, :] = moved(act_rows, t)
    out[:, 15:, :] = jnp.zeros((n_gy, out.shape[1] - 15, LANES), F32)
    for d in range(n_gy):
        for i in range(n_gx):
            out[d, SLOT_ROWS + i : SLOT_ROWS + i + 1, :] = packed[i * n_gy + d : i * n_gy + d + 1]
    split_slots([out[d] for d in range(n_gy)], "gy", 0, row_slots(send, 0, out.shape[1]), keep)


def strips_body(state, kappa, vel, target, out):
    lane = iota((state.shape[2], LANES), 1)
    fields = [state.at[0], state.at[1], kappa, vel.at[0], vel.at[1], vel.at[2], target.at[0], target.at[1]]
    for tile in range(4):
        packed = jnp.zeros(lane.shape, F32)
        for g in range(2 * FX):
            plane = fields[2 * tile + g // FX][g % FX]
            packed = jnp.where(lane // (2 * RIM) == g, roll(plane, RIM + 2 * RIM * g, 1), packed)
        out[tile * lane.shape[0] : (tile + 1) * lane.shape[0], :] = packed


def rim_body(n_gx, even, odd, keep, got, sent, rim_target, sens_keep):
    is_odd = lax.rem(lax.axis_index("gy"), 2) == 1
    height = rim_target.shape[0]
    tiles = odd.shape[0] // height
    for tile in range(tiles):
        rows = slice(tile * height, (tile + 1) * height)
        left, right = low_high(even[rows, :], odd[rows, :], is_odd)
        lane = iota(left.shape, 1)
        value = jnp.where(lane % (2 * RIM) < RIM, roll(right, -RIM, 1), roll(left, RIM, 1))
        if tile == tiles - 1:
            rim_target[...] = value
        else:
            sent[rows, :] = value
    base = (tiles - 1) * height
    n_gy = 2 * keep.shape[0]
    rows = keep.shape[1]
    got = row_slots(got, got.shape[0] - keep.shape[0] * rows, rows)
    slots = join_slots(keep, got, "gy", n_gy.bit_length() - 2)
    for d in range(n_gy):
        sent[base + d * SLOT_ROWS : base + (d + 1) * SLOT_ROWS, :] = slots[d][:SLOT_ROWS]
    base = base + n_gy * SLOT_ROWS
    rows = [
        jnp.concatenate([slots[d][SLOT_ROWS + i : SLOT_ROWS + i + 1] for d in range(n_gy)], axis=0)
        for i in range(n_gx)
    ]
    split_slots(rows, "gx", 0, row_slots(sent, base, n_gy), sens_keep)


def rim_tile(packed, group):
    lane = iota(packed.shape, 1)
    right = roll(packed, -2 * RIM * group, 1)
    left = roll(packed, LANES - 2 * RIM - 2 * RIM * group, 1)
    return jnp.where(lane < RIM, right, jnp.where(lane >= LANES - RIM, left, 0.0))


def extended(field, main, main_e, main_o, rim, rim_e, rim_o, is_odd, x):
    height = main.shape[2]
    at, group = pl.ds(field // 2 * height, height), (field % 2) * FX + x % FX
    if x // FX == 1:
        centre, halo = main[field, x % FX], rim[at]
    elif x // FX == 0:
        centre = jnp.where(is_odd, main_e[field, x], main_o[field, x])
        halo = jnp.where(is_odd, rim_e[at], rim_o[at])
    else:
        centre = jnp.where(is_odd, main_o[field, x - 2 * FX], main_e[field, x - 2 * FX])
        halo = jnp.where(is_odd, rim_o[at], rim_e[at])
    return centre, rim_tile(halo, group)


def source_tile(n_gy, height, wide_y, records_in, planes, skip, out, stacked, placing, turned):
    records = n_gy * SLOT_ROWS
    blocks_y = wide_y // FY
    r_of, r_to = iota((records, records), 0), iota((records, records), 1)
    slot = r_of % SLOT_ROWS
    meta = jnp.zeros((records, LANES), F32)
    for k in range(CAPA):
        move = (slot < 12) & (slot % 4 == k) & (r_to == r_of - slot + 12 + slot // 4)
        meta = meta + pick(move.astype(BF16), roll(records_in, -32 * k, 1))
    q_of, l_of = iota((FOOT, FOOT), 0), iota((FOOT, FOOT), 1)
    unpack = (l_of == (q_of % 32) * FY + q_of // 32).astype(BF16)
    side = (iota((records, 1), 0) % SLOT_ROWS) // 4
    meta_t = meta.T
    block_row = meta_t[BLOCK_AT : BLOCK_AT + 1, :].astype(jnp.int32) - 1
    bz_row = block_row // blocks_y
    turned[...] = pick(unpack, records_in, ((1,), (1,)), 2)
    block_col = meta[:, BLOCK_AT : BLOCK_AT + 1].astype(jnp.int32) - 1
    by = block_col % blocks_y
    usable = (block_col >= 0) & (
        (side == 1)
        | ((side == 0) & (by * FY >= wide_y - RIM))
        | ((side == 2) & (by * FY < RIM))
    )
    start = jnp.where(side == 1, by * FY, wide_y + by * FY)
    start = jnp.where(usable, start, -FY)
    wide_lane = iota((records, 2 * wide_y), 1)
    for fy in range(FY):
        placing[fy * records : (fy + 1) * records, :] = (wide_lane == start + fy).astype(BF16)
    rows_out = planes * height
    for s in range(2):
        force = meta_t[CTRL_AT + s : CTRL_AT + s + 1, :]
        for fy in range(FY):
            lanes = slice(fy * records, (fy + 1) * records)
            for i in range(planes):
                at = pl.multiple_of(fy * 32 + (i + skip) * FZ, FZ)
                scaled = turned[pl.ds(at, FZ), :] * force
                for bz in range(height // FZ):
                    at = i * height + bz * FZ
                    stacked[at : at + FZ, lanes] = jnp.where(bz_row == bz, scaled, 0.0)
        value = spread(placing[...], stacked[:rows_out, :], count=2)
        for i in range(planes):
            out[s, i] = value[i * height : (i + 1) * height]
    return meta, meta_t


def own_source_body(n_gy, height, wide_y, got, source, foot_hot, foot_own, stacked, placing, turned):
    records = n_gy * SLOT_ROWS
    blocks_y = wide_y // FY
    base = 3 * height
    records_in = got[base : base + records, :]
    meta, meta_t = source_tile(
        n_gy, height, wide_y, records_in, FX, 0, source, stacked, placing, turned
    )
    held = n_gy * CAPA
    r_of, r_to = iota((held, records), 0), iota((held, records), 1)
    own = (r_to == r_of // CAPA * SLOT_ROWS + CAPA + r_of % CAPA).astype(BF16)
    block_row = spread(own, meta_t[CTRL_AT : CTRL_AT + 8], ((1,), (1,)))[BLOCK_AT - CTRL_AT :]
    bz_row = (block_row[:1].astype(jnp.int32) - 1) // blocks_y
    block_col = pick(own, meta)[:, BLOCK_AT : BLOCK_AT + 1].astype(jnp.int32) - 1
    start = jnp.where(block_col >= 0, block_col % blocks_y * FY, -FY)
    q_of, l_of = iota((FOOT, FOOT), 0), iota((FOOT, FOOT), 1)
    unpack = (l_of == (q_of % 32) * FY + q_of // 32).astype(BF16)
    foot_t = pick(unpack, pick(own, records_in), ((1,), (1,)))
    lane = iota((held, wide_y), 1)
    for fy in range(FY):
        lanes = slice(fy * held, (fy + 1) * held)
        foot_hot[lanes, :] = (lane == start + fy).astype(BF16)
        for x in range(FX):
            piece = foot_t[fy * 32 + x * FZ : fy * 32 + (x + 1) * FZ, :]
            for bz in range(height // FZ):
                at = x * height + bz * FZ
                foot_own[at : at + FZ, lanes] = jnp.where(bz_row == bz, piece, 0.0)


def side_source_body(n_gy, height, wide_y, low_parity, got, source, stacked, placing, turned):
    is_low = lax.rem(lax.axis_index("gx"), 2) == low_parity
    records_in = got[3 * height : 3 * height + n_gy * SLOT_ROWS, :]
    skip = jnp.where(is_low, 1, 0)
    source_tile(
        n_gy, height, wide_y, records_in, FX - 1, skip, source, stacked, placing, turned
    )


def sensors_body(height, keep, got, spot_hot, lane_hot, z_hot, rim_hot, readings, table):
    n_gx = 2 * keep.shape[0]
    got = row_slots(got, got.shape[0] - keep.shape[0] * keep.shape[1], keep.shape[1])
    rows = jnp.concatenate(join_slots(keep, got, "gx", n_gx.bit_length() - 2), axis=0)
    devices = rows.shape[0]
    slots = 3 * CAPS * devices
    own = slots // 3
    for n, t in enumerate((1, 0, 2)):
        for k in range(CAPS):
            at = (n * CAPS + k) * devices
            table[at : at + devices, :] = roll(rows, -PITCH * (CAPS * t + k), 1)
    cells = []
    for part in range(slots // LANES):
        lanes = slice(part * LANES, (part + 1) * LANES)
        turned = table[lanes, :].T
        cell = turned[CELL_AT : CELL_AT + 1, :].astype(jnp.int32) - 1
        at_y = cell % LANES
        slot_id = iota((1, LANES), 1) + part * LANES
        live = (cell >= 0) & (
            (slot_id < own)
            | ((slot_id < 2 * own) & (at_y >= LANES - RIM))
            | ((slot_id >= 2 * own) & (at_y < RIM))
        )
        cell = jnp.where(live, cell, -1)
        readings[0:8, lanes] = turned[OBS_AT : OBS_AT + 8]
        readings[8:16, lanes] = jnp.broadcast_to((cell + 1).astype(F32), (8, LANES))
        cells.append(cell)
    cell = jnp.concatenate(cells, axis=1)
    spot, lane = own_hot(cell[:, :own], height)
    spot_hot[...] = spot
    lane_hot[...] = lane
    z, rim = rim_hot_pair(cell[:, own:], height)
    z_hot[...] = z
    rim_hot[...] = rim


def own_hot(cell, height):
    spot = jnp.where(cell >= 0, cell // LANES, -1)
    at_y = jnp.where(cell >= 0, cell % LANES, -1)
    slots = cell.shape[1]
    return (
        (iota((FX * height, slots), 0) == spot).astype(BF16),
        (iota((LANES, slots), 0) == at_y).astype(BF16),
    )


def rim_hot_pair(cell, height):
    spot, at_y = cell // LANES, cell % LANES
    z = jnp.where(cell >= 0, spot % height, -1)
    lane = jnp.where(at_y < RIM, at_y, at_y - LANES + 2 * RIM)
    lane = jnp.where(cell >= 0, spot // height * 2 * RIM + lane, -1)
    slots = cell.shape[1]
    return (
        (iota((height, slots), 0) == z).astype(BF16),
        (iota((2 * RIM * FX, slots), 0) == lane).astype(BF16),
    )


def paired(hot):
    blank = jnp.zeros_like(hot)
    return jnp.concatenate(
        [jnp.concatenate([hot, blank], axis=1), jnp.concatenate([blank, hot], axis=1)], axis=0
    )


def inject(row_hot, lane_hot, values):
    placed = jnp.concatenate([lane_hot.astype(F32) * value for value in values], axis=0)
    total = None
    for part in pieces(placed, 2):
        term = dot(row_hot, part, ((1,), (1,)))
        total = term if total is None else total + term
    return total


def pack_rims(halos):
    packed = jnp.zeros(halos[0].shape, F32)
    lane = iota(packed.shape, 1)
    for g, halo in enumerate(halos):
        at = lane - 2 * RIM * g
        packed = jnp.where((at >= 0) & (at < RIM), roll(halo, 2 * RIM * g, 1), packed)
        packed = jnp.where(
            (at >= RIM) & (at < 2 * RIM), roll(halo, 2 * RIM * g + 2 * RIM, 1), packed
        )
    return packed


def coeffs_body(main, main_e, main_o, rim, rim_e, rim_o, coeffs, start, half_k):
    refs = (main, main_e, main_o, rim, rim_e, rim_o)
    is_odd = lax.rem(lax.axis_index("gx"), 2) == 1
    wide = 3 * FX
    height = half_k.shape[1]
    shape = (height, 2 * LANES)
    z = iota(shape, 0)
    for x in range(wide):
        centre, halo = extended(2, *refs, is_odd, x)
        half_k[x, :, :LANES] = 0.5 * centre
        half_k[x, :, LANES:] = 0.5 * halo
        for s in range(2):
            centre, halo = extended(s, *refs, is_odd, x)
            start[s, x, :, :LANES] = centre
            start[s, x, :, LANES:] = halo
    for x in range(wide):
        k = half_k[x]
        faces = (
            k + half_k[min(x + 1, wide - 1)],
            k + half_k[max(x - 1, 0)],
            k + roll(k, -1, 1),
            k + roll(k, 1, 1),
            k + jnp.where(z == height - 1, 0.0, roll(k, -1, 0)),
            k + jnp.where(z == 0, 0.0, roll(k, 1, 0)),
        )
        total = (faces[0] + faces[1]) + (faces[2] + faces[3]) + (faces[4] + faces[5])
        drift = []
        for axis in range(3):
            centre, halo = extended(3 + axis, *refs, is_odd, x)
            drift.append(0.5 * jnp.concatenate([centre, halo], axis=1))
        for s in range(2):
            coeffs[s, 6, x] = 1.0 - SCALES[s] * total
            for face in range(6):
                value = faces[face] if s == 0 else SCALES[s] * faces[face]
                value = value - drift[face // 2] if face % 2 == 0 else value + drift[face // 2]
                if face == 4:
                    value = jnp.where(z == height - 1, 0.0, value)
                if face == 5:
                    value = jnp.where(z == 0, 0.0, value)
                coeffs[s, face, x] = value


def inside_rows(n_gx, n_gy):
    row_id, col_id = lax.axis_index("gx"), lax.axis_index("gy")
    lane = iota((1, 2 * LANES), 1)
    lanes_in = (
        (lane < LANES)
        | ((lane < LANES + RIM) & (col_id < n_gy - 1))
        | ((lane >= 2 * LANES - RIM) & (col_id > 0))
    ).astype(F32)
    low = jnp.where(row_id > 0, lanes_in, 0.0)
    high = jnp.where(row_id < n_gx - 1, lanes_in, 0.0)
    return lambda x: low if x < FX else (lanes_in if x < 2 * FX else high)


def forward_body(n_gx, n_gy, steps, coeffs, start, rim_target, own_source, source_e, source_o, spot_hot, lane_hot, z_hot, rim_hot, readings, target, final, sent, residuals, cur):
    height = start.shape[2]
    wide = 3 * FX
    cells = FX * height
    slots = readings.shape[1]
    own = slots // 3
    rest = slots - own
    inside = inside_rows(n_gx, n_gy)
    fields = [start, cur.at[0], cur.at[1], cur.at[0], cur.at[1]]
    residuals[...] = jnp.zeros(residuals.shape, F32)
    live = (readings[8:9, :] > 0.5).astype(F32)
    is_odd = lax.rem(lax.axis_index("gx"), 2) == 1
    lane_pair, rim_pair = paired(lane_hot[...]), paired(rim_hot[...])
    spots = spot_hot[...].astype(F32)
    heights = z_hot[...].astype(F32)

    def source(s, x):
        if x < FX:
            return jnp.where(is_odd, source_e[s, x - 1], source_o[s, x - 1])
        if x < 2 * FX:
            return own_source[s, x - FX]
        return jnp.where(is_odd, source_o[s, x - 2 * FX], source_e[s, x - 2 * FX])

    for n in range(steps):
        before, after = fields[n], fields[n + 1]
        for x in range(n + 1, wide - n - 1):
            row = inside(x)
            for s in range(2):
                c = before[s, x]
                value = coeffs[s, 6, x] * c + source(s, x)
                value = value + coeffs[s, 0, x] * before[s, x + 1]
                value = value + coeffs[s, 1, x] * before[s, x - 1]
                value = value + coeffs[s, 2, x] * roll(c, -1, 1)
                value = value + coeffs[s, 3, x] * roll(c, 1, 1)
                value = value + coeffs[s, 4, x] * roll(c, -1, 0)
                value = value + coeffs[s, 5, x] * roll(c, 1, 0)
                after[s, x] = value * row
        both = jnp.concatenate(
            [after[s, FX : 2 * FX, :, :LANES].reshape(cells, LANES) for s in range(2)], axis=1
        )
        seen = spread(lane_pair, both)
        packed = pack_rims([after[s, FX + p, :, LANES:] for s in range(2) for p in range(FX)])
        seen_rim = spread(rim_pair, packed)
        for s in range(2):
            at = s * steps + n
            value = jnp.sum(seen[:, s * own : (s + 1) * own] * spots, axis=0, keepdims=True)
            value = (value - readings[at : at + 1, :own]) * live[:, :own]
            residuals[at : at + 1, :own] = value
            value = jnp.sum(seen_rim[:, s * rest : (s + 1) * rest] * heights, axis=0, keepdims=True)
            value = (value - readings[at : at + 1, own:]) * live[:, own:]
            residuals[at : at + 1, own:] = value
    residuals[8:16, :] = readings[8:16, :]
    last = fields[steps]
    ends = [residuals[s * steps + steps - 1 : (s + 1) * steps, :] for s in range(2)]
    put = inject(spot_hot[...], lane_hot[...], [end[:, :own] for end in ends])
    put_rim = inject(z_hot[...], rim_hot[...], [end[:, own:] for end in ends])
    for s in range(2):
        for p in range(FX):
            rows = slice(p * height, (p + 1) * height)
            got = last[s, FX + p, :, :LANES]
            final[s, p] = got
            g = s * FX + p
            sent[g * height : (g + 1) * height, :] = (
                got - target[s, p] + put[rows, s * LANES : (s + 1) * LANES]
            )
    base = 2 * FX * height
    sent[base : base + height, :] = packed - rim_target[...] + put_rim
    base = base + height
    for part in range(slots // LANES):
        lanes = slice(part * LANES, (part + 1) * LANES)
        rows = [residuals[s * steps + n : s * steps + n + 1, lanes] for s in range(2) for n in range(steps - 1)]
        for i, values in enumerate(rows + [residuals[8:9, lanes]] * (8 - len(rows))):
            sent[base + 8 * part + i : base + 8 * part + i + 1, :] = values


def own_puts_body(steps, spot_hot, lane_hot, z_hot, rim_hot, residuals, puts):
    slots = residuals.shape[1]
    own = slots // 3
    _, _, planes, height, _ = puts.shape
    for n in range(steps - 1):
        values = [residuals[s * steps + n : s * steps + n + 1, :] for s in range(2)]
        put = inject(spot_hot[...], lane_hot[...], [value[:, :own] for value in values])
        put_rim = inject(z_hot[...], rim_hot[...], [value[:, own:] for value in values])
        for s in range(2):
            for p in range(planes):
                rows = slice(p * height, (p + 1) * height)
                puts[n, s, p, :, :LANES] = put[rows, s * LANES : (s + 1) * LANES]
                puts[n, s, p, :, LANES:] = rim_tile(put_rim, s * FX + p)


def adjoint_body(n_gx, n_gy, steps, coeffs, sent, sent_e, sent_o, own_puts, foot_hot, foot_own, back_keep, back_send, second, cur, puts, summed):
    is_odd = lax.rem(lax.axis_index("gx"), 2) == 1
    height = coeffs.shape[3]
    wide = 3 * FX
    cells = FX * height
    base = 2 * FX * height
    table = base + height
    slots = (sent.shape[0] - table) // 8 * LANES
    own = slots // 3
    inside = inside_rows(n_gx, n_gy)
    for q in (1, 0, 2):
        def take(lo, hi):
            if q == 1:
                return sent[lo:hi, :]
            if q == 0:
                return jnp.where(is_odd, sent_e[lo:hi, :], sent_o[lo:hi, :])
            return jnp.where(is_odd, sent_o[lo:hi, :], sent_e[lo:hi, :])
        packed_rim = take(base, base + height)
        for s in range(2):
            for p in range(FX):
                g = s * FX + p
                cur[0, s, q * FX + p, :, :LANES] = take(g * height, (g + 1) * height)
                cur[0, s, q * FX + p, :, LANES:] = rim_tile(packed_rim, g)
        if q == 1:
            continue
        rows = jnp.concatenate(
            [take(table + 8 * i, table + 8 * i + 8) for i in range(slots // LANES)], axis=1
        )
        cell = rows[7:8, :].astype(jnp.int32) - 1
        spot, lane = own_hot(cell[:, :own], height)
        z, rim = rim_hot_pair(cell[:, own:], height)
        for n in range(steps - 1):
            reach = (n + 1) * height
            part = slice(cells - reach, cells) if q == 0 else slice(0, reach)
            first = FX - n - 1 if q == 0 else 0
            values = [rows[s * (steps - 1) + n : s * (steps - 1) + n + 1, :] for s in range(2)]
            put = inject(spot[part], lane, [value[:, :own] for value in values])
            put_rim = inject(z, rim, [value[:, own:] for value in values])
            for s in range(2):
                for i in range(n + 1):
                    x = q * FX + first + i
                    puts[n, s, x, :, :LANES] = put[
                        i * height : (i + 1) * height, s * LANES : (s + 1) * LANES
                    ]
                    puts[n, s, x, :, LANES:] = rim_tile(put_rim, s * FX + first + i)
    for s in range(2):
        summed[s * cells : (s + 1) * cells, :] = sent[s * cells : (s + 1) * cells, :]
    for turn in range(steps - 1):
        now, later = turn % 2, (turn + 1) % 2
        n = steps - 2 - turn
        for x in range(turn + 1, wide - turn - 1):
            for s in range(2):
                put = own_puts[n, s, x - FX] if FX <= x < 2 * FX else puts[n, s, x]
                value = adjoint_value(coeffs, cur.at[now], s, x, 0) + put
                value = value * inside(x)
                if turn == steps - 2:
                    second[s, x - steps + 1] = value
                else:
                    cur[later, s, x] = value
                if FX <= x < 2 * FX:
                    at = s * cells + (x - FX) * height
                    summed[at : at + height, :] = summed[at : at + height, :] + value[:, :LANES]
    seen = spread(foot_hot[...], summed[...], ((1,), (1,)), count=2)
    width = foot_own.shape[1]
    held = width // FY
    out_from = iota((1, width), 1) // CAPA
    totals = []
    for s in range(2):
        row = jnp.sum(seen[s * cells : (s + 1) * cells] * foot_own[...], axis=0, keepdims=True)
        total = row
        for fy in range(1, FY):
            total = total + roll(row, -fy * held, 1)
        totals.append(total)
    block = jnp.concatenate(totals + [jnp.zeros((6, width), F32)], axis=0)
    slots = [jnp.where(out_from == d, block, 0.0) for d in range(n_gy)]
    part_slots(slots, "gy", 0, 1, (back_keep, back_send))


def adjoint_value(coeffs, field, s, x, shift):
    w = field[s, x - shift]
    value = coeffs[s, 6, x] * w
    value = value + coeffs[s, 1, x + 1] * field[s, x + 1 - shift]
    value = value + coeffs[s, 0, x - 1] * field[s, x - 1 - shift]
    value = value + roll(coeffs[s, 3, x] * w, -1, 1)
    value = value + roll(coeffs[s, 2, x] * w, 1, 1)
    value = value + roll(coeffs[s, 5, x] * w, -1, 0)
    return value + roll(coeffs[s, 4, x] * w, 1, 0)


def last_body(steps, coeffs, second, first):
    for x in range(FX, 2 * FX):
        for s in range(2):
            first[s, x - FX] = adjoint_value(coeffs, second, s, x, steps - 1)[:, :LANES]


def returned_body(n_gy, *refs):
    low, width = stages(n_gy)[-1]
    parts, (owner, out) = refs[: 1 << width], refs[1 << width :]
    slots = merge_slots(parts, n_gy, "gy", low, width)
    records = slots[0].shape[1]
    base = lax.axis_index("gy") * CAPA
    choice = slot_choices(owner[...], n_gy, CAPA)
    lane = iota((n_gy, records), 1)
    for s in range(2):
        rows = jnp.concatenate([slot[s : s + 1] for slot in slots], axis=0)
        total = jnp.zeros(choice[0].shape, F32)
        for k in range(CAPA):
            column = jnp.sum(jnp.where(lane == base + k, rows, 0.0), axis=1, keepdims=True)
            total = total + choice[k].astype(F32) * column
        out[s : s + 1, :] = jnp.sum(total, axis=0, keepdims=True)


def per_device(
    initial_state,
    eddy_diffusivity,
    velocity,
    target,
    sensor_cell,
    sensor_owner,
    observations,
    actuator_block,
    actuator_owner,
    controls,
    footprint,
):
    _, wide_x, height, wide_y = initial_state.shape
    steps = observations.shape[2]
    n_gx, n_gy = lax.axis_size("gx"), lax.axis_size("gy")
    devices = n_gx * n_gy
    sens, acts = sensor_cell.shape[0], actuator_block.shape[0]
    records = n_gy * SLOT_ROWS
    slots = 3 * CAPS * devices
    cells = FX * height
    wide = 3 * FX
    shape = jax.ShapeDtypeStruct
    vmem = pltpu.VMEM
    a_owner_row = actuator_owner.reshape(1, acts)
    main = jnp.concatenate([initial_state, eddy_diffusivity[None], velocity], axis=0)
    slot_rows = SLOT_ROWS + -(-n_gx // 8) * 8
    half = shape((n_gy // 2, slot_rows, LANES), F32)
    sens_half = shape((n_gx // 2, n_gy, LANES), F32)
    strip_rows = 4 * height
    acts_send, acts_keep = call(
        functools.partial(records_out_body, n_gx, n_gy),
        (
            shape((n_gy // 2 * slot_rows, LANES), F32),
            half,
        ),
        [
            vmem((LANES, sens), F32),
            vmem((LANES, acts), F32),
            vmem((n_gy, slot_rows, LANES), F32),
        ],
        sensor_cell.reshape(1, sens),
        sensor_owner.reshape(1, sens),
        observations.transpose(1, 2, 0),
        actuator_block.reshape(1, acts),
        a_owner_row,
        controls.T,
        footprint,
    )
    strips = call(
        strips_body,
        shape((strip_rows, LANES), F32),
        [],
        initial_state,
        eddy_diffusivity,
        velocity,
        target,
    )
    main_e, main_o = exchange(main, "gx")
    strips_e, strips_o = exchange(strips, "gy")
    acts_keep, acts_got = route(acts_keep, swap(acts_send, "gy", 1, 0), "gy")
    rim, rim_target, sens_keep = call(
        functools.partial(rim_body, n_gx),
        (
            shape((3 * height + records + n_gx // 2 * n_gy, LANES), F32),
            shape((height, LANES), F32),
            sens_half,
        ),
        [],
        strips_e, strips_o, acts_keep, acts_got,
    )
    rim_e, rim_o = exchange(rim, "gx")
    held = n_gy * CAPA
    scratch = [
        vmem((cells, FY * records), F32),
        vmem((FY * records, 2 * LANES), BF16),
        vmem((FOOT, records), F32),
    ]
    own_source, foot_hot, foot_own = call(
        functools.partial(own_source_body, n_gy, height, wide_y),
        (
            shape((2, FX, height, 2 * LANES), F32),
            shape((FY * held, LANES), BF16),
            shape((cells, FY * held), F32),
        ),
        scratch,
        rim,
        us=1.5,
    )
    source_e, source_o = [
        call(
            functools.partial(side_source_body, n_gy, height, wide_y, low_parity),
            shape((2, FX - 1, height, 2 * LANES), F32),
            scratch,
            got,
            us=0.8,
        )
        for low_parity, got in ((1, rim_e), (0, rim_o))
    ]
    sens_keep, sens_got = route(sens_keep, rim_e, "gx", after=foot_hot)
    coeffs, start = call(
        coeffs_body,
        (
            shape((2, 7, wide, height, 2 * LANES), F32),
            shape((2, wide, height, 2 * LANES), F32),
        ),
        [vmem((wide, height, 2 * LANES), F32)],
        main, main_e, main_o, rim, rim_e, rim_o,
        us=1.6,
    )
    sens_keep, start = lax.optimization_barrier((sens_keep, start))
    own_slots = slots // 3
    rest = slots - own_slots
    *hots, readings = call(
        functools.partial(sensors_body, height),
        (
            shape((cells, own_slots), BF16),
            shape((LANES, own_slots), BF16),
            shape((height, rest), BF16),
            shape((2 * RIM * FX, rest), BF16),
            shape((16, slots), F32),
        ),
        [vmem((slots, LANES), F32)],
        sens_keep, sens_got,
    )
    sent_rows = 2 * cells + height + slots // LANES * 8
    final, sent, residuals = call(
        functools.partial(forward_body, n_gx, n_gy, steps),
        (
            shape((2, FX, height, LANES), F32),
            shape((sent_rows, LANES), F32),
            shape((16, slots), F32),
        ),
        [vmem((2, 2, wide, height, 2 * LANES), F32)],
        coeffs, start, rim_target, own_source, source_e, source_o, *hots, readings, target,
        us=5.0,
    )
    sent_e, sent_o = exchange(sent, "gx")
    own_puts = call(
        functools.partial(own_puts_body, steps),
        shape((steps - 1, 2, FX, height, 2 * LANES), F32),
        [],
        *hots, residuals,
        us=0.7,
    )
    back_keep, back_send, second = call(
        functools.partial(adjoint_body, n_gx, n_gy, steps),
        (
            shape((n_gy // 2, 8, FY * held), F32),
            shape((n_gy // 2, 8, FY * held), F32),
            shape((2, wide - 2 * steps + 2, height, 2 * LANES), F32),
        ),
        [
            vmem((2, 2, wide, height, 2 * LANES), F32),
            vmem((steps - 1, 2, wide, height, 2 * LANES), F32),
            vmem((2 * cells, LANES), F32),
        ],
        coeffs, sent, sent_e, sent_o, own_puts, foot_hot, foot_own,
        us=4.0,
    )
    back = send_back([back_keep, back_send], n_gy)
    first = call(
        functools.partial(last_body, steps),
        shape((2, FX, height, LANES), F32),
        [],
        coeffs, second,
        us=1.0,
    )
    returned = call(
        functools.partial(returned_body, n_gy), shape((2, acts), F32), [], *back, a_owner_row
    )
    return (final, first, returned.T)


def solution(mesh):
    in_specs = (
        P(None, "gx", None, "gy"),
        P("gx", None, "gy"),
        P(None, "gx", None, "gy"),
        P(None, "gx", None, "gy"),
        P(("gx", "gy")),
        P(("gx", "gy"), None),
        P(("gx", "gy"), None, None),
        P(("gx", "gy")),
        P(("gx", "gy"), None),
        P(("gx", "gy"), None),
        P(("gx", "gy"), None),
    )
    out_specs = (P(None, "gx", None, "gy"), P(None, "gx", None, "gy"), P(("gx", "gy"), None))
    return jax.shard_map(
        per_device, mesh=mesh, in_specs=in_specs, out_specs=out_specs, check_vma=False
    )
```

```python
import functools

import jax
import jax.numpy as jnp
from jax import lax
from jax.experimental import pallas as pl
from jax.experimental.pallas import tpu as pltpu
from jax.sharding import PartitionSpec as P

FX = 4
FZ = 8
FY = 4
CAPS = 4
CAPA = 4
FOOT = 128
RIM = 8
LANES = 128
SLOT_ROWS = 16
OBS_AT = 0
CELL_AT = 8
PITCH = 10
CTRL_AT = 16
BLOCK_AT = 18
PRANDTL = 0.85
SCALES = (1.0, 1.0 / PRANDTL)
F32 = jnp.float32
BF16 = jnp.bfloat16
VMEM_BYTES = 20 * 1024 * 1024


def iota(shape, dim):
    return lax.broadcasted_iota(jnp.int32, shape, dim)


def pieces(values, count=3):
    out = []
    for _ in range(count):
        part = values.astype(BF16)
        out.append(part)
        values = values - part.astype(F32)
    return out


def dot(a, b, dims=((1,), (0,))):
    return lax.dot_general(a, b, (dims, ((), ())), preferred_element_type=F32)


def pick(choice, values, dims=((1,), (0,)), count=3):
    total = None
    for part in pieces(values, count):
        term = dot(choice, part, dims)
        total = term if total is None else total + term
    return total


def spread(choice, values, dims=((1,), (0,)), count=3):
    total = None
    for part in pieces(values, count):
        term = dot(part, choice, dims)
        total = term if total is None else total + term
    return total


def roll(values, amount, axis):
    size = values.shape[axis]
    amount = amount % size
    if amount == 0:
        return values
    return pltpu.roll(values, amount, axis)


def swaps(count):
    even = [(i, i ^ 1) for i in range(count) if (i ^ 1) < count]
    odd = [(i, i + 1 if i % 2 else i - 1) for i in range(1, count) if (i % 2 == 0) or i + 1 < count]
    return even, odd


def exchange(values, axis):
    even, odd = swaps(lax.axis_size(axis))
    return lax.ppermute(values, axis, even), lax.ppermute(values, axis, odd)


def low_high(even, odd, is_odd):
    return jnp.where(is_odd, even, odd), jnp.where(is_odd, odd, even)


def call(body, out_shape, scratch, *args, us=0.2):
    return pl.pallas_call(
        body,
        cost_estimate=pl.CostEstimate(
            flops=0, transcendentals=0, bytes_accessed=int(us * 3.6e6)
        ),
        out_shape=out_shape,
        scratch_shapes=scratch,
        compiler_params=pltpu.CompilerParams(vmem_limit_bytes=VMEM_BYTES),
    )(*args)


def slot_choices(owner_row, owners, count):
    records = owner_row.shape[1]
    named = owner_row == iota((owners, records), 0)
    earlier = (iota((records, records), 0) < iota((records, records), 1)).astype(BF16)
    rank = dot(named.astype(BF16), earlier)
    return [(named & (rank == k)).astype(BF16) for k in range(count)]


class row_slots:
    def __init__(self, ref, base, rows):
        self.ref, self.base, self.rows = ref, base, rows
        self.shape = ((ref.shape[0] - base) // rows, rows, ref.shape[1])

    def __getitem__(self, at):
        return self.ref[self.base + at * self.rows : self.base + (at + 1) * self.rows, :]

    def __setitem__(self, at, value):
        self.ref[self.base + at * self.rows : self.base + (at + 1) * self.rows, :] = value


def without_bit(slot, bit):
    return (slot >> (bit + 1) << bit) | (slot & ((1 << bit) - 1))


def bit_of(axis, bit):
    return lax.rem(lax.axis_index(axis) >> bit, 2)


def split_slots(slots, axis, bit, send, keep):
    mine = bit_of(axis, bit) == 1
    for d, low in enumerate(slots):
        if d >> bit & 1:
            continue
        high = slots[d | 1 << bit]
        at = without_bit(d, bit)
        send[at] = jnp.where(mine, low, high)
        keep[at] = jnp.where(mine, high, low)


def join_slots(keep, got, axis, bit):
    mine = bit_of(axis, bit)
    return [
        jnp.where(mine == (d >> bit & 1), keep[without_bit(d, bit)], got[without_bit(d, bit)])
        for d in range(2 * keep.shape[0])
    ]


def route_body(axis, bit, keep, got, next_send, next_keep):
    got = row_slots(got, got.shape[0] - keep.shape[0] * keep.shape[1], keep.shape[1])
    next_send = row_slots(next_send, 0, keep.shape[1])
    split_slots(join_slots(keep, got, axis, bit), axis, bit + 1, next_send, next_keep)


def swap(values, axis, pattern, low):
    count = lax.axis_size(axis)
    return lax.ppermute(values, axis, [(i, i ^ pattern << low) for i in range(count)])


def route(keep, got, axis, after=None):
    bits = lax.axis_size(axis).bit_length() - 1
    for bit in range(bits - 1):
        send = jax.ShapeDtypeStruct((keep.shape[0] * keep.shape[1], LANES), F32)
        half = jax.ShapeDtypeStruct(keep.shape, F32)
        send, keep = call(functools.partial(route_body, axis, bit), (send, half), [], keep, got)
        if after is not None:
            send, after = lax.optimization_barrier((send, after))
        got = swap(send, axis, 1, bit + 1)
    return keep, got


def choose(mine, values):
    out = values[0]
    for m in range(1, len(values)):
        out = jnp.where(mine == m, values[m], out)
    return out


def group_slots(count, low, width):
    span = 1 << width
    rests = [d for d in range(count) if (d >> low) % span == 0]
    return [[rest | p << low for p in range(span)] for rest in rests]


def my_bits(axis, low, width):
    return lax.rem(lax.axis_index(axis) >> low, 1 << width)


def part_slots(slots, axis, low, width, outs):
    mine = my_bits(axis, low, width)
    span = 1 << width
    for at, group in enumerate(group_slots(len(slots), low, width)):
        for v in range(span):
            outs[v][at] = choose(mine, [slots[group[m ^ v]] for m in range(span)])


def merge_slots(parts, count, axis, low, width):
    mine = my_bits(axis, low, width)
    span = 1 << width
    slots = [None] * count
    for at, group in enumerate(group_slots(count, low, width)):
        for p in range(span):
            slots[group[p]] = choose(mine, [parts[m ^ p][at] for m in range(span)])
    return slots


def stages(count):
    bits = count.bit_length() - 1
    return [(0, 1)] + [(low, min(2, bits - low)) for low in range(1, bits, 2)]


def return_body(count, before, after, *refs):
    parts, outs = refs[: 1 << before[1]], refs[1 << before[1] :]
    part_slots(merge_slots(parts, count, "gy", *before), "gy", *after, outs)


def send_back(parts, count):
    plan = stages(count)
    for i, stage in enumerate(plan):
        parts = [parts[0]] + [swap(p, "gy", v, stage[0]) for v, p in enumerate(parts) if v]
        if i + 1 < len(plan):
            after = plan[i + 1]
            piece = jax.ShapeDtypeStruct((count >> after[1],) + parts[0].shape[1:], F32)
            parts = call(
                functools.partial(return_body, count, stage, after),
                (piece,) * (1 << after[1]),
                [],
                *parts,
            )
    return parts


def records_out_body(n_gx, n_gy, cell, s_owner, obs, block, a_owner, ctrl, foot, send, keep, s_meta, a_meta, out):
    owners = n_gx * n_gy
    steps = obs.shape[1]
    s_meta[...] = jnp.zeros(s_meta.shape, F32)
    for s in range(2):
        s_meta[OBS_AT + s * steps : OBS_AT + (s + 1) * steps, :] = obs[s]
    s_meta[CELL_AT : CELL_AT + 1, :] = (cell[...] + 1).astype(F32)
    a_meta[...] = jnp.zeros(a_meta.shape, F32)
    a_meta[CTRL_AT : CTRL_AT + 2, :] = ctrl[...]
    a_meta[BLOCK_AT : BLOCK_AT + 1, :] = (block[...] + 1).astype(F32)
    s_all, a_all, f_all = s_meta[...], a_meta[...], foot[...]
    s_choice = slot_choices(s_owner[...], owners, CAPS)
    a_choice = slot_choices(a_owner[...], n_gy, CAPA)
    act_rows = jnp.zeros((n_gy, LANES), F32)
    sens_rows, foot_rows = [], []
    for k in range(CAPS):
        sens_rows.append(pick(s_choice[k], s_all, ((1,), (1,))))
        act_rows = act_rows + roll(pick(a_choice[k], a_all, ((1,), (1,))), 32 * k, 1)
        foot_rows.append(pick(a_choice[k], f_all))

    def moved(values, t):
        at = iota(values.shape, 0) % n_gy
        if t == 0:
            return jnp.where(at == 0, 0.0, roll(values, 1, 0))
        if t == 2:
            return jnp.where(at == n_gy - 1, 0.0, roll(values, values.shape[0] - 1, 0))
        return values

    packed = jnp.zeros((owners, LANES), F32)
    for t in range(3):
        for k in range(CAPS):
            out[:, 4 * t + k, :] = moved(foot_rows[k], t)
            packed = packed + roll(moved(sens_rows[k], t), PITCH * (CAPS * t + k), 1)
        out[:, 12 + t, :] = moved(act_rows, t)
    out[:, 15:, :] = jnp.zeros((n_gy, out.shape[1] - 15, LANES), F32)
    for d in range(n_gy):
        for i in range(n_gx):
            out[d, SLOT_ROWS + i : SLOT_ROWS + i + 1, :] = packed[i * n_gy + d : i * n_gy + d + 1]
    split_slots([out[d] for d in range(n_gy)], "gy", 0, row_slots(send, 0, out.shape[1]), keep)


def strips_body(state, kappa, vel, target, out):
    lane = iota((state.shape[2], LANES), 1)
    fields = [state.at[0], state.at[1], kappa, vel.at[0], vel.at[1], vel.at[2], target.at[0], target.at[1]]
    for tile in range(4):
        packed = jnp.zeros(lane.shape, F32)
        for g in range(2 * FX):
            plane = fields[2 * tile + g // FX][g % FX]
            packed = jnp.where(lane // (2 * RIM) == g, roll(plane, RIM + 2 * RIM * g, 1), packed)
        out[tile * lane.shape[0] : (tile + 1) * lane.shape[0], :] = packed


def rim_body(n_gx, even, odd, keep, got, sent, rim_target, sens_keep):
    is_odd = lax.rem(lax.axis_index("gy"), 2) == 1
    height = rim_target.shape[0]
    tiles = odd.shape[0] // height
    for tile in range(tiles):
        rows = slice(tile * height, (tile + 1) * height)
        left, right = low_high(even[rows, :], odd[rows, :], is_odd)
        lane = iota(left.shape, 1)
        value = jnp.where(lane % (2 * RIM) < RIM, roll(right, -RIM, 1), roll(left, RIM, 1))
        if tile == tiles - 1:
            rim_target[...] = value
        else:
            sent[rows, :] = value
    base = (tiles - 1) * height
    n_gy = 2 * keep.shape[0]
    rows = keep.shape[1]
    got = row_slots(got, got.shape[0] - keep.shape[0] * rows, rows)
    slots = join_slots(keep, got, "gy", n_gy.bit_length() - 2)
    for d in range(n_gy):
        sent[base + d * SLOT_ROWS : base + (d + 1) * SLOT_ROWS, :] = slots[d][:SLOT_ROWS]
    base = base + n_gy * SLOT_ROWS
    rows = [
        jnp.concatenate([slots[d][SLOT_ROWS + i : SLOT_ROWS + i + 1] for d in range(n_gy)], axis=0)
        for i in range(n_gx)
    ]
    split_slots(rows, "gx", 0, row_slots(sent, base, n_gy), sens_keep)


def rim_tile(packed, group):
    lane = iota(packed.shape, 1)
    if isinstance(group, int):
        right = roll(packed, -2 * RIM * group, 1)
        left = roll(packed, LANES - 2 * RIM - 2 * RIM * group, 1)
    else:
        right = pltpu.roll(packed, lax.rem(LANES - 2 * RIM * group, LANES), 1)
        left = pltpu.roll(packed, LANES - 2 * RIM - 2 * RIM * group, 1)
    return jnp.where(lane < RIM, right, jnp.where(lane >= LANES - RIM, left, 0.0))


def x_odd():
    return lax.rem(lax.axis_index("gx"), 2) == 1


def flip(plane):
    return jnp.where(x_odd(), plane, FX - 1 - plane)


class planes:
    def __init__(self, axis, *parts):
        self.axis, self.parts = axis, parts

    def find(self, key):
        at = key[self.axis]
        for ref, first in self.parts:
            if first <= at < first + ref.shape[self.axis]:
                return ref, key[: self.axis] + (at - first,) + key[self.axis + 1 :]

    def __getitem__(self, key):
        ref, key = self.find(key)
        return ref[key]

    def __setitem__(self, key, value):
        ref, key = self.find(key)
        ref[key] = value


def extended(field, main, rim, w):
    height = main.shape[2]
    p = flip(w % FX)
    rows = slice(field // 2 * height, (field // 2 + 1) * height)
    return main[field, p], rim_tile(rim[rows, :], (field % 2) * FX + p)


def source_tile(n_gy, height, wide_y, records_in, planes, skip, out, stacked, placing, turned):
    records = n_gy * SLOT_ROWS
    blocks_y = wide_y // FY
    r_of, r_to = iota((records, records), 0), iota((records, records), 1)
    slot = r_of % SLOT_ROWS
    meta = jnp.zeros((records, LANES), F32)
    for k in range(CAPA):
        move = (slot < 12) & (slot % 4 == k) & (r_to == r_of - slot + 12 + slot // 4)
        meta = meta + pick(move.astype(BF16), roll(records_in, -32 * k, 1))
    q_of, l_of = iota((FOOT, FOOT), 0), iota((FOOT, FOOT), 1)
    unpack = (l_of == (q_of % 32) * FY + q_of // 32).astype(BF16)
    side = (iota((records, 1), 0) % SLOT_ROWS) // 4
    meta_t = meta.T
    block_row = meta_t[BLOCK_AT : BLOCK_AT + 1, :].astype(jnp.int32) - 1
    bz_row = block_row // blocks_y
    turned[...] = pick(unpack, records_in, ((1,), (1,)), 2)
    block_col = meta[:, BLOCK_AT : BLOCK_AT + 1].astype(jnp.int32) - 1
    by = block_col % blocks_y
    usable = (block_col >= 0) & (
        (side == 1)
        | ((side == 0) & (by * FY >= wide_y - RIM))
        | ((side == 2) & (by * FY < RIM))
    )
    start = jnp.where(side == 1, by * FY, wide_y + by * FY)
    start = jnp.where(usable, start, -FY)
    wide_lane = iota((records, 2 * wide_y), 1)
    for fy in range(FY):
        placing[fy * records : (fy + 1) * records, :] = (wide_lane == start + fy).astype(BF16)
    rows_out = planes * height
    for s in range(2):
        force = meta_t[CTRL_AT + s : CTRL_AT + s + 1, :]
        for fy in range(FY):
            lanes = slice(fy * records, (fy + 1) * records)
            for i in range(planes):
                at = pl.multiple_of(fy * 32 + (i + skip) * FZ, FZ)
                scaled = turned[pl.ds(at, FZ), :] * force
                for bz in range(height // FZ):
                    at = i * height + bz * FZ
                    stacked[at : at + FZ, lanes] = jnp.where(bz_row == bz, scaled, 0.0)
        value = spread(placing[...], stacked[:rows_out, :], count=2)
        for i in range(planes):
            out[s, i] = value[i * height : (i + 1) * height]
    return meta, meta_t


def own_source_body(n_gy, height, wide_y, got, source, foot_hot, foot_own, stacked, placing, turned):
    records = n_gy * SLOT_ROWS
    blocks_y = wide_y // FY
    base = 3 * height
    records_in = got[base : base + records, :]
    meta, meta_t = source_tile(
        n_gy, height, wide_y, records_in, FX, 0, source, stacked, placing, turned
    )
    held = n_gy * CAPA
    r_of, r_to = iota((held, records), 0), iota((held, records), 1)
    own = (r_to == r_of // CAPA * SLOT_ROWS + CAPA + r_of % CAPA).astype(BF16)
    block_row = spread(own, meta_t[CTRL_AT : CTRL_AT + 8], ((1,), (1,)))[BLOCK_AT - CTRL_AT :]
    bz_row = (block_row[:1].astype(jnp.int32) - 1) // blocks_y
    block_col = pick(own, meta)[:, BLOCK_AT : BLOCK_AT + 1].astype(jnp.int32) - 1
    start = jnp.where(block_col >= 0, block_col % blocks_y * FY, -FY)
    q_of, l_of = iota((FOOT, FOOT), 0), iota((FOOT, FOOT), 1)
    unpack = (l_of == (q_of % 32) * FY + q_of // 32).astype(BF16)
    foot_t = pick(unpack, pick(own, records_in), ((1,), (1,)))
    lane = iota((held, wide_y), 1)
    for fy in range(FY):
        lanes = slice(fy * held, (fy + 1) * held)
        foot_hot[lanes, :] = (lane == start + fy).astype(BF16)
        for x in range(FX):
            piece = foot_t[fy * 32 + x * FZ : fy * 32 + (x + 1) * FZ, :]
            for bz in range(height // FZ):
                at = x * height + bz * FZ
                foot_own[at : at + FZ, lanes] = jnp.where(bz_row == bz, piece, 0.0)


def side_source_body(n_gy, height, wide_y, low_parity, got, source, stacked, placing, turned):
    is_low = lax.rem(lax.axis_index("gx"), 2) == low_parity
    records_in = got[3 * height : 3 * height + n_gy * SLOT_ROWS, :]
    skip = jnp.where(is_low, 1, 0)
    source_tile(
        n_gy, height, wide_y, records_in, FX - 1, skip, source, stacked, placing, turned
    )


def sensors_body(height, keep, got, spot_hot, lane_hot, z_hot, rim_hot, readings, table):
    n_gx = 2 * keep.shape[0]
    got = row_slots(got, got.shape[0] - keep.shape[0] * keep.shape[1], keep.shape[1])
    rows = jnp.concatenate(join_slots(keep, got, "gx", n_gx.bit_length() - 2), axis=0)
    devices = rows.shape[0]
    slots = 3 * CAPS * devices
    own = slots // 3
    for n, t in enumerate((1, 0, 2)):
        for k in range(CAPS):
            at = (n * CAPS + k) * devices
            table[at : at + devices, :] = roll(rows, -PITCH * (CAPS * t + k), 1)
    cells = []
    for part in range(slots // LANES):
        lanes = slice(part * LANES, (part + 1) * LANES)
        turned = table[lanes, :].T
        cell = turned[CELL_AT : CELL_AT + 1, :].astype(jnp.int32) - 1
        at_y = cell % LANES
        slot_id = iota((1, LANES), 1) + part * LANES
        live = (cell >= 0) & (
            (slot_id < own)
            | ((slot_id < 2 * own) & (at_y >= LANES - RIM))
            | ((slot_id >= 2 * own) & (at_y < RIM))
        )
        cell = jnp.where(live, cell, -1)
        readings[0:8, lanes] = turned[OBS_AT : OBS_AT + 8]
        readings[8:16, lanes] = jnp.broadcast_to((cell + 1).astype(F32), (8, LANES))
        cells.append(cell)
    cell = jnp.concatenate(cells, axis=1)
    spot, lane = own_hot(cell[:, :own], height)
    spot_hot[...] = spot
    lane_hot[...] = lane
    z, rim = rim_hot_pair(cell[:, own:], height)
    z_hot[...] = z
    rim_hot[...] = rim


def own_hot(cell, height):
    spot = jnp.where(cell >= 0, cell // LANES, -1)
    at_y = jnp.where(cell >= 0, cell % LANES, -1)
    slots = cell.shape[1]
    return (
        (iota((FX * height, slots), 0) == spot).astype(BF16),
        (iota((LANES, slots), 0) == at_y).astype(BF16),
    )


def rim_hot_pair(cell, height):
    spot, at_y = cell // LANES, cell % LANES
    z = jnp.where(cell >= 0, spot % height, -1)
    lane = jnp.where(at_y < RIM, at_y, at_y - LANES + 2 * RIM)
    lane = jnp.where(cell >= 0, spot // height * 2 * RIM + lane, -1)
    slots = cell.shape[1]
    return (
        (iota((height, slots), 0) == z).astype(BF16),
        (iota((2 * RIM * FX, slots), 0) == lane).astype(BF16),
    )


def paired(hot):
    blank = jnp.zeros_like(hot)
    return jnp.concatenate(
        [jnp.concatenate([hot, blank], axis=1), jnp.concatenate([blank, hot], axis=1)], axis=0
    )


def inject(row_hot, lane_hot, values):
    placed = jnp.concatenate([lane_hot.astype(F32) * value for value in values], axis=0)
    total = None
    for part in pieces(placed, 2):
        term = dot(row_hot, part, ((1,), (1,)))
        total = term if total is None else total + term
    return total


def pack_rims(halos):
    packed = jnp.zeros(halos[0].shape, F32)
    lane = iota(packed.shape, 1)
    for g, halo in enumerate(halos):
        at = lane - 2 * RIM * g
        packed = jnp.where((at >= 0) & (at < RIM), roll(halo, 2 * RIM * g, 1), packed)
        packed = jnp.where(
            (at >= RIM) & (at < 2 * RIM), roll(halo, 2 * RIM * g + 2 * RIM, 1), packed
        )
    return packed


def coeffs_body(first, last, sources, *refs):
    count = 2 * len(sources)
    ins, (coeffs, start, half_k) = refs[:count], refs[count:]
    main_of = {at: (ins[2 * i], ins[2 * i + 1]) for i, at in enumerate(sources)}
    height = half_k.shape[1]
    z = iota((height, 2 * LANES), 0)
    sign = jnp.where(x_odd(), 0.5, -0.5)
    lowest, highest = sources[0] * FX, sources[-1] * FX + FX - 1
    for w in range(max(lowest, first - 1), min(highest, last + 1) + 1):
        centre, halo = extended(2, *main_of[w // FX], w)
        half_k[w, :, :LANES] = 0.5 * centre
        half_k[w, :, LANES:] = 0.5 * halo
    for i in range(start.shape[1]):
        w = start_first(first) + i
        for s in range(2):
            centre, halo = extended(s, *main_of[w // FX], w)
            start[s, i, :, :LANES] = centre
            start[s, i, :, LANES:] = halo
    for w in range(first, last + 1):
        k = half_k[w]
        faces = (
            k + half_k[min(w + 1, highest)],
            k + half_k[max(w - 1, lowest)],
            k + roll(k, -1, 1),
            k + roll(k, 1, 1),
            k + jnp.where(z == height - 1, 0.0, roll(k, -1, 0)),
            k + jnp.where(z == 0, 0.0, roll(k, 1, 0)),
        )
        total = (faces[0] + faces[1]) + (faces[2] + faces[3]) + (faces[4] + faces[5])
        drift = []
        for axis in range(3):
            centre, halo = extended(3 + axis, *main_of[w // FX], w)
            drift.append((0.5 if axis else sign) * jnp.concatenate([centre, halo], axis=1))
        at = w - first
        for s in range(2):
            coeffs[s, 6, at] = 1.0 - SCALES[s] * total
            for face in range(6):
                value = faces[face] if s == 0 else SCALES[s] * faces[face]
                value = value - drift[face // 2] if face % 2 == 0 else value + drift[face // 2]
                if face == 4:
                    value = jnp.where(z == height - 1, 0.0, value)
                if face == 5:
                    value = jnp.where(z == 0, 0.0, value)
                coeffs[s, face, at] = value


def start_first(first):
    return 0 if first == 0 else 2 * FX


def inside_rows(n_gx, n_gy):
    row_id, col_id = lax.axis_index("gx"), lax.axis_index("gy")
    lane = iota((1, 2 * LANES), 1)
    lanes_in = (
        (lane < LANES)
        | ((lane < LANES + RIM) & (col_id < n_gy - 1))
        | ((lane >= 2 * LANES - RIM) & (col_id > 0))
    ).astype(F32)
    beyond = jnp.where(x_odd(), row_id < n_gx - 1, row_id > 0)
    far = jnp.where(beyond, lanes_in, 0.0)
    return lambda w: lanes_in if w < 2 * FX else far


def forward_body(n_gx, n_gy, steps, coeffs_e, coeffs_o, start_e, start_o, rim_target, own_source, source_e, source_o, spot_hot, lane_hot, z_hot, rim_hot, readings, target, final, sent, residuals, cur, kept):
    wide = 3 * FX
    inside = inside_rows(n_gx, n_gy)
    coeffs = planes(2, (coeffs_e, 0), (coeffs_o, coeffs_e.shape[2]))
    start = planes(1, (start_e, 0), (start_o, 2 * FX))
    fields = [start, cur.at[0], cur.at[1], cur.at[0], cur.at[1]]

    def source(s, w):
        if w < FX:
            return source_e[s, jnp.where(x_odd(), w - 1, FX - 1 - w)]
        if w < 2 * FX:
            return own_source[s, flip(w - FX)]
        return source_o[s, jnp.where(x_odd(), w - 2 * FX, 3 * FX - 2 - w)]

    for n in range(steps):
        before, after = fields[n], fields[n + 1]
        for x in range(n + 1, wide - n - 1):
            row = inside(x)
            for s in range(2):
                c = before[s, x]
                value = coeffs[s, 6, x] * c + source(s, x)
                value = value + coeffs[s, 0, x] * before[s, x + 1]
                value = value + coeffs[s, 1, x] * before[s, x - 1]
                value = value + coeffs[s, 2, x] * roll(c, -1, 1)
                value = value + coeffs[s, 3, x] * roll(c, 1, 1)
                value = value + coeffs[s, 4, x] * roll(c, -1, 0)
                value = value + coeffs[s, 5, x] * roll(c, 1, 0)
                value = value * row
                if n < steps - 1:
                    after[s, x] = value
                if FX <= x < 2 * FX:
                    kept[n, s, flip(x - FX)] = value
    misfits(
        steps, kept, rim_target, spot_hot, lane_hot, z_hot, rim_hot, readings, target, sent, residuals
    )
    final[...] = kept[steps - 1, :, :, :, :LANES]


def misfits(steps, kept, rim_target, spot_hot, lane_hot, z_hot, rim_hot, readings, target, sent, residuals):
    height = kept.shape[3]
    cells = FX * height
    slots = readings.shape[1]
    own = slots // 3
    rest = slots - own
    residuals[...] = jnp.zeros(residuals.shape, F32)
    live = (readings[8:9, :] > 0.5).astype(F32)
    lane_pair, rim_pair = paired(lane_hot[...]), paired(rim_hot[...])
    spots = spot_hot[...].astype(F32)
    heights = z_hot[...].astype(F32)
    for n in range(steps):
        both = jnp.concatenate(
            [kept[n, s, :, :, :LANES].reshape(cells, LANES) for s in range(2)], axis=1
        )
        seen = spread(lane_pair, both)
        packed = pack_rims([kept[n, s, p, :, LANES:] for s in range(2) for p in range(FX)])
        seen_rim = spread(rim_pair, packed)
        for s in range(2):
            at = s * steps + n
            value = jnp.sum(seen[:, s * own : (s + 1) * own] * spots, axis=0, keepdims=True)
            value = (value - readings[at : at + 1, :own]) * live[:, :own]
            residuals[at : at + 1, :own] = value
            value = jnp.sum(seen_rim[:, s * rest : (s + 1) * rest] * heights, axis=0, keepdims=True)
            value = (value - readings[at : at + 1, own:]) * live[:, own:]
            residuals[at : at + 1, own:] = value
    residuals[8:16, :] = readings[8:16, :]
    ends = [residuals[s * steps + steps - 1 : (s + 1) * steps, :] for s in range(2)]
    put = inject(spot_hot[...], lane_hot[...], [end[:, :own] for end in ends])
    put_rim = inject(z_hot[...], rim_hot[...], [end[:, own:] for end in ends])
    for s in range(2):
        for p in range(FX):
            rows = slice(p * height, (p + 1) * height)
            got = kept[steps - 1, s, p, :, :LANES]
            g = s * FX + p
            sent[g * height : (g + 1) * height, :] = (
                got - target[s, p] + put[rows, s * LANES : (s + 1) * LANES]
            )
    base = 2 * FX * height
    sent[base : base + height, :] = packed - rim_target[...] + put_rim
    base = base + height
    for part in range(slots // LANES):
        lanes = slice(part * LANES, (part + 1) * LANES)
        rows = [residuals[s * steps + n : s * steps + n + 1, lanes] for s in range(2) for n in range(steps - 1)]
        for i, values in enumerate(rows + [residuals[8:9, lanes]] * (8 - len(rows))):
            sent[base + 8 * part + i : base + 8 * part + i + 1, :] = values


def unpack_fields(sent, fields):
    height = fields.shape[2]
    base = 2 * FX * height
    packed = sent[base : base + height, :]
    for s in range(2):
        for p in range(FX):
            g = s * FX + p
            fields[s, flip(p), :, :LANES] = sent[g * height : (g + 1) * height, :]
            fields[s, flip(p), :, LANES:] = rim_tile(packed, g)


def own_adjoint_body(steps, spot_hot, lane_hot, z_hot, rim_hot, residuals, sent, puts, fields):
    unpack_fields(sent, fields)
    slots = residuals.shape[1]
    own = slots // 3
    height = puts.shape[3]
    for n in range(steps - 1):
        values = [residuals[s * steps + n : s * steps + n + 1, :] for s in range(2)]
        put = inject(spot_hot[...], lane_hot[...], [value[:, :own] for value in values])
        put_rim = inject(z_hot[...], rim_hot[...], [value[:, own:] for value in values])
        for s in range(2):
            for p in range(FX):
                rows = slice(p * height, (p + 1) * height)
                puts[n, s, flip(p), :, :LANES] = put[rows, s * LANES : (s + 1) * LANES]
                puts[n, s, flip(p), :, LANES:] = rim_tile(put_rim, s * FX + p)


def side_adjoint_body(steps, low_parity, sent, puts, fields):
    unpack_fields(sent, fields)
    height = puts.shape[3]
    cells = FX * height
    table = 2 * cells + height
    slots = (sent.shape[0] - table) // 8 * LANES
    own = slots // 3
    is_low = lax.rem(lax.axis_index("gx"), 2) == low_parity
    rows = jnp.concatenate(
        [sent[table + 8 * i : table + 8 * i + 8, :] for i in range(slots // LANES)], axis=1
    )
    cell = rows[7:8, :].astype(jnp.int32) - 1
    spot, lane = own_hot(cell[:, :own], height)
    z, rim = rim_hot_pair(cell[:, own:], height)
    for n in range(steps - 1):
        reach = (n + 1) * height
        near = jnp.where(is_low, spot[cells - reach :].astype(F32), spot[:reach].astype(F32))
        values = [rows[s * (steps - 1) + n : s * (steps - 1) + n + 1, :] for s in range(2)]
        put = inject(near.astype(BF16), lane, [value[:, :own] for value in values])
        put_rim = inject(z, rim, [value[:, own:] for value in values])
        for s in range(2):
            for i in range(n + 1):
                p = jnp.where(is_low, FX - n - 1 + i, i)
                puts[n, s, flip(p), :, :LANES] = put[
                    i * height : (i + 1) * height, s * LANES : (s + 1) * LANES
                ]
                puts[n, s, flip(p), :, LANES:] = rim_tile(put_rim, s * FX + p)


def adjoint_body(n_gx, n_gy, steps, coeffs_e, coeffs_o, puts_own, fields_own, puts_e, fields_e, puts_o, fields_o, foot_hot, foot_own, back_keep, back_send, second, cur, summed):
    height = coeffs_e.shape[3]
    wide = 3 * FX
    cells = FX * height
    inside = inside_rows(n_gx, n_gy)
    coeffs = planes(2, (coeffs_e, 0), (coeffs_o, coeffs_e.shape[2]))
    puts = planes(2, (puts_e, 0), (puts_own, FX), (puts_o, 2 * FX))
    start = planes(1, (fields_e, 0), (fields_own, FX), (fields_o, 2 * FX))
    for s in range(2):
        for p in range(FX):
            at = s * cells + p * height
            summed[at : at + height, :] = fields_own[s, flip(p), :, :LANES]
    for turn in range(steps - 1):
        field = start if turn == 0 else cur.at[turn % 2]
        n = steps - 2 - turn
        for x in range(turn + 1, wide - turn - 1):
            for s in range(2):
                value = adjoint_value(coeffs, field, s, x, 0) + puts[n, s, x]
                value = value * inside(x)
                if turn == steps - 2:
                    second[s, x - steps + 1] = value
                else:
                    cur[(turn + 1) % 2, s, x] = value
                if FX <= x < 2 * FX:
                    at = pl.multiple_of(s * cells + flip(x - FX) * height, 8)
                    rows = pl.ds(at, height)
                    summed[rows, :] = summed[rows, :] + value[:, :LANES]
    seen = spread(foot_hot[...], summed[...], ((1,), (1,)), count=2)
    width = foot_own.shape[1]
    held = width // FY
    out_from = iota((1, width), 1) // CAPA
    totals = []
    for s in range(2):
        row = jnp.sum(seen[s * cells : (s + 1) * cells] * foot_own[...], axis=0, keepdims=True)
        total = row
        for fy in range(1, FY):
            total = total + roll(row, -fy * held, 1)
        totals.append(total)
    block = jnp.concatenate(totals + [jnp.zeros((6, width), F32)], axis=0)
    slots = [jnp.where(out_from == d, block, 0.0) for d in range(n_gy)]
    part_slots(slots, "gy", 0, 1, (back_keep, back_send))


def adjoint_value(coeffs, field, s, x, shift):
    w = field[s, x - shift]
    value = coeffs[s, 6, x] * w
    value = value + coeffs[s, 1, x + 1] * field[s, x + 1 - shift]
    value = value + coeffs[s, 0, x - 1] * field[s, x - 1 - shift]
    value = value + roll(coeffs[s, 3, x] * w, -1, 1)
    value = value + roll(coeffs[s, 2, x] * w, 1, 1)
    value = value + roll(coeffs[s, 5, x] * w, -1, 0)
    return value + roll(coeffs[s, 4, x] * w, 1, 0)


def last_body(steps, coeffs_e, coeffs_o, second, first):
    coeffs = planes(2, (coeffs_e, 0), (coeffs_o, coeffs_e.shape[2]))
    for x in range(FX, 2 * FX):
        for s in range(2):
            first[s, flip(x - FX)] = adjoint_value(coeffs, second, s, x, steps - 1)[:, :LANES]


def returned_body(n_gy, *refs):
    low, width = stages(n_gy)[-1]
    parts, (owner, out) = refs[: 1 << width], refs[1 << width :]
    slots = merge_slots(parts, n_gy, "gy", low, width)
    records = slots[0].shape[1]
    base = lax.axis_index("gy") * CAPA
    choice = slot_choices(owner[...], n_gy, CAPA)
    lane = iota((n_gy, records), 1)
    for s in range(2):
        rows = jnp.concatenate([slot[s : s + 1] for slot in slots], axis=0)
        total = jnp.zeros(choice[0].shape, F32)
        for k in range(CAPA):
            column = jnp.sum(jnp.where(lane == base + k, rows, 0.0), axis=1, keepdims=True)
            total = total + choice[k].astype(F32) * column
        out[s : s + 1, :] = jnp.sum(total, axis=0, keepdims=True)


def per_device(
    initial_state,
    eddy_diffusivity,
    velocity,
    target,
    sensor_cell,
    sensor_owner,
    observations,
    actuator_block,
    actuator_owner,
    controls,
    footprint,
):
    _, wide_x, height, wide_y = initial_state.shape
    steps = observations.shape[2]
    n_gx, n_gy = lax.axis_size("gx"), lax.axis_size("gy")
    devices = n_gx * n_gy
    sens, acts = sensor_cell.shape[0], actuator_block.shape[0]
    records = n_gy * SLOT_ROWS
    slots = 3 * CAPS * devices
    cells = FX * height
    wide = 3 * FX
    shape = jax.ShapeDtypeStruct
    vmem = pltpu.VMEM
    a_owner_row = actuator_owner.reshape(1, acts)
    main = jnp.concatenate([initial_state, eddy_diffusivity[None], velocity], axis=0)
    slot_rows = SLOT_ROWS + -(-n_gx // 8) * 8
    half = shape((n_gy // 2, slot_rows, LANES), F32)
    sens_half = shape((n_gx // 2, n_gy, LANES), F32)
    strip_rows = 4 * height
    acts_send, acts_keep = call(
        functools.partial(records_out_body, n_gx, n_gy),
        (
            shape((n_gy // 2 * slot_rows, LANES), F32),
            half,
        ),
        [
            vmem((LANES, sens), F32),
            vmem((LANES, acts), F32),
            vmem((n_gy, slot_rows, LANES), F32),
        ],
        sensor_cell.reshape(1, sens),
        sensor_owner.reshape(1, sens),
        observations.transpose(1, 2, 0),
        actuator_block.reshape(1, acts),
        a_owner_row,
        controls.T,
        footprint,
    )
    strips = call(
        strips_body,
        shape((strip_rows, LANES), F32),
        [],
        initial_state,
        eddy_diffusivity,
        velocity,
        target,
    )
    main_e, main_o = exchange(main, "gx")
    strips_e, strips_o = exchange(strips, "gy")
    acts_keep, acts_got = route(acts_keep, swap(acts_send, "gy", 1, 0), "gy")
    rim, rim_target, sens_keep = call(
        functools.partial(rim_body, n_gx),
        (
            shape((3 * height + records + n_gx // 2 * n_gy, LANES), F32),
            shape((height, LANES), F32),
            sens_half,
        ),
        [],
        strips_e, strips_o, acts_keep, acts_got,
    )
    rim_e, rim_o = exchange(rim, "gx")
    held = n_gy * CAPA
    scratch = [
        vmem((cells, FY * records), F32),
        vmem((FY * records, 2 * LANES), BF16),
        vmem((FOOT, records), F32),
    ]
    own_source, foot_hot, foot_own = call(
        functools.partial(own_source_body, n_gy, height, wide_y),
        (
            shape((2, FX, height, 2 * LANES), F32),
            shape((FY * held, LANES), BF16),
            shape((cells, FY * held), F32),
        ),
        scratch,
        rim,
        us=1.5,
    )
    split = 2 * FX - 1
    coeffs_e, start_e = call(
        functools.partial(coeffs_body, 0, split - 1, (0, 1)),
        (
            shape((2, 7, split, height, 2 * LANES), F32),
            shape((2, 2 * FX, height, 2 * LANES), F32),
        ),
        [vmem((wide, height, 2 * LANES), F32)],
        main_e, rim_e, main, rim,
        us=1.0,
    )
    source_e = call(
        functools.partial(side_source_body, n_gy, height, wide_y, 1),
        shape((2, FX - 1, height, 2 * LANES), F32),
        scratch,
        rim_e,
        us=0.9,
    )
    rim_o, start_e, source_e = lax.optimization_barrier((rim_o, start_e, source_e))
    source_o = call(
        functools.partial(side_source_body, n_gy, height, wide_y, 0),
        shape((2, FX - 1, height, 2 * LANES), F32),
        scratch,
        rim_o,
        us=0.9,
    )
    sens_keep, sens_got = route(sens_keep, rim_e, "gx", after=foot_hot)
    coeffs_o, start_o = call(
        functools.partial(coeffs_body, split, wide - 1, (1, 2)),
        (
            shape((2, 7, wide - split, height, 2 * LANES), F32),
            shape((2, FX, height, 2 * LANES), F32),
        ),
        [vmem((wide, height, 2 * LANES), F32)],
        main, rim, main_o, rim_o,
        us=0.7,
    )
    sens_keep, start_o = lax.optimization_barrier((sens_keep, start_o))
    own_slots = slots // 3
    rest = slots - own_slots
    *hots, readings = call(
        functools.partial(sensors_body, height),
        (
            shape((cells, own_slots), BF16),
            shape((LANES, own_slots), BF16),
            shape((height, rest), BF16),
            shape((2 * RIM * FX, rest), BF16),
            shape((16, slots), F32),
        ),
        [vmem((slots, LANES), F32)],
        sens_keep, sens_got,
    )
    sent_rows = 2 * cells + height + slots // LANES * 8
    final, sent, residuals = call(
        functools.partial(forward_body, n_gx, n_gy, steps),
        (
            shape((2, FX, height, LANES), F32),
            shape((sent_rows, LANES), F32),
            shape((16, slots), F32),
        ),
        [
            vmem((2, 2, wide, height, 2 * LANES), F32),
            vmem((steps, 2, FX, height, 2 * LANES), F32),
        ],
        coeffs_e, coeffs_o, start_e, start_o, rim_target, own_source, source_e, source_o, *hots, readings, target,
        us=5.0,
    )
    sent_e, sent_o = exchange(sent, "gx")
    side = (
        shape((steps - 1, 2, FX, height, 2 * LANES), F32),
        shape((2, FX, height, 2 * LANES), F32),
    )
    own_side = call(
        functools.partial(own_adjoint_body, steps), side, [], *hots, residuals, sent, us=0.7
    )
    even_side, odd_side = [
        call(functools.partial(side_adjoint_body, steps, parity), side, [], got, us=0.5)
        for parity, got in ((1, sent_e), (0, sent_o))
    ]
    back_keep, back_send, second = call(
        functools.partial(adjoint_body, n_gx, n_gy, steps),
        (
            shape((n_gy // 2, 8, FY * held), F32),
            shape((n_gy // 2, 8, FY * held), F32),
            shape((2, wide - 2 * steps + 2, height, 2 * LANES), F32),
        ),
        [vmem((2, 2, wide, height, 2 * LANES), F32), vmem((2 * cells, LANES), F32)],
        coeffs_e, coeffs_o, *own_side, *even_side, *odd_side, foot_hot, foot_own,
        us=3.0,
    )
    back = send_back([back_keep, back_send], n_gy)
    first = call(
        functools.partial(last_body, steps),
        shape((2, FX, height, LANES), F32),
        [],
        coeffs_e, coeffs_o, second,
        us=1.0,
    )
    returned = call(
        functools.partial(returned_body, n_gy), shape((2, acts), F32), [], *back, a_owner_row
    )
    return (final, first, returned.T)


def solution(mesh):
    in_specs = (
        P(None, "gx", None, "gy"),
        P("gx", None, "gy"),
        P(None, "gx", None, "gy"),
        P(None, "gx", None, "gy"),
        P(("gx", "gy")),
        P(("gx", "gy"), None),
        P(("gx", "gy"), None, None),
        P(("gx", "gy")),
        P(("gx", "gy"), None),
        P(("gx", "gy"), None),
        P(("gx", "gy"), None),
    )
    out_specs = (P(None, "gx", None, "gy"), P(None, "gx", None, "gy"), P(("gx", "gy"), None))
    return jax.shard_map(
        per_device, mesh=mesh, in_specs=in_specs, out_specs=out_specs, check_vma=False
    )
```

```python
import functools

import jax
import jax.numpy as jnp
from jax import lax
from jax.experimental import pallas as pl
from jax.experimental.pallas import tpu as pltpu
from jax.sharding import PartitionSpec as P

FX = 4
FZ = 8
FY = 4
CAPS = 4
CAPA = 4
FOOT = 128
RIM = 8
LANES = 128
SLOT_ROWS = 16
OBS_AT = 0
CELL_AT = 8
PITCH = 10
CTRL_AT = 16
BLOCK_AT = 18
PRANDTL = 0.85
SCALES = (1.0, 1.0 / PRANDTL)
F32 = jnp.float32
BF16 = jnp.bfloat16
VMEM_BYTES = 20 * 1024 * 1024


def iota(shape, dim):
    return lax.broadcasted_iota(jnp.int32, shape, dim)


def pieces(values, count=3):
    out = []
    for _ in range(count):
        part = values.astype(BF16)
        out.append(part)
        values = values - part.astype(F32)
    return out


def dot(a, b, dims=((1,), (0,))):
    return lax.dot_general(a, b, (dims, ((), ())), preferred_element_type=F32)


def pick(choice, values, dims=((1,), (0,)), count=3):
    total = None
    for part in pieces(values, count):
        term = dot(choice, part, dims)
        total = term if total is None else total + term
    return total


def spread(choice, values, dims=((1,), (0,)), count=3):
    total = None
    for part in pieces(values, count):
        term = dot(part, choice, dims)
        total = term if total is None else total + term
    return total


def roll(values, amount, axis):
    size = values.shape[axis]
    amount = amount % size
    if amount == 0:
        return values
    return pltpu.roll(values, amount, axis)


def swaps(count):
    even = [(i, i ^ 1) for i in range(count) if (i ^ 1) < count]
    odd = [(i, i + 1 if i % 2 else i - 1) for i in range(1, count) if (i % 2 == 0) or i + 1 < count]
    return even, odd


def exchange(values, axis):
    even, odd = swaps(lax.axis_size(axis))
    return lax.ppermute(values, axis, even), lax.ppermute(values, axis, odd)


def low_high(even, odd, is_odd):
    return jnp.where(is_odd, even, odd), jnp.where(is_odd, odd, even)


def call(body, out_shape, scratch, *args, us=0.2):
    return pl.pallas_call(
        body,
        cost_estimate=pl.CostEstimate(
            flops=0, transcendentals=0, bytes_accessed=int(us * 3.6e6)
        ),
        out_shape=out_shape,
        scratch_shapes=scratch,
        compiler_params=pltpu.CompilerParams(vmem_limit_bytes=VMEM_BYTES),
    )(*args)


def slot_choices(owner_row, owners, count):
    records = owner_row.shape[1]
    named = owner_row == iota((owners, records), 0)
    earlier = (iota((records, records), 0) < iota((records, records), 1)).astype(BF16)
    rank = dot(named.astype(BF16), earlier)
    return [(named & (rank == k)).astype(BF16) for k in range(count)]


class row_slots:
    def __init__(self, ref, base, rows):
        self.ref, self.base, self.rows = ref, base, rows
        self.shape = ((ref.shape[0] - base) // rows, rows, ref.shape[1])

    def __getitem__(self, at):
        return self.ref[self.base + at * self.rows : self.base + (at + 1) * self.rows, :]

    def __setitem__(self, at, value):
        self.ref[self.base + at * self.rows : self.base + (at + 1) * self.rows, :] = value


def without_bit(slot, bit):
    return (slot >> (bit + 1) << bit) | (slot & ((1 << bit) - 1))


def bit_of(axis, bit):
    return lax.rem(lax.axis_index(axis) >> bit, 2)


def split_slots(slots, axis, bit, send, keep):
    mine = bit_of(axis, bit) == 1
    for d, low in enumerate(slots):
        if d >> bit & 1:
            continue
        high = slots[d | 1 << bit]
        at = without_bit(d, bit)
        send[at] = jnp.where(mine, low, high)
        keep[at] = jnp.where(mine, high, low)


def join_slots(keep, got, axis, bit):
    mine = bit_of(axis, bit)
    return [
        jnp.where(mine == (d >> bit & 1), keep[without_bit(d, bit)], got[without_bit(d, bit)])
        for d in range(2 * keep.shape[0])
    ]


def route_body(axis, bit, keep, got, next_send, next_keep):
    got = row_slots(got, got.shape[0] - keep.shape[0] * keep.shape[1], keep.shape[1])
    next_send = row_slots(next_send, 0, keep.shape[1])
    split_slots(join_slots(keep, got, axis, bit), axis, bit + 1, next_send, next_keep)


def swap(values, axis, pattern, low):
    count = lax.axis_size(axis)
    return lax.ppermute(values, axis, [(i, i ^ pattern << low) for i in range(count)])


def route(keep, got, axis, after=None):
    bits = lax.axis_size(axis).bit_length() - 1
    for bit in range(bits - 1):
        send = jax.ShapeDtypeStruct((keep.shape[0] * keep.shape[1], LANES), F32)
        half = jax.ShapeDtypeStruct(keep.shape, F32)
        send, keep = call(functools.partial(route_body, axis, bit), (send, half), [], keep, got)
        if after is not None:
            send, after = lax.optimization_barrier((send, after))
        got = swap(send, axis, 1, bit + 1)
    return keep, got


def choose(mine, values):
    out = values[0]
    for m in range(1, len(values)):
        out = jnp.where(mine == m, values[m], out)
    return out


def group_slots(count, low, width):
    span = 1 << width
    rests = [d for d in range(count) if (d >> low) % span == 0]
    return [[rest | p << low for p in range(span)] for rest in rests]


def my_bits(axis, low, width):
    return lax.rem(lax.axis_index(axis) >> low, 1 << width)


def part_slots(slots, axis, low, width, outs):
    mine = my_bits(axis, low, width)
    span = 1 << width
    for at, group in enumerate(group_slots(len(slots), low, width)):
        for v in range(span):
            outs[v][at] = choose(mine, [slots[group[m ^ v]] for m in range(span)])


def merge_slots(parts, count, axis, low, width):
    mine = my_bits(axis, low, width)
    span = 1 << width
    slots = [None] * count
    for at, group in enumerate(group_slots(count, low, width)):
        for p in range(span):
            slots[group[p]] = choose(mine, [parts[m ^ p][at] for m in range(span)])
    return slots


def stages(count):
    bits = count.bit_length() - 1
    return [(0, 1)] + [(low, min(2, bits - low)) for low in range(1, bits, 2)]


def return_body(count, before, after, *refs):
    parts, outs = refs[: 1 << before[1]], refs[1 << before[1] :]
    part_slots(merge_slots(parts, count, "gy", *before), "gy", *after, outs)


def send_back(parts, count):
    plan = stages(count)
    for i, stage in enumerate(plan):
        parts = [parts[0]] + [swap(p, "gy", v, stage[0]) for v, p in enumerate(parts) if v]
        if i + 1 < len(plan):
            after = plan[i + 1]
            piece = jax.ShapeDtypeStruct((count >> after[1],) + parts[0].shape[1:], F32)
            parts = call(
                functools.partial(return_body, count, stage, after),
                (piece,) * (1 << after[1]),
                [],
                *parts,
            )
    return parts


def records_out_body(n_gx, n_gy, cell, s_owner, obs, block, a_owner, ctrl, foot, send, keep, s_meta, a_meta, out):
    owners = n_gx * n_gy
    steps = obs.shape[1]
    s_meta[...] = jnp.zeros(s_meta.shape, F32)
    for s in range(2):
        s_meta[OBS_AT + s * steps : OBS_AT + (s + 1) * steps, :] = obs[s]
    s_meta[CELL_AT : CELL_AT + 1, :] = (cell[...] + 1).astype(F32)
    a_meta[...] = jnp.zeros(a_meta.shape, F32)
    a_meta[CTRL_AT : CTRL_AT + 2, :] = ctrl[...]
    a_meta[BLOCK_AT : BLOCK_AT + 1, :] = (block[...] + 1).astype(F32)
    s_all, a_all, f_all = s_meta[...], a_meta[...], foot[...]
    s_choice = slot_choices(s_owner[...], owners, CAPS)
    a_choice = slot_choices(a_owner[...], n_gy, CAPA)
    act_rows = jnp.zeros((n_gy, LANES), F32)
    sens_rows, foot_rows = [], []
    for k in range(CAPS):
        sens_rows.append(pick(s_choice[k], s_all, ((1,), (1,))))
        act_rows = act_rows + roll(pick(a_choice[k], a_all, ((1,), (1,))), 32 * k, 1)
        foot_rows.append(pick(a_choice[k], f_all))

    def moved(values, t):
        at = iota(values.shape, 0) % n_gy
        if t == 0:
            return jnp.where(at == 0, 0.0, roll(values, 1, 0))
        if t == 2:
            return jnp.where(at == n_gy - 1, 0.0, roll(values, values.shape[0] - 1, 0))
        return values

    packed = jnp.zeros((owners, LANES), F32)
    for t in range(3):
        for k in range(CAPS):
            out[:, 4 * t + k, :] = moved(foot_rows[k], t)
            packed = packed + roll(moved(sens_rows[k], t), PITCH * (CAPS * t + k), 1)
        out[:, 12 + t, :] = moved(act_rows, t)
    out[:, 15:, :] = jnp.zeros((n_gy, out.shape[1] - 15, LANES), F32)
    for d in range(n_gy):
        for i in range(n_gx):
            out[d, SLOT_ROWS + i : SLOT_ROWS + i + 1, :] = packed[i * n_gy + d : i * n_gy + d + 1]
    split_slots([out[d] for d in range(n_gy)], "gy", 0, row_slots(send, 0, out.shape[1]), keep)


def strips_body(state, kappa, vel, target, out):
    lane = iota((state.shape[2], LANES), 1)
    fields = [state.at[0], state.at[1], kappa, vel.at[0], vel.at[1], vel.at[2], target.at[0], target.at[1]]
    for tile in range(4):
        packed = jnp.zeros(lane.shape, F32)
        for g in range(2 * FX):
            plane = fields[2 * tile + g // FX][g % FX]
            packed = jnp.where(lane // (2 * RIM) == g, roll(plane, RIM + 2 * RIM * g, 1), packed)
        out[tile * lane.shape[0] : (tile + 1) * lane.shape[0], :] = packed


def rim_body(n_gx, even, odd, keep, got, sent, rim_target, sens_keep):
    is_odd = lax.rem(lax.axis_index("gy"), 2) == 1
    height = rim_target.shape[0]
    tiles = odd.shape[0] // height
    for tile in range(tiles):
        rows = slice(tile * height, (tile + 1) * height)
        left, right = low_high(even[rows, :], odd[rows, :], is_odd)
        lane = iota(left.shape, 1)
        value = jnp.where(lane % (2 * RIM) < RIM, roll(right, -RIM, 1), roll(left, RIM, 1))
        if tile == tiles - 1:
            rim_target[...] = value
        else:
            sent[rows, :] = value
    base = (tiles - 1) * height
    n_gy = 2 * keep.shape[0]
    rows = keep.shape[1]
    got = row_slots(got, got.shape[0] - keep.shape[0] * rows, rows)
    slots = join_slots(keep, got, "gy", n_gy.bit_length() - 2)
    for d in range(n_gy):
        sent[base + d * SLOT_ROWS : base + (d + 1) * SLOT_ROWS, :] = slots[d][:SLOT_ROWS]
    base = base + n_gy * SLOT_ROWS
    rows = [
        jnp.concatenate([slots[d][SLOT_ROWS + i : SLOT_ROWS + i + 1] for d in range(n_gy)], axis=0)
        for i in range(n_gx)
    ]
    split_slots(rows, "gx", 0, row_slots(sent, base, n_gy), sens_keep)


def rim_tile(packed, group):
    lane = iota(packed.shape, 1)
    if isinstance(group, int):
        right = roll(packed, -2 * RIM * group, 1)
        left = roll(packed, LANES - 2 * RIM - 2 * RIM * group, 1)
    else:
        right = pltpu.roll(packed, lax.rem(LANES - 2 * RIM * group, LANES), 1)
        left = pltpu.roll(packed, LANES - 2 * RIM - 2 * RIM * group, 1)
    return jnp.where(lane < RIM, right, jnp.where(lane >= LANES - RIM, left, 0.0))


def x_odd():
    return lax.rem(lax.axis_index("gx"), 2) == 1


def flip(plane):
    return jnp.where(x_odd(), plane, FX - 1 - plane)


class planes:
    def __init__(self, axis, *parts):
        self.axis, self.parts = axis, parts

    def find(self, key):
        at = key[self.axis]
        for ref, first in self.parts:
            if first <= at < first + ref.shape[self.axis]:
                return ref, key[: self.axis] + (at - first,) + key[self.axis + 1 :]

    def __getitem__(self, key):
        ref, key = self.find(key)
        return ref[key]

    def __setitem__(self, key, value):
        ref, key = self.find(key)
        ref[key] = value


def extended(field, main, rim, w):
    height = main.shape[2]
    p = flip(w % FX)
    rows = slice(field // 2 * height, (field // 2 + 1) * height)
    return main[field, p], rim_tile(rim[rows, :], (field % 2) * FX + p)


def source_tile(n_gy, height, wide_y, records_in, planes, skip, out, stacked, placing, turned):
    records = n_gy * SLOT_ROWS
    blocks_y = wide_y // FY
    r_of, r_to = iota((records, records), 0), iota((records, records), 1)
    slot = r_of % SLOT_ROWS
    meta = jnp.zeros((records, LANES), F32)
    for k in range(CAPA):
        move = (slot < 12) & (slot % 4 == k) & (r_to == r_of - slot + 12 + slot // 4)
        meta = meta + pick(move.astype(BF16), roll(records_in, -32 * k, 1), count=2)
    q_of, l_of = iota((FOOT, FOOT), 0), iota((FOOT, FOOT), 1)
    unpack = (l_of == (q_of % 32) * FY + q_of // 32).astype(BF16)
    side = (iota((records, 1), 0) % SLOT_ROWS) // 4
    meta_t = meta.T
    block_row = meta_t[BLOCK_AT : BLOCK_AT + 1, :].astype(jnp.int32) - 1
    bz_row = block_row // blocks_y
    turned[...] = pick(unpack, records_in, ((1,), (1,)), 2)
    block_col = meta[:, BLOCK_AT : BLOCK_AT + 1].astype(jnp.int32) - 1
    by = block_col % blocks_y
    usable = (block_col >= 0) & (
        (side == 1)
        | ((side == 0) & (by * FY >= wide_y - RIM))
        | ((side == 2) & (by * FY < RIM))
    )
    start = jnp.where(side == 1, by * FY, wide_y + by * FY)
    start = jnp.where(usable, start, -FY)
    wide_lane = iota((records, 2 * wide_y), 1)
    for fy in range(FY):
        placing[fy * records : (fy + 1) * records, :] = (wide_lane == start + fy).astype(BF16)
    rows_out = planes * height
    for s in range(2):
        force = meta_t[CTRL_AT + s : CTRL_AT + s + 1, :]
        for fy in range(FY):
            lanes = slice(fy * records, (fy + 1) * records)
            for i in range(planes):
                at = pl.multiple_of(fy * 32 + (i + skip) * FZ, FZ)
                scaled = turned[pl.ds(at, FZ), :] * force
                for bz in range(height // FZ):
                    at = i * height + bz * FZ
                    stacked[at : at + FZ, lanes] = jnp.where(bz_row == bz, scaled, 0.0)
        value = spread(placing[...], stacked[:rows_out, :], count=2)
        for i in range(planes):
            out[s, i] = value[i * height : (i + 1) * height]
    return meta, meta_t


def own_source_body(n_gy, height, wide_y, got, source, foot_hot, foot_own, stacked, placing, turned):
    records = n_gy * SLOT_ROWS
    blocks_y = wide_y // FY
    base = 3 * height
    records_in = got[base : base + records, :]
    meta, meta_t = source_tile(
        n_gy, height, wide_y, records_in, FX, 0, source, stacked, placing, turned
    )
    held = n_gy * CAPA
    r_of, r_to = iota((held, records), 0), iota((held, records), 1)
    own = (r_to == r_of // CAPA * SLOT_ROWS + CAPA + r_of % CAPA).astype(BF16)
    block_row = spread(own, meta_t[CTRL_AT : CTRL_AT + 8], ((1,), (1,)))[BLOCK_AT - CTRL_AT :]
    bz_row = (block_row[:1].astype(jnp.int32) - 1) // blocks_y
    block_col = pick(own, meta)[:, BLOCK_AT : BLOCK_AT + 1].astype(jnp.int32) - 1
    start = jnp.where(block_col >= 0, block_col % blocks_y * FY, -FY)
    q_of, l_of = iota((FOOT, FOOT), 0), iota((FOOT, FOOT), 1)
    unpack = (l_of == (q_of % 32) * FY + q_of // 32).astype(BF16)
    foot_t = pick(unpack, pick(own, records_in), ((1,), (1,)))
    lane = iota((held, wide_y), 1)
    for fy in range(FY):
        lanes = slice(fy * held, (fy + 1) * held)
        foot_hot[lanes, :] = (lane == start + fy).astype(BF16)
        for x in range(FX):
            piece = foot_t[fy * 32 + x * FZ : fy * 32 + (x + 1) * FZ, :]
            for bz in range(height // FZ):
                at = x * height + bz * FZ
                foot_own[at : at + FZ, lanes] = jnp.where(bz_row == bz, piece, 0.0)


def side_source_body(n_gy, height, wide_y, low_parity, got, source, stacked, placing, turned):
    is_low = lax.rem(lax.axis_index("gx"), 2) == low_parity
    records_in = got[3 * height : 3 * height + n_gy * SLOT_ROWS, :]
    skip = jnp.where(is_low, 1, 0)
    source_tile(
        n_gy, height, wide_y, records_in, FX - 1, skip, source, stacked, placing, turned
    )


def sensors_body(height, keep, got, spot_hot, lane_hot, z_hot, rim_hot, readings, table):
    n_gx = 2 * keep.shape[0]
    got = row_slots(got, got.shape[0] - keep.shape[0] * keep.shape[1], keep.shape[1])
    rows = jnp.concatenate(join_slots(keep, got, "gx", n_gx.bit_length() - 2), axis=0)
    devices = rows.shape[0]
    slots = 3 * CAPS * devices
    own = slots // 3
    for n, t in enumerate((1, 0, 2)):
        for k in range(CAPS):
            at = (n * CAPS + k) * devices
            table[at : at + devices, :] = roll(rows, -PITCH * (CAPS * t + k), 1)
    cells = []
    for part in range(slots // LANES):
        lanes = slice(part * LANES, (part + 1) * LANES)
        turned = table[lanes, :].T
        cell = turned[CELL_AT : CELL_AT + 1, :].astype(jnp.int32) - 1
        at_y = cell % LANES
        slot_id = iota((1, LANES), 1) + part * LANES
        live = (cell >= 0) & (
            (slot_id < own)
            | ((slot_id < 2 * own) & (at_y >= LANES - RIM))
            | ((slot_id >= 2 * own) & (at_y < RIM))
        )
        cell = jnp.where(live, cell, -1)
        readings[0:8, lanes] = turned[OBS_AT : OBS_AT + 8]
        readings[8:16, lanes] = jnp.broadcast_to((cell + 1).astype(F32), (8, LANES))
        cells.append(cell)
    cell = jnp.concatenate(cells, axis=1)
    spot, lane = own_hot(cell[:, :own], height)
    spot_hot[...] = spot
    lane_hot[...] = lane
    z, rim = rim_hot_pair(cell[:, own:], height)
    z_hot[...] = z
    rim_hot[...] = rim


def own_hot(cell, height):
    spot = jnp.where(cell >= 0, cell // LANES, -1)
    at_y = jnp.where(cell >= 0, cell % LANES, -1)
    slots = cell.shape[1]
    return (
        (iota((FX * height, slots), 0) == spot).astype(BF16),
        (iota((LANES, slots), 0) == at_y).astype(BF16),
    )


def rim_hot_pair(cell, height):
    spot, at_y = cell // LANES, cell % LANES
    z = jnp.where(cell >= 0, spot % height, -1)
    lane = jnp.where(at_y < RIM, at_y, at_y - LANES + 2 * RIM)
    lane = jnp.where(cell >= 0, spot // height * 2 * RIM + lane, -1)
    slots = cell.shape[1]
    return (
        (iota((height, slots), 0) == z).astype(BF16),
        (iota((2 * RIM * FX, slots), 0) == lane).astype(BF16),
    )


def paired(hot):
    blank = jnp.zeros_like(hot)
    return jnp.concatenate(
        [jnp.concatenate([hot, blank], axis=1), jnp.concatenate([blank, hot], axis=1)], axis=0
    )


def inject(row_hot, lane_hot, values):
    placed = jnp.concatenate([lane_hot.astype(F32) * value for value in values], axis=0)
    total = None
    for part in pieces(placed, 2):
        term = dot(row_hot, part, ((1,), (1,)))
        total = term if total is None else total + term
    return total


def pack_rims(halos):
    packed = jnp.zeros(halos[0].shape, F32)
    lane = iota(packed.shape, 1)
    for g, halo in enumerate(halos):
        at = lane - 2 * RIM * g
        packed = jnp.where((at >= 0) & (at < RIM), roll(halo, 2 * RIM * g, 1), packed)
        packed = jnp.where(
            (at >= RIM) & (at < 2 * RIM), roll(halo, 2 * RIM * g + 2 * RIM, 1), packed
        )
    return packed


def coeffs_body(first, last, sources, *refs):
    count = 2 * len(sources)
    ins, (coeffs, start, half_k) = refs[:count], refs[count:]
    main_of = {at: (ins[2 * i], ins[2 * i + 1]) for i, at in enumerate(sources)}
    height = half_k.shape[1]
    z = iota((height, 2 * LANES), 0)
    sign = jnp.where(x_odd(), 0.5, -0.5)
    lowest, highest = sources[0] * FX, sources[-1] * FX + FX - 1
    for w in range(max(lowest, first - 1), min(highest, last + 1) + 1):
        centre, halo = extended(2, *main_of[w // FX], w)
        half_k[w, :, :LANES] = 0.5 * centre
        half_k[w, :, LANES:] = 0.5 * halo
    for i in range(start.shape[1]):
        w = start_first(first) + i
        for s in range(2):
            centre, halo = extended(s, *main_of[w // FX], w)
            start[s, i, :, :LANES] = centre
            start[s, i, :, LANES:] = halo
    for w in range(first, last + 1):
        k = half_k[w]
        faces = (
            k + half_k[min(w + 1, highest)],
            k + half_k[max(w - 1, lowest)],
            k + roll(k, -1, 1),
            k + roll(k, 1, 1),
            k + jnp.where(z == height - 1, 0.0, roll(k, -1, 0)),
            k + jnp.where(z == 0, 0.0, roll(k, 1, 0)),
        )
        total = (faces[0] + faces[1]) + (faces[2] + faces[3]) + (faces[4] + faces[5])
        drift = []
        for axis in range(3):
            centre, halo = extended(3 + axis, *main_of[w // FX], w)
            drift.append((0.5 if axis else sign) * jnp.concatenate([centre, halo], axis=1))
        at = w - first
        for s in range(2):
            coeffs[s, 6, at] = 1.0 - SCALES[s] * total
            for face in range(6):
                value = faces[face] if s == 0 else SCALES[s] * faces[face]
                value = value - drift[face // 2] if face % 2 == 0 else value + drift[face // 2]
                if face == 4:
                    value = jnp.where(z == height - 1, 0.0, value)
                if face == 5:
                    value = jnp.where(z == 0, 0.0, value)
                coeffs[s, face, at] = value


def start_first(first):
    return 0 if first == 0 else 2 * FX


def inside_rows(n_gx, n_gy):
    row_id, col_id = lax.axis_index("gx"), lax.axis_index("gy")
    lane = iota((1, 2 * LANES), 1)
    lanes_in = (
        (lane < LANES)
        | ((lane < LANES + RIM) & (col_id < n_gy - 1))
        | ((lane >= 2 * LANES - RIM) & (col_id > 0))
    ).astype(F32)
    beyond = jnp.where(x_odd(), row_id < n_gx - 1, row_id > 0)
    far = jnp.where(beyond, lanes_in, 0.0)
    return lambda w: lanes_in if w < 2 * FX else far


def forward_body(n_gx, n_gy, steps, coeffs_e, coeffs_o, start_e, start_o, rim_target, own_source, source_e, source_o, spot_hot, lane_hot, z_hot, rim_hot, readings, target, final, sent, residuals, cur, kept):
    wide = 3 * FX
    inside = inside_rows(n_gx, n_gy)
    coeffs = planes(2, (coeffs_e, 0), (coeffs_o, coeffs_e.shape[2]))
    start = planes(1, (start_e, 0), (start_o, 2 * FX))
    fields = [start, cur.at[0], cur.at[1], cur.at[0], cur.at[1]]

    def source(s, w):
        if w < FX:
            return source_e[s, jnp.where(x_odd(), w - 1, FX - 1 - w)]
        if w < 2 * FX:
            return own_source[s, flip(w - FX)]
        return source_o[s, jnp.where(x_odd(), w - 2 * FX, 3 * FX - 2 - w)]

    for n in range(steps):
        before, after = fields[n], fields[n + 1]
        for x in range(n + 1, wide - n - 1):
            row = inside(x)
            for s in range(2):
                c = before[s, x]
                value = coeffs[s, 6, x] * c + source(s, x)
                value = value + coeffs[s, 0, x] * before[s, x + 1]
                value = value + coeffs[s, 1, x] * before[s, x - 1]
                value = value + coeffs[s, 2, x] * roll(c, -1, 1)
                value = value + coeffs[s, 3, x] * roll(c, 1, 1)
                value = value + coeffs[s, 4, x] * roll(c, -1, 0)
                value = value + coeffs[s, 5, x] * roll(c, 1, 0)
                value = value * row
                if n < steps - 1:
                    after[s, x] = value
                if FX <= x < 2 * FX:
                    kept[n, s, flip(x - FX)] = value
    misfits(
        steps, kept, rim_target, spot_hot, lane_hot, z_hot, rim_hot, readings, target, sent, residuals
    )
    final[...] = kept[steps - 1, :, :, :, :LANES]


def misfits(steps, kept, rim_target, spot_hot, lane_hot, z_hot, rim_hot, readings, target, sent, residuals):
    height = kept.shape[3]
    cells = FX * height
    slots = readings.shape[1]
    own = slots // 3
    rest = slots - own
    residuals[...] = jnp.zeros(residuals.shape, F32)
    live = (readings[8:9, :] > 0.5).astype(F32)
    lane_pair, rim_pair = paired(lane_hot[...]), paired(rim_hot[...])
    spots = spot_hot[...].astype(F32)
    heights = z_hot[...].astype(F32)
    for n in range(steps):
        both = jnp.concatenate(
            [kept[n, s, :, :, :LANES].reshape(cells, LANES) for s in range(2)], axis=1
        )
        seen = spread(lane_pair, both, count=2)
        packed = pack_rims([kept[n, s, p, :, LANES:] for s in range(2) for p in range(FX)])
        seen_rim = spread(rim_pair, packed, count=2)
        for s in range(2):
            at = s * steps + n
            value = jnp.sum(seen[:, s * own : (s + 1) * own] * spots, axis=0, keepdims=True)
            value = (value - readings[at : at + 1, :own]) * live[:, :own]
            residuals[at : at + 1, :own] = value
            value = jnp.sum(seen_rim[:, s * rest : (s + 1) * rest] * heights, axis=0, keepdims=True)
            value = (value - readings[at : at + 1, own:]) * live[:, own:]
            residuals[at : at + 1, own:] = value
    residuals[8:16, :] = readings[8:16, :]
    ends = [residuals[s * steps + steps - 1 : (s + 1) * steps, :] for s in range(2)]
    put = inject(spot_hot[...], lane_hot[...], [end[:, :own] for end in ends])
    put_rim = inject(z_hot[...], rim_hot[...], [end[:, own:] for end in ends])
    for s in range(2):
        for p in range(FX):
            rows = slice(p * height, (p + 1) * height)
            got = kept[steps - 1, s, p, :, :LANES]
            g = s * FX + p
            sent[g * height : (g + 1) * height, :] = (
                got - target[s, p] + put[rows, s * LANES : (s + 1) * LANES]
            )
    base = 2 * FX * height
    sent[base : base + height, :] = packed - rim_target[...] + put_rim
    base = base + height
    for part in range(slots // LANES):
        lanes = slice(part * LANES, (part + 1) * LANES)
        rows = [residuals[s * steps + n : s * steps + n + 1, lanes] for s in range(2) for n in range(steps - 1)]
        for i, values in enumerate(rows + [residuals[8:9, lanes]] * (8 - len(rows))):
            sent[base + 8 * part + i : base + 8 * part + i + 1, :] = values


def unpack_fields(sent, fields):
    height = fields.shape[2]
    base = 2 * FX * height
    packed = sent[base : base + height, :]
    for s in range(2):
        for p in range(FX):
            g = s * FX + p
            fields[s, flip(p), :, :LANES] = sent[g * height : (g + 1) * height, :]
            fields[s, flip(p), :, LANES:] = rim_tile(packed, g)


def own_adjoint_body(steps, spot_hot, lane_hot, z_hot, rim_hot, residuals, sent, puts, fields):
    unpack_fields(sent, fields)
    slots = residuals.shape[1]
    own = slots // 3
    height = puts.shape[3]
    for n in range(steps - 1):
        values = [residuals[s * steps + n : s * steps + n + 1, :] for s in range(2)]
        put = inject(spot_hot[...], lane_hot[...], [value[:, :own] for value in values])
        put_rim = inject(z_hot[...], rim_hot[...], [value[:, own:] for value in values])
        for s in range(2):
            for p in range(FX):
                rows = slice(p * height, (p + 1) * height)
                puts[n, s, flip(p), :, :LANES] = put[rows, s * LANES : (s + 1) * LANES]
                puts[n, s, flip(p), :, LANES:] = rim_tile(put_rim, s * FX + p)


def side_adjoint_body(steps, low_parity, sent, puts, fields):
    unpack_fields(sent, fields)
    height = puts.shape[3]
    cells = FX * height
    table = 2 * cells + height
    slots = (sent.shape[0] - table) // 8 * LANES
    own = slots // 3
    is_low = lax.rem(lax.axis_index("gx"), 2) == low_parity
    rows = jnp.concatenate(
        [sent[table + 8 * i : table + 8 * i + 8, :] for i in range(slots // LANES)], axis=1
    )
    cell = rows[7:8, :].astype(jnp.int32) - 1
    spot, lane = own_hot(cell[:, :own], height)
    z, rim = rim_hot_pair(cell[:, own:], height)
    for n in range(steps - 1):
        reach = (n + 1) * height
        near = jnp.where(is_low, spot[cells - reach :].astype(F32), spot[:reach].astype(F32))
        values = [rows[s * (steps - 1) + n : s * (steps - 1) + n + 1, :] for s in range(2)]
        put = inject(near.astype(BF16), lane, [value[:, :own] for value in values])
        put_rim = inject(z, rim, [value[:, own:] for value in values])
        for s in range(2):
            for i in range(n + 1):
                p = jnp.where(is_low, FX - n - 1 + i, i)
                puts[n, s, flip(p), :, :LANES] = put[
                    i * height : (i + 1) * height, s * LANES : (s + 1) * LANES
                ]
                puts[n, s, flip(p), :, LANES:] = rim_tile(put_rim, s * FX + p)


def adjoint_body(n_gx, n_gy, steps, coeffs_e, coeffs_o, puts_own, fields_own, puts_e, fields_e, puts_o, fields_o, foot_hot, foot_own, back_keep, back_send, second, cur, summed):
    height = coeffs_e.shape[3]
    wide = 3 * FX
    cells = FX * height
    inside = inside_rows(n_gx, n_gy)
    coeffs = planes(2, (coeffs_e, 0), (coeffs_o, coeffs_e.shape[2]))
    puts = planes(2, (puts_e, 0), (puts_own, FX), (puts_o, 2 * FX))
    start = planes(1, (fields_e, 0), (fields_own, FX), (fields_o, 2 * FX))
    for s in range(2):
        for p in range(FX):
            at = s * cells + p * height
            summed[at : at + height, :] = fields_own[s, flip(p), :, :LANES]
    for turn in range(steps - 1):
        field = start if turn == 0 else cur.at[turn % 2]
        n = steps - 2 - turn
        for x in range(turn + 1, wide - turn - 1):
            for s in range(2):
                value = adjoint_value(coeffs, field, s, x, 0) + puts[n, s, x]
                value = value * inside(x)
                if turn == steps - 2:
                    second[s, x - steps + 1] = value
                else:
                    cur[(turn + 1) % 2, s, x] = value
                if FX <= x < 2 * FX:
                    at = pl.multiple_of(s * cells + flip(x - FX) * height, 8)
                    rows = pl.ds(at, height)
                    summed[rows, :] = summed[rows, :] + value[:, :LANES]
    seen = spread(foot_hot[...], summed[...], ((1,), (1,)), count=2)
    width = foot_own.shape[1]
    held = width // FY
    out_from = iota((1, width), 1) // CAPA
    totals = []
    for s in range(2):
        row = jnp.sum(seen[s * cells : (s + 1) * cells] * foot_own[...], axis=0, keepdims=True)
        total = row
        for fy in range(1, FY):
            total = total + roll(row, -fy * held, 1)
        totals.append(total)
    block = jnp.concatenate(totals + [jnp.zeros((6, width), F32)], axis=0)
    slots = [jnp.where(out_from == d, block, 0.0) for d in range(n_gy)]
    part_slots(slots, "gy", 0, 1, (back_keep, back_send))


def adjoint_value(coeffs, field, s, x, shift):
    w = field[s, x - shift]
    value = coeffs[s, 6, x] * w
    value = value + coeffs[s, 1, x + 1] * field[s, x + 1 - shift]
    value = value + coeffs[s, 0, x - 1] * field[s, x - 1 - shift]
    value = value + roll(coeffs[s, 3, x] * w, -1, 1)
    value = value + roll(coeffs[s, 2, x] * w, 1, 1)
    value = value + roll(coeffs[s, 5, x] * w, -1, 0)
    return value + roll(coeffs[s, 4, x] * w, 1, 0)


def last_body(steps, coeffs_e, coeffs_o, second, first):
    coeffs = planes(2, (coeffs_e, 0), (coeffs_o, coeffs_e.shape[2]))
    for x in range(FX, 2 * FX):
        for s in range(2):
            first[s, flip(x - FX)] = adjoint_value(coeffs, second, s, x, steps - 1)[:, :LANES]


def returned_body(n_gy, *refs):
    low, width = stages(n_gy)[-1]
    parts, (owner, out) = refs[: 1 << width], refs[1 << width :]
    slots = merge_slots(parts, n_gy, "gy", low, width)
    records = slots[0].shape[1]
    base = lax.axis_index("gy") * CAPA
    choice = slot_choices(owner[...], n_gy, CAPA)
    lane = iota((n_gy, records), 1)
    for s in range(2):
        rows = jnp.concatenate([slot[s : s + 1] for slot in slots], axis=0)
        total = jnp.zeros(choice[0].shape, F32)
        for k in range(CAPA):
            column = jnp.sum(jnp.where(lane == base + k, rows, 0.0), axis=1, keepdims=True)
            total = total + choice[k].astype(F32) * column
        out[s : s + 1, :] = jnp.sum(total, axis=0, keepdims=True)


def per_device(
    initial_state,
    eddy_diffusivity,
    velocity,
    target,
    sensor_cell,
    sensor_owner,
    observations,
    actuator_block,
    actuator_owner,
    controls,
    footprint,
):
    _, wide_x, height, wide_y = initial_state.shape
    steps = observations.shape[2]
    n_gx, n_gy = lax.axis_size("gx"), lax.axis_size("gy")
    devices = n_gx * n_gy
    sens, acts = sensor_cell.shape[0], actuator_block.shape[0]
    records = n_gy * SLOT_ROWS
    slots = 3 * CAPS * devices
    cells = FX * height
    wide = 3 * FX
    shape = jax.ShapeDtypeStruct
    vmem = pltpu.VMEM
    a_owner_row = actuator_owner.reshape(1, acts)
    main = jnp.concatenate([initial_state, eddy_diffusivity[None], velocity], axis=0)
    slot_rows = SLOT_ROWS + -(-n_gx // 8) * 8
    half = shape((n_gy // 2, slot_rows, LANES), F32)
    sens_half = shape((n_gx // 2, n_gy, LANES), F32)
    strip_rows = 4 * height
    acts_send, acts_keep = call(
        functools.partial(records_out_body, n_gx, n_gy),
        (
            shape((n_gy // 2 * slot_rows, LANES), F32),
            half,
        ),
        [
            vmem((LANES, sens), F32),
            vmem((LANES, acts), F32),
            vmem((n_gy, slot_rows, LANES), F32),
        ],
        sensor_cell.reshape(1, sens),
        sensor_owner.reshape(1, sens),
        observations.transpose(1, 2, 0),
        actuator_block.reshape(1, acts),
        a_owner_row,
        controls.T,
        footprint,
    )
    strips = call(
        strips_body,
        shape((strip_rows, LANES), F32),
        [],
        initial_state,
        eddy_diffusivity,
        velocity,
        target,
    )
    main_e, main_o = exchange(main, "gx")
    strips_e, strips_o = exchange(strips, "gy")
    acts_keep, acts_got = route(acts_keep, swap(acts_send, "gy", 1, 0), "gy")
    rim, rim_target, sens_keep = call(
        functools.partial(rim_body, n_gx),
        (
            shape((3 * height + records + n_gx // 2 * n_gy, LANES), F32),
            shape((height, LANES), F32),
            sens_half,
        ),
        [],
        strips_e, strips_o, acts_keep, acts_got,
    )
    rim_e, rim_o = exchange(rim, "gx")
    held = n_gy * CAPA
    scratch = [
        vmem((cells, FY * records), F32),
        vmem((FY * records, 2 * LANES), BF16),
        vmem((FOOT, records), F32),
    ]
    own_source, foot_hot, foot_own = call(
        functools.partial(own_source_body, n_gy, height, wide_y),
        (
            shape((2, FX, height, 2 * LANES), F32),
            shape((FY * held, LANES), BF16),
            shape((cells, FY * held), F32),
        ),
        scratch,
        rim,
        us=1.5,
    )
    split = 2 * FX - 1
    coeffs_e, start_e = call(
        functools.partial(coeffs_body, 0, split - 1, (0, 1)),
        (
            shape((2, 7, split, height, 2 * LANES), F32),
            shape((2, 2 * FX, height, 2 * LANES), F32),
        ),
        [vmem((wide, height, 2 * LANES), F32)],
        main_e, rim_e, main, rim,
        us=1.0,
    )
    source_e = call(
        functools.partial(side_source_body, n_gy, height, wide_y, 1),
        shape((2, FX - 1, height, 2 * LANES), F32),
        scratch,
        rim_e,
        us=0.9,
    )
    rim_o, start_e, source_e = lax.optimization_barrier((rim_o, start_e, source_e))
    source_o = call(
        functools.partial(side_source_body, n_gy, height, wide_y, 0),
        shape((2, FX - 1, height, 2 * LANES), F32),
        scratch,
        rim_o,
        us=0.9,
    )
    sens_keep, sens_got = route(sens_keep, rim_e, "gx", after=foot_hot)
    coeffs_o, start_o = call(
        functools.partial(coeffs_body, split, wide - 1, (1, 2)),
        (
            shape((2, 7, wide - split, height, 2 * LANES), F32),
            shape((2, FX, height, 2 * LANES), F32),
        ),
        [vmem((wide, height, 2 * LANES), F32)],
        main, rim, main_o, rim_o,
        us=0.7,
    )
    sens_keep, start_o = lax.optimization_barrier((sens_keep, start_o))
    own_slots = slots // 3
    rest = slots - own_slots
    *hots, readings = call(
        functools.partial(sensors_body, height),
        (
            shape((cells, own_slots), BF16),
            shape((LANES, own_slots), BF16),
            shape((height, rest), BF16),
            shape((2 * RIM * FX, rest), BF16),
            shape((16, slots), F32),
        ),
        [vmem((slots, LANES), F32)],
        sens_keep, sens_got,
    )
    sent_rows = 2 * cells + height + slots // LANES * 8
    final, sent, residuals = call(
        functools.partial(forward_body, n_gx, n_gy, steps),
        (
            shape((2, FX, height, LANES), F32),
            shape((sent_rows, LANES), F32),
            shape((16, slots), F32),
        ),
        [
            vmem((2, 2, wide, height, 2 * LANES), F32),
            vmem((steps, 2, FX, height, 2 * LANES), F32),
        ],
        coeffs_e, coeffs_o, start_e, start_o, rim_target, own_source, source_e, source_o, *hots, readings, target,
        us=5.0,
    )
    sent_e, sent_o = exchange(sent, "gx")
    side = (
        shape((steps - 1, 2, FX, height, 2 * LANES), F32),
        shape((2, FX, height, 2 * LANES), F32),
    )
    own_side = call(
        functools.partial(own_adjoint_body, steps), side, [], *hots, residuals, sent, us=0.7
    )
    even_side, odd_side = [
        call(functools.partial(side_adjoint_body, steps, parity), side, [], got, us=0.5)
        for parity, got in ((1, sent_e), (0, sent_o))
    ]
    back_keep, back_send, second = call(
        functools.partial(adjoint_body, n_gx, n_gy, steps),
        (
            shape((n_gy // 2, 8, FY * held), F32),
            shape((n_gy // 2, 8, FY * held), F32),
            shape((2, wide - 2 * steps + 2, height, 2 * LANES), F32),
        ),
        [vmem((2, 2, wide, height, 2 * LANES), F32), vmem((2 * cells, LANES), F32)],
        coeffs_e, coeffs_o, *own_side, *even_side, *odd_side, foot_hot, foot_own,
        us=3.0,
    )
    back = send_back([back_keep, back_send], n_gy)
    first = call(
        functools.partial(last_body, steps),
        shape((2, FX, height, LANES), F32),
        [],
        coeffs_e, coeffs_o, second,
        us=1.0,
    )
    returned = call(
        functools.partial(returned_body, n_gy), shape((2, acts), F32), [], *back, a_owner_row
    )
    return (final, first, returned.T)


def solution(mesh):
    in_specs = (
        P(None, "gx", None, "gy"),
        P("gx", None, "gy"),
        P(None, "gx", None, "gy"),
        P(None, "gx", None, "gy"),
        P(("gx", "gy")),
        P(("gx", "gy"), None),
        P(("gx", "gy"), None, None),
        P(("gx", "gy")),
        P(("gx", "gy"), None),
        P(("gx", "gy"), None),
        P(("gx", "gy"), None),
    )
    out_specs = (P(None, "gx", None, "gy"), P(None, "gx", None, "gy"), P(("gx", "gy"), None))
    return jax.shard_map(
        per_device, mesh=mesh, in_specs=in_specs, out_specs=out_specs, check_vma=False
    )
```
